32 devices in a mesh: section: 2 (over x), dp: 8 (over z, y), tensor: 2 (over core).
Axes of the slice: x: 2, y: 2, z: 4, core: 2. Of those that a mesh axis runs over, the one named last changes fastest.
Arguments:
- frames: bfloat16 [4, 1024, 1024], P(None, 'dp'), may hold values from -6 to 6
- codes: int32 [4, 1024, 3], P(None, 'dp'), may hold values from 0 to 1023
- lengths: int32 [4, 16], replicated, may hold values from 0 to 1024, as said below
- gains: float32 [2, 2, 1024], P('section'), may hold values from 0.5 to 1.5
- w_qkv: bfloat16 [2, 1024, 3, 1024], P('section', None, None, 'tensor'), may hold values from -0.1875 to 0.1875
- w_out: bfloat16 [2, 1024, 1024], P('section', 'tensor'), may hold values from -0.5 to 0.5
- w_up: bfloat16 [2, 1024, 4096], P('section', None, 'tensor'), may hold values from -0.1875 to 0.1875
- w_down: bfloat16 [2, 4096, 1024], P('section', 'tensor'), may hold values from -0.09375 to 0.09375
- table: bfloat16 [3, 1024, 1024], replicated, may hold values from -6 to 6
- cotangent: bfloat16 [4, 1024, 3, 1024], P(None, 'dp'), may hold values from -6 to 6
Outputs:
- global_out: bfloat16 [4, 1024, 1024], P(None, 'dp')
- local_out: bfloat16 [4, 1024, 3, 1024], P(None, 'dp')
- input_grads: float32 [2, 4, 1024, 1024], P('section', None, 'dp')
- grad_qkv: float32 [2, 1024, 3, 1024], P('section', 'dp', None, 'tensor')
- grad_out: float32 [2, 1024, 1024], P('section', 'tensor', 'dp')
- grad_up: float32 [2, 1024, 4096], P('section', 'dp', 'tensor')
- grad_down: float32 [2, 4096, 1024], P('section', 'tensor', 'dp')
- grad_gains: float32 [2, 2, 1024], P('section', None, 'dp')
- grad_table: float32 [3, 1024, 1024], P(None, ('section', 'dp'))
The draws below stay inside these ranges and needn't reach their ends.
Inputs may be any that keep to these rules, and one draw needn't show every extreme that they name: In every draw one micro-batch, drawn from the seed, holds a single sequence of 1024 frames; in the others the lengths add up to less than 1024 and the frames after the last sequence are padding. A slot of length 0 is unused.
All inputs are finite; a program needn't handle non-finite values.
Results may differ from the reference program's by a relative error of at most 0.015.
Values may be sent and summed in bfloat16 or wider, within the bound.
No kernel may reach another device: no remote copies, remote signals or barrier semaphores. Data moves between devices by JAX's collectives and lax.ppermute only.
A program may use at most 256 MiB of HBM per device.

```python
import jax
import jax.numpy as jnp
from jax import lax

D = 1024
HEADS = 16
HEAD = 64
FF = 4096
CODEBOOKS = 3
VOCAB = 1024
MB = 4
SLOTS = 16
SECTIONS = 2
SEQ_FRAMES = 1024


def draw_lengths(key, part):
    key = jax.random.fold_in(key, 7)
    pick_key, size_key, pad_key = jax.random.split(key, 3)
    unit = max(SEQ_FRAMES // 256, 1)
    roots = jax.random.randint(size_key, (MB, SLOTS), 1, 17).astype(jnp.int32)
    wanted = unit * roots * roots
    budget = SEQ_FRAMES - jax.random.randint(pad_key, (MB, 1), 1, SEQ_FRAMES // 8 + 1).astype(jnp.int32)
    ends = jnp.cumsum(wanted, axis=1).astype(jnp.int32)
    starts = ends - wanted
    kept = jnp.clip(budget - starts, 0, wanted)
    chosen = jax.random.randint(pick_key, (), 0, MB).astype(jnp.int32)
    single = jnp.zeros((MB, SLOTS), jnp.int32).at[:, 0].set(SEQ_FRAMES)
    picked = jnp.arange(MB, dtype=jnp.int32)[:, None] == chosen
    return jnp.where(picked, single, kept).astype(jnp.int32)


def place_ends(entries, own_key, least, high):
    dims = entries.shape
    spot = [jax.random.randint(jax.random.fold_in(own_key, axis), (), 0, dims[axis]) for axis in range(len(dims))]
    entries = entries.at[tuple(spot)].set(least)
    longest = dims.index(max(dims))
    spot[longest] = (spot[longest] + 1) % dims[longest]
    return entries.at[tuple(spot)].set(high)


def steps_of(rng, extent, shards, least, largest):
    loudness, own = 1.0, jax.random.fold_in(rng, 6)
    for dim, shards_of in shards:
        draws = jnp.exp(jax.random.uniform(jax.random.fold_in(own, dim), (shards_of,), jnp.float32, least / len(shards), largest / len(shards)))
        loudness = loudness * jnp.repeat(draws, extent[dim] // shards_of).reshape([-1 if axis == dim else 1 for axis in range(len(extent))])
    return loudness


def noise(own_key, dims, deviation, most, shards=(), held_as=jnp.bfloat16):
    factor_of = steps_of(own_key, dims, shards, -0.22, 0.18) if shards else 1.0
    array = jax.random.normal(own_key, dims, jnp.float32) * deviation * factor_of
    return jnp.minimum(jnp.maximum(array, -most), most).astype(held_as)


def setup_inputs(seed: int = 0) -> dict:
    splits = jax.random.split(jax.random.key(seed), 11)
    frames = noise(splits[0], (MB, SEQ_FRAMES, D), 1.0, 6.0, ((1, 8),))
    codes = place_ends(jax.random.randint(splits[1], (MB, SEQ_FRAMES, CODEBOOKS), 0, VOCAB), jax.random.fold_in(splits[1], 1), 0, VOCAB - 1).astype(jnp.int32)
    lengths = draw_lengths(jax.random.fold_in(splits[10], 71), 0)
    gains = jnp.clip(1.0 + 0.1 * jax.random.normal(splits[3], (SECTIONS, 2, D), jnp.float32), 0.5, 1.5)
    w_qkv = noise(splits[4], (SECTIONS, D, 3, D), D ** -0.5, 0.1875, ((0, 2), (3, 2)))
    w_out = noise(splits[5], (SECTIONS, D, D), (D // 8) ** -0.5, 0.5, ((0, 2), (1, 2)))
    w_up = noise(splits[6], (SECTIONS, D, FF), D ** -0.5, 0.1875, ((0, 2), (2, 2)))
    w_down = noise(splits[7], (SECTIONS, FF, D), FF ** -0.5, 0.09375, ((0, 2), (1, 2)))
    table = noise(splits[8], (CODEBOOKS, VOCAB, D), 1.0, 6.0)
    cotangent = noise(splits[9], (MB, SEQ_FRAMES, CODEBOOKS, D), 1.0, 6.0, ((1, 8),))
    return dict(frames=frames, codes=codes, lengths=lengths, gains=gains, w_qkv=w_qkv, w_out=w_out, w_up=w_up, w_down=w_down, table=table, cotangent=cotangent)


@jax.custom_vjp
def low(v):
    return lax.optimization_barrier(v.astype(jnp.bfloat16)).astype(jnp.float32)

@jax.custom_vjp
def low_back(v):
    return v

def low_keep(v):
    return (low(v), None)

def low_pass(kept, grad):
    return (grad,)

def back_keep(v):
    return (v, None)

def back_low(kept, grad):
    return (low(grad),)
low.defvjp(low_keep, low_pass)
low_back.defvjp(back_keep, back_low)
eps = 1e-05
far = -1e+30
highest = lax.Precision.HIGHEST

def scaled(values, gain_row):
    return values * lax.rsqrt(lax.optimization_barrier(jnp.mean(values * values, axis=-1, keepdims=True)) + eps) * gain_row

def layer(inputs, gain_pair, proj, mix, rise, fall, attend):
    normed = low(scaled(inputs, gain_pair[0]))
    packed = low(low_back(jnp.dot(normed, proj.reshape(proj.shape[0], -1), precision=highest)))
    attended = low(low_back(attend(packed)))
    resid = inputs + low_back(jnp.dot(attended, mix, precision=highest))
    normed_mid = low(scaled(resid, gain_pair[1]))
    rise_out = low_back(jnp.dot(normed_mid, rise, precision=highest))
    active = low(jax.nn.gelu(rise_out, approximate=True))
    return resid + low_back(jnp.dot(active, fall, precision=highest))

def frame_attention(packed, doc, live, positions):
    total = packed.shape[0]
    factor = HEAD ** (-0.5)
    parts = packed.reshape(total, 3, HEADS, HEAD)
    keys_all = parts[:, 1]
    values_all = parts[:, 2]
    block_rows = min(512, total)

    def one_block(inputs):
        queries, row_pos = inputs
        scores = low_back(jnp.einsum('qhe,khe->hqk', queries, keys_all, precision=highest))
        same = (doc[row_pos][:, None] == doc[None, :]) & (positions[None, :] <= row_pos[:, None]) & live[None, :]
        mask = same | (positions[None, :] == row_pos[:, None])
        probs = jax.nn.softmax(jnp.where(mask[None], scores * factor, far), axis=-1)
        return jnp.einsum('hqk,khe->qhe', low(probs), values_all, precision=highest)
    queries = parts[:, 0].reshape(total // block_rows, block_rows, HEADS, HEAD)
    row_pos = positions.reshape(total // block_rows, block_rows)
    attended = lax.map(jax.checkpoint(one_block), (queries, row_pos))
    return attended.reshape(total, D)

def codebook_attention(packed):
    factor = HEAD ** (-0.5)
    frame_count = packed.shape[0] // CODEBOOKS
    parts = packed.reshape(frame_count, CODEBOOKS, 3, HEADS, HEAD)
    scores = low_back(jnp.einsum('nche,ndhe->nhcd', parts[:, :, 0], parts[:, :, 1], precision=highest))
    order = jnp.arange(CODEBOOKS).astype(jnp.int32)
    mask = order[None, :] <= order[:, None]
    probs = jax.nn.softmax(jnp.where(mask, scores * factor, far), axis=-1)
    attended = jnp.einsum('nhcd,ndhe->nche', low(probs), parts[:, :, 2], precision=highest)
    return attended.reshape(frame_count * CODEBOOKS, D)

def reference(frames, codes, lengths, gains, w_qkv, w_out, w_up, w_down, table, cotangent):
    positions = jnp.arange(SEQ_FRAMES).astype(jnp.int32)
    books = jnp.arange(CODEBOOKS).astype(jnp.int32)

    def forward(frames32, gains32, proj, mix, rise, fall, table32, probe):

        def one(inputs):
            frame_rows, code_rows, slot_lengths, probe_rows = inputs
            doc_ends = jnp.cumsum(slot_lengths).astype(jnp.int32)
            doc = lax.optimization_barrier(jnp.sum((positions[:, None] >= doc_ends[None, :]).astype(jnp.int32), axis=1))
            live = positions < doc_ends[-1]
            global_rows = layer(frame_rows, gains32[0], proj[0], mix[0], rise[0], fall[0], lambda packed: frame_attention(packed, doc, live, positions))
            carried = low(low_back(global_rows)) + probe_rows
            mixed = carried[:, None, :] + table32[books[None, :], code_rows]
            local_rows = layer(mixed.reshape(-1, D), gains32[1], proj[1], mix[1], rise[1], fall[1], codebook_attention)
            return (global_rows, local_rows.reshape(mixed.shape))
        return lax.map(jax.checkpoint(one), (frames32, codes, lengths, probe))
    probe = jnp.zeros(frames.shape, jnp.float32)
    primals = (frames.astype(jnp.float32), gains.astype(jnp.float32), w_qkv.astype(jnp.float32), w_out.astype(jnp.float32), w_up.astype(jnp.float32), w_down.astype(jnp.float32), table.astype(jnp.float32), probe)
    outputs, pull = jax.vjp(forward, *primals)
    out_global, out_local = outputs
    grads = pull((jnp.zeros_like(out_global), cotangent.astype(jnp.float32)))
    grad_frames, grad_gains, grad_proj, grad_mix, grad_rise, grad_fall, grad_table, grad_probe = grads
    return (out_global.astype(jnp.bfloat16), out_local.astype(jnp.bfloat16), jnp.stack([grad_frames, grad_probe]), grad_proj, grad_mix, grad_rise, grad_fall, grad_gains, grad_table)
```

```python
import functools

import jax
import jax.numpy as jnp
from jax import lax
from jax.experimental import pallas as pl
from jax.experimental.pallas import tpu as pltpu
from jax.sharding import PartitionSpec as P

HEAD = 64
CODEBOOKS = 3


eps = 1e-05
far = -1e30


def from_behind(block, axis, distance):
    devices = range(lax.axis_size(axis))
    route = [(i - distance, i) for i in devices if i - distance in devices]
    return lax.ppermute(block, axis, route)


def rms_scale(values):
    return lax.rsqrt(jnp.mean(values * values, axis=-1, keepdims=True) + eps)


def rms_back(values, gain_row, grad_normed):
    factor = rms_scale(values)
    normal = values * factor
    grad_unit = grad_normed * gain_row
    grad_values = factor * (
        grad_unit - normal * jnp.mean(grad_unit * normal, axis=-1, keepdims=True)
    )
    return (grad_values, jnp.sum(grad_normed * normal, axis=0))


def head_total(partial_sum):
    return lax.psum(partial_sum, "tensor")


def matmul(left, right):
    return jnp.dot(left, right, preferred_element_type=jnp.float32)


def across_rows(left, right):
    return lax.dot_general(
        left, right, (((0,), (0,)), ((), ())), preferred_element_type=jnp.float32
    )


def against_rows(left, right):
    return lax.dot_general(
        left, right, (((1,), (1,)), ((), ())), preferred_element_type=jnp.float32
    )


def smooth_gate(values):
    return jax.nn.gelu(values, approximate=True)


def doc_index(positions, doc_ends):
    return jnp.sum((positions[:, None] >= doc_ends[None, :]).astype(jnp.int32), axis=1)


def allowed_mask(query_pos, key_pos, doc_ends):
    same_doc = doc_index(query_pos, doc_ends)[:, None] == doc_index(key_pos, doc_ends)[None, :]
    earlier = key_pos[None, :] <= query_pos[:, None]
    live = (key_pos < doc_ends[-1])[None, :]
    return same_doc & earlier & live | (key_pos[None, :] == query_pos[:, None])


def masked_softmax(scores, mask, factor):
    logits = jnp.where(mask, scores * factor, far)
    top = jnp.max(logits, axis=-1, keepdims=True)
    weights = jnp.exp(logits - top)
    mass = jnp.sum(weights, axis=-1, keepdims=True)
    return (weights / mass, (top + jnp.log(mass))[..., 0])


def frame_forward(packed, query_pos, doc_ends, head_count):
    row_count = packed.shape[0]
    width = packed.shape[1] // 3
    factor = HEAD ** (-0.5)
    parts = packed.reshape(row_count, 3, width)
    all_keys, all_values = (
        lax.all_gather(parts[:, 1], "dp", axis=0, tiled=True),
        lax.all_gather(parts[:, 2], "dp", axis=0, tiled=True),
    )
    key_count = all_keys.shape[0]
    key_pos = jnp.arange(key_count, dtype=jnp.int32)
    mask = allowed_mask(query_pos, key_pos, doc_ends)
    queries = parts[:, 0].reshape(row_count, head_count, -1)
    scores = jnp.einsum(
        "qhe,khe->hqk",
        queries,
        all_keys.reshape(key_count, head_count, -1),
        preferred_element_type=jnp.float32,
    )
    probs, log_mass = masked_softmax(scores, mask[None], factor)
    attended = jnp.einsum(
        "hqk,khe->qhe",
        probs.astype(jnp.bfloat16),
        all_values.reshape(key_count, head_count, -1),
        preferred_element_type=jnp.float32,
    )
    return (attended.reshape(row_count, width), log_mass)


def frame_backward(packed, grad_att, log_mass, query_pos, doc_ends, head_count):
    row_count = packed.shape[0]
    width = packed.shape[1] // 3
    factor = HEAD ** (-0.5)
    parts = packed.reshape(row_count, 3, width)
    all_keys, all_values = (
        lax.all_gather(parts[:, 1], "dp", axis=0, tiled=True),
        lax.all_gather(parts[:, 2], "dp", axis=0, tiled=True),
    )
    key_count = all_keys.shape[0]
    key_pos = jnp.arange(key_count, dtype=jnp.int32)
    queries = parts[:, 0].reshape(row_count, head_count, -1)
    grad_heads = grad_att.reshape(row_count, head_count, -1)
    keys_heads = all_keys.reshape(key_count, head_count, -1)
    scores = jnp.einsum("qhe,khe->hqk", queries, keys_heads, preferred_element_type=jnp.float32)
    mask = allowed_mask(query_pos, key_pos, doc_ends)
    probs = jnp.exp(jnp.where(mask[None], scores * factor, far) - log_mass[:, :, None])
    grad_probs = jnp.einsum(
        "qhe,khe->hqk",
        grad_heads,
        all_values.reshape(key_count, head_count, -1),
        preferred_element_type=jnp.float32,
    )
    spread = jnp.sum(probs * grad_probs, axis=-1)
    grad_scores = (probs * (grad_probs - spread[:, :, None]) * factor).astype(jnp.bfloat16)
    grad_queries = jnp.einsum(
        "hqk,khe->qhe", grad_scores, keys_heads, preferred_element_type=jnp.float32
    ).reshape(row_count, width)
    keys_term = jnp.einsum(
        "hqk,qhe->khe", grad_scores, queries, preferred_element_type=jnp.float32
    ).reshape(key_count, width)
    values_term = jnp.einsum(
        "hqk,qhe->khe", probs.astype(jnp.bfloat16), grad_heads, preferred_element_type=jnp.float32
    ).reshape(key_count, width)
    grad_keys, grad_values = (
        lax.psum_scatter(keys_term, "dp", scatter_dimension=0, tiled=True),
        lax.psum_scatter(values_term, "dp", scatter_dimension=0, tiled=True),
    )
    return jnp.stack([grad_queries, grad_keys, grad_values], axis=1).reshape(row_count, 3 * width)


def codebook_forward(packed, head_count):
    row_count = packed.shape[0]
    width = packed.shape[1] // 3
    factor = HEAD ** (-0.5)
    parts = packed.reshape(row_count // CODEBOOKS, CODEBOOKS, 3, head_count, -1)
    scores = jnp.einsum(
        "nche,ndhe->nhcd", parts[:, :, 0], parts[:, :, 1], preferred_element_type=jnp.float32
    )
    order = jnp.arange(CODEBOOKS, dtype=jnp.int32)
    mask = order[None, :] <= order[:, None]
    probs, log_mass = masked_softmax(scores, mask, factor)
    attended = jnp.einsum(
        "nhcd,ndhe->nche",
        probs.astype(jnp.bfloat16),
        parts[:, :, 2],
        preferred_element_type=jnp.float32,
    )
    return (attended.reshape(row_count, width), probs)


def codebook_backward(packed, grad_att, probs, head_count):
    row_count = packed.shape[0]
    width = packed.shape[1] // 3
    factor = HEAD ** (-0.5)
    parts = packed.reshape(row_count // CODEBOOKS, CODEBOOKS, 3, head_count, -1)
    grad_heads = grad_att.reshape(row_count // CODEBOOKS, CODEBOOKS, head_count, -1)
    grad_probs = jnp.einsum(
        "nche,ndhe->nhcd", grad_heads, parts[:, :, 2], preferred_element_type=jnp.float32
    )
    spread = jnp.sum(probs * grad_probs, axis=-1, keepdims=True)
    grad_scores = (probs * (grad_probs - spread) * factor).astype(jnp.bfloat16)
    grad_queries = jnp.einsum(
        "nhcd,ndhe->nche", grad_scores, parts[:, :, 1], preferred_element_type=jnp.float32
    )
    grad_keys = jnp.einsum(
        "nhcd,nche->ndhe", grad_scores, parts[:, :, 0], preferred_element_type=jnp.float32
    )
    grad_values = jnp.einsum(
        "nhcd,nche->ndhe",
        probs.astype(jnp.bfloat16),
        grad_heads,
        preferred_element_type=jnp.float32,
    )
    return jnp.stack([grad_queries, grad_keys, grad_values], axis=2).reshape(row_count, 3 * width)


def layer_forward(inputs, gain_pair, layer_weights, attend):
    w_proj, w_mix, w_rise, w_fall = layer_weights
    normed = (inputs * rms_scale(inputs) * gain_pair[0]).astype(jnp.bfloat16)
    packed = matmul(normed, w_proj.reshape(w_proj.shape[0], -1)).astype(jnp.bfloat16)
    attended, saved = attend(packed)
    attended_low = attended.astype(jnp.bfloat16)
    resid = inputs + head_total(matmul(attended_low, w_mix))
    normed_mid = (resid * rms_scale(resid) * gain_pair[1]).astype(jnp.bfloat16)
    rise = matmul(normed_mid, w_rise)
    active = smooth_gate(rise).astype(jnp.bfloat16)
    result = resid + head_total(matmul(active, w_fall))
    return (result, (normed, packed, attended_low, saved, resid, normed_mid, rise, active))


def layer_backward(inputs, gain_pair, layer_weights, kept, grad_result, attend_back):
    w_proj, w_mix, w_rise, w_fall = layer_weights
    normed, packed, attended_low, saved, resid, normed_mid, rise, active = kept
    grad_fall_low = grad_result.astype(jnp.bfloat16)
    grad_fall_w = across_rows(active, grad_fall_low)
    grad_active = against_rows(grad_fall_low, w_fall)
    grad_rise = jax.vjp(smooth_gate, rise)[1](grad_active)[0].astype(jnp.bfloat16)
    grad_rise_w = across_rows(normed_mid, grad_rise)
    grad_mid = head_total(against_rows(grad_rise, w_rise))
    back_mid, gain_mid = rms_back(resid, gain_pair[1], grad_mid)
    grad_resid = grad_result + back_mid
    resid_low = grad_resid.astype(jnp.bfloat16)
    grad_mix_w = across_rows(attended_low, resid_low)
    grad_att = against_rows(resid_low, w_mix).astype(jnp.bfloat16)
    grad_packed = attend_back(packed, grad_att, saved).astype(jnp.bfloat16)
    flat_proj = w_proj.reshape(w_proj.shape[0], -1)
    grad_proj_w = across_rows(normed, grad_packed).reshape(w_proj.shape)
    grad_normed = head_total(against_rows(grad_packed, flat_proj))
    back_in, gain_in = rms_back(inputs, gain_pair[0], grad_normed)
    return (
        grad_resid + back_in,
        (grad_proj_w, grad_mix_w, grad_rise_w, grad_fall_w, jnp.stack([gain_in, gain_mid])),
    )


def plain_body(frames, codes, lengths, gains, w_qkv, w_out, w_up, w_down, table, cotangent):
    on_first = lax.axis_index("section") == 0
    head_count = w_qkv.shape[3] // HEAD
    layer_weights = (w_qkv[0], w_out[0], w_up[0], w_down[0])
    gains_here = gains[0]
    frame_count = frames.shape[1]
    query_pos = lax.axis_index("dp") * frame_count + jnp.arange(frame_count, dtype=jnp.int32)
    zero_grads = (
        jnp.zeros(w_qkv.shape[1:], jnp.float32),
        jnp.zeros(w_out.shape[1:], jnp.float32),
        jnp.zeros(w_up.shape[1:], jnp.float32),
        jnp.zeros(w_down.shape[1:], jnp.float32),
        jnp.zeros(gains.shape[1:], jnp.float32),
    )

    def global_forward_rows(frame_rows, slot_lengths):
        doc_ends = jnp.cumsum(slot_lengths)
        return (
            doc_ends,
            layer_forward(
                frame_rows.astype(jnp.float32),
                gains_here,
                layer_weights,
                lambda packed: frame_forward(packed, query_pos, doc_ends, head_count),
            ),
        )

    def global_step(carry, inputs):
        doc_ends, (result, kept) = global_forward_rows(inputs[0], inputs[1])
        return (carry, result.astype(jnp.bfloat16))

    global_low = lax.scan(global_step, jnp.zeros((), jnp.int32), (frames, lengths))[1]
    arrived = from_behind(global_low, "section", 1)
    books = jnp.arange(CODEBOOKS, dtype=jnp.int32)
    looked_up = table[books[None, None, :], codes]
    local_in = arrived.astype(jnp.float32)[:, :, None, :] + looked_up.astype(jnp.float32)
    local_rows = local_in.reshape(-1, local_in.shape[-1])
    local_result, local_kept = layer_forward(
        local_rows, gains_here, layer_weights, lambda packed: codebook_forward(packed, head_count)
    )
    grad_rows, local_grads = layer_backward(
        local_rows,
        gains_here,
        layer_weights,
        local_kept,
        cotangent.astype(jnp.float32).reshape(local_rows.shape),
        lambda packed, grad_att, saved: codebook_backward(packed, grad_att, saved, head_count),
    )
    grad_frame = jnp.sum(grad_rows.reshape(local_in.shape), axis=2)
    table_slots = (books[None, None, :] * table.shape[1] + codes).reshape(-1)
    table_term = jax.ops.segment_sum(
        grad_rows, table_slots, num_segments=table.shape[0] * table.shape[1]
    ).reshape(table.shape)
    local_low = local_result.astype(jnp.bfloat16).reshape(cotangent.shape)
    table_part = jnp.where(on_first, jnp.zeros(table.shape, jnp.float32), table_term)
    grad_frame = jnp.where(on_first, jnp.zeros(frames.shape, jnp.float32), grad_frame)
    grad_table = lax.psum_scatter(table_part, ("section", "dp"), scatter_dimension=1, tiled=True)
    grad_back, local_copy = from_behind((grad_frame.astype(jnp.bfloat16), local_low), "section", -1)

    def global_back(totals, inputs):
        frame_rows, slot_lengths, grad_low = inputs
        doc_ends, (result, kept) = global_forward_rows(frame_rows, slot_lengths)
        grad_in, grads = layer_backward(
            frame_rows.astype(jnp.float32),
            gains_here,
            layer_weights,
            kept,
            grad_low.astype(jnp.float32),
            lambda packed, grad_att, saved: frame_backward(
                packed, grad_att, saved, query_pos, doc_ends, head_count
            ),
        )
        return (jax.tree.map(jnp.add, totals, grads), grad_in)

    global_grads, grad_frames = lax.scan(global_back, zero_grads, (frames, lengths, grad_back))

    def pick(global_part, local_part):
        return jnp.where(on_first, global_part, local_part)

    proj_sum, mix_sum, rise_sum, fall_sum, gain_sum = jax.tree.map(pick, global_grads, local_grads)
    proj_share, mix_share, rise_share, fall_share, gain_share = (
        lax.psum_scatter(proj_sum, "dp", scatter_dimension=0, tiled=True),
        lax.psum_scatter(mix_sum, "dp", scatter_dimension=1, tiled=True),
        lax.psum_scatter(rise_sum, "dp", scatter_dimension=0, tiled=True),
        lax.psum_scatter(fall_sum, "dp", scatter_dimension=1, tiled=True),
        lax.psum_scatter(gain_sum, "dp", scatter_dimension=1, tiled=True),
    )
    global_out = jnp.where(on_first, global_low, arrived)
    local_out = jnp.where(on_first, local_copy, local_low)
    input_grads = jnp.where(on_first, grad_frames, grad_frame)[None]
    return (
        global_out,
        local_out,
        input_grads,
        proj_share[None],
        mix_share[None],
        rise_share[None],
        fall_share[None],
        gain_share[None],
        grad_table,
    )


def lasting(us):
    return pl.CostEstimate(flops=int(us * 1.1e9), bytes_accessed=int(us * 1e6), transcendentals=0)

f32=jnp.float32; bf=jnp.bfloat16

def mm(a,b): return jnp.dot(a,b,preferred_element_type=f32)
def mm_nt(a,b): return lax.dot_general(a,b,(((1,),(1,)),((),())),preferred_element_type=f32)

def gelu_both(v):
    c0=0.7978845608028654; a=0.044715
    sq=v*v
    th=jnp.tanh(c0*v*(1.0+a*sq))
    half=0.5*(1.0+th)
    act=v*half
    grad=half+0.5*v*(1.0-th*th)*(c0*(1.0+3.0*a*sq))
    return act,grad

def local_kernel(g_ref, emb_ref, cot_ref, gao_ref, gax_ref, gains_ref, e_ref, et_ref,
                 pqo, pqx, woo, wox, wuo, wux,
                 normed_o, atto_o, attx_o, resid_o, mid_o, acto_o, actx_o, griso_o, grisx_o, glow_o, gpo_o, gpx_o, dx_o, gframe_o, gg_o,
                 q_s, k_s, v_s, p_s, r_s, gm_s, gatt_s):
    F=g_ref.shape[0]; R=3*F; D=g_ref.shape[1]; H2=D//2
    step=pl.program_id(0)
    gain0=gains_ref[0:1,:]; gain1=gains_ref[1:2,:]
    g=g_ref[...].astype(f32)
    scr=(q_s,k_s,v_s)
    r0s=[]
    for c in range(3):
        x=g+emb_ref[c].astype(f32)
        r0=lax.rsqrt(jnp.mean(x*x,axis=-1,keepdims=True)+eps)
        r0s.append(r0)
        normed_o[c]=(x*r0*gain0).astype(bf)
    normed=normed_o[...].reshape(R,D)
    for j in range(3):
        scr[j][:,0:H2]=mm(normed,pqo[j]).astype(bf)
        scr[j][:,H2:D]=mm(normed,pqx[j]).astype(bf)
    E=e_ref[...]; ET=et_ref[...]
    def headsum(prod):
        hi=prod.astype(bf)
        lo=(prod-hi.astype(f32)).astype(bf)
        return mm(hi,E)+mm(lo,E)
    pidx={}
    n=0
    for c in range(3):
        qc=q_s[c*F:(c+1)*F,:].astype(f32)
        ss=[headsum(qc*k_s[c2*F:(c2+1)*F,:].astype(f32))*0.125 for c2 in range(c+1)]
        top=functools.reduce(jnp.maximum,ss)
        ws=[jnp.exp(s-top) for s in ss]
        mass=functools.reduce(jnp.add,ws)
        acc=None
        for c2 in range(c+1):
            p=ws[c2]/mass
            p_s[n]=p; pidx[c,c2]=n; n+=1
            t=mm(p.astype(bf),ET)*v_s[c2*F:(c2+1)*F,:].astype(f32)
            acc=t if acc is None else acc+t
        att=acc.astype(bf)
        atto_o[c]=att[:,0:H2]; attx_o[c]=att[:,H2:D]
    xs=(g_ref[...].astype(f32)[None]+emb_ref[...].astype(f32)).reshape(R,D)
    resid=xs+mm(atto_o[...].reshape(R,H2),woo[...])+mm(attx_o[...].reshape(R,H2),wox[...])
    r1=lax.rsqrt(jnp.mean(resid*resid,axis=-1,keepdims=True)+eps)
    resid_o[...]=resid.reshape(3,F,D)
    nm=(resid*r1*gain1).astype(bf)
    mid_o[...]=nm.reshape(3,F,D)
    ch=512
    gm=None
    for (wu,act_o,gris_o,ga_ref) in ((wuo,acto_o,griso_o,gao_ref),(wux,actx_o,grisx_o,gax_ref)):
        for j in range(wu.shape[1]//ch):
            sl=slice(j*ch,(j+1)*ch)
            w=wu[:,sl]
            act,gr=gelu_both(mm(nm,w))
            act_o[:,:,sl]=act.astype(bf).reshape(3,F,ch)
            gl=(ga_ref[:,:,sl].reshape(R,ch).astype(f32)*gr).astype(bf)
            gris_o[:,:,sl]=gl.reshape(3,F,ch)
            t=mm_nt(gl,w)
            if gm is None:
                gm_s[...]=t; gm=1
            else:
                gm_s[...]+=t
    gmid=gm_s[...]
    n1=resid_o[...].reshape(R,D)*r1
    u=gmid*gain1
    gres=cot_ref[...].reshape(R,D).astype(f32)+r1*(u-n1*jnp.mean(u*n1,axis=-1,keepdims=True))
    gsum1=jnp.sum(gmid*n1,axis=0,keepdims=True)
    r_s[...]=gres
    glow=gres.astype(bf)
    glow_o[...]=glow.reshape(3,F,D)
    gatt_s[:,0:H2]=mm_nt(glow,woo[...]).astype(bf)
    gatt_s[:,H2:D]=mm_nt(glow,wox[...]).astype(bf)
    gk=[None]*3; gv=[None]*3
    def add(a,b): return b if a is None else a+b
    for c in range(3):
        ga=gatt_s[c*F:(c+1)*F,:].astype(f32)
        gps=[headsum(ga*v_s[c2*F:(c2+1)*F,:].astype(f32)) for c2 in range(c+1)]
        ps=[p_s[pidx[c,c2]] for c2 in range(c+1)]
        spread=functools.reduce(jnp.add,[p*gp for p,gp in zip(ps,gps)])
        qc=q_s[c*F:(c+1)*F,:].astype(f32)
        gq=None
        for c2 in range(c+1):
            gs=mm((ps[c2]*(gps[c2]-spread)*0.125).astype(bf),ET)
            pb=mm(ps[c2].astype(bf),ET)
            gq=add(gq,gs*k_s[c2*F:(c2+1)*F,:].astype(f32))
            gk[c2]=add(gk[c2],gs*qc)
            gv[c2]=add(gv[c2],pb*ga)
        gq=gq.astype(bf)
        gpo_o[0,c]=gq[:,0:H2]; gpx_o[0,c]=gq[:,H2:D]
    for c in range(3):
        a=gk[c].astype(bf); gpo_o[1,c]=a[:,0:H2]; gpx_o[1,c]=a[:,H2:D]
        a=gv[c].astype(bf); gpo_o[2,c]=a[:,0:H2]; gpx_o[2,c]=a[:,H2:D]
    gn=None
    for j in range(3):
        gn=add(gn,mm_nt(gpo_o[j].reshape(R,H2),pqo[j]))
        gn=gn+mm_nt(gpx_o[j].reshape(R,H2),pqx[j])
    gm_s[...]=gn
    tot=None; gsum0=None
    for c in range(3):
        gn=gm_s[c*F:(c+1)*F,:]
        n0=(g_ref[...].astype(f32)+emb_ref[c].astype(f32))*r0s[c]
        w=gn*gain0
        dx=r_s[c*F:(c+1)*F,:]+r0s[c]*(w-n0*jnp.mean(w*n0,axis=-1,keepdims=True))
        gsum0=add(gsum0,jnp.sum(gn*n0,axis=0,keepdims=True))
        dx_o[c]=dx.astype(bf)
        tot=add(tot,dx)
    gframe_o[...]=tot
    @pl.when(step==0)
    def _(): gg_o[...]=jnp.zeros_like(gg_o)
    gg_o[0:1,:]+=gsum0
    gg_o[1:2,:]+=gsum1

def local_call(g,emb,cot,gao,gax,gains,pqo,pqx,woo,wox,wuo,wux,tile=128):
    N,D=g.shape; H2=D//2; FH=wuo.shape[1]; F=tile
    E=(jnp.arange(D)[:,None]//HEAD==jnp.arange(128)[None,:]).astype(bf)
    ET=E.T
    c3=lambda w: pl.BlockSpec((3,F,w),lambda i:(0,i,0))
    whole=lambda shp: pl.BlockSpec(shp,lambda i:(0,)*len(shp),pipeline_mode=pl.Buffered(1))
    sd=jax.ShapeDtypeStruct
    out_shape=(sd((3,N,D),bf),sd((3,N,H2),bf),sd((3,N,H2),bf),sd((3,N,D),f32),sd((3,N,D),bf),
       sd((3,N,FH),bf),sd((3,N,FH),bf),sd((3,N,FH),bf),sd((3,N,FH),bf),sd((3,N,D),bf),
       sd((3,3,N,H2),bf),sd((3,3,N,H2),bf),sd((3,N,D),bf),sd((N,D),f32),sd((2,D),f32))
    gp=pl.BlockSpec((3,3,F,H2),lambda i:(0,0,i,0))
    return pl.pallas_call(local_kernel, grid=(N//F,),
      in_specs=[pl.BlockSpec((F,D),lambda i:(i,0)),c3(D),c3(D),c3(FH),c3(FH),whole((2,D)),whole(E.shape),whole(ET.shape),
        whole(pqo.shape),whole(pqx.shape),whole(woo.shape),whole(wox.shape),whole(wuo.shape),whole(wux.shape)],
      out_specs=(c3(D),c3(H2),c3(H2),c3(D),c3(D),c3(FH),c3(FH),c3(FH),c3(FH),c3(D),gp,gp,c3(D),pl.BlockSpec((F,D),lambda i:(i,0)),pl.BlockSpec((2,D),lambda i:(0,0))),
      out_shape=out_shape,
      scratch_shapes=[pltpu.VMEM((3*F,D),bf)]*3+[pltpu.VMEM((6,F,128),f32),pltpu.VMEM((3*F,D),f32),pltpu.VMEM((3*F,D),f32),pltpu.VMEM((3*F,D),bf)],
      compiler_params=pltpu.CompilerParams(vmem_limit_bytes=63 * 1024 * 1024),
      cost_estimate=lasting(57),
      name="local_layer",
    )(g,emb,cot,gao,gax,gains,E,ET,pqo,pqx,woo,wox,wuo,wux)

def attend_kernel(at_ref, q_ref, k_ref, v_ref, qid_ref, kid_ref, o_ref):
    @pl.when(at_ref[0] == 0)
    def _():
        bias = jnp.where(
            ((qid_ref[:, 1:2] == kid_ref[1:2, :]) & (kid_ref[0:1, :] <= qid_ref[:, 0:1]))
            | (kid_ref[0:1, :] == qid_ref[:, 0:1]),
            0.0,
            far,
        )
        lane = lax.broadcasted_iota(jnp.int32, (1, 2 * HEAD), 1) // HEAD
        for pair in range(q_ref.shape[1] // (2 * HEAD)):
            cols = slice(pair * 2 * HEAD, (pair + 1) * 2 * HEAD)
            q, k, v = q_ref[:, cols], k_ref[:, cols], v_ref[:, cols]
            total = None
            for side in range(2):
                here = lane == side
                scores = mm_nt(jnp.where(here, q, jnp.zeros_like(q)), k) * HEAD ** (-0.5) + bias
                top = jnp.max(scores, axis=-1, keepdims=True)
                weights = jnp.exp(scores - top)
                mass = jnp.sum(weights, axis=-1, keepdims=True)
                probs = (weights * (1.0 / mass)).astype(bf)
                term = mm(probs, jnp.where(here, v, jnp.zeros_like(v)))
                total = term if total is None else total + term
            o_ref[:, cols] = total.astype(bf)


def attend_call(at, q, k, v, qid, kid, rows):
    total, width = q.shape
    part = pl.BlockSpec((rows, width), lambda i, s: (i, 0))
    whole = pl.BlockSpec((total, width), lambda i, s: (0, 0))
    return pl.pallas_call(
        attend_kernel,
        grid_spec=pltpu.PrefetchScalarGridSpec(
            num_scalar_prefetch=1,
            grid=(total // rows,),
            in_specs=[part, whole, whole, pl.BlockSpec((rows, 2), lambda i, s: (i, 0)), pl.BlockSpec(kid.shape, lambda i, s: (0, 0))],
            out_specs=part,
        ),
        out_shape=jax.ShapeDtypeStruct((total, width), bf),
        compiler_params=pltpu.CompilerParams(vmem_limit_bytes=60 * 1024 * 1024),
        cost_estimate=lasting(11),
        name="frame_attention",
    )(at, q, k, v, qid, kid)


def attend_back_kernel(at_ref, q_ref, k_ref, v_ref, g_ref, qid_ref, kid_ref, gq_ref, gk_ref, gv_ref, ks_ref, vs_ref):
    @pl.when(at_ref[0] == 0)
    def _():
        step = pl.program_id(0)

        @pl.when(step == 0)
        def _():
            ks_ref[...] = jnp.zeros_like(ks_ref)
            vs_ref[...] = jnp.zeros_like(vs_ref)

        bias = jnp.where(
            ((qid_ref[:, 1:2] == kid_ref[1:2, :]) & (kid_ref[0:1, :] <= qid_ref[:, 0:1]))
            | (kid_ref[0:1, :] == qid_ref[:, 0:1]),
            0.0,
            far,
        )
        lane = lax.broadcasted_iota(jnp.int32, (1, 2 * HEAD), 1) // HEAD
        for pair in range(q_ref.shape[1] // (2 * HEAD)):
            cols = slice(pair * 2 * HEAD, (pair + 1) * 2 * HEAD)
            q, k, v, g = q_ref[:, cols], k_ref[:, cols], v_ref[:, cols], g_ref[:, cols]
            gq = None
            for side in range(2):
                here = lane == side
                qh = jnp.where(here, q, jnp.zeros_like(q))
                gh = jnp.where(here, g, jnp.zeros_like(g))
                kh = jnp.where(here, k, jnp.zeros_like(k))
                scores = mm_nt(qh, k) * HEAD ** (-0.5) + bias
                top = jnp.max(scores, axis=-1, keepdims=True)
                weights = jnp.exp(scores - top)
                mass = jnp.sum(weights, axis=-1, keepdims=True)
                probs = weights * (1.0 / mass)
                grad_probs = mm_nt(gh, v)
                spread = jnp.sum(probs * grad_probs, axis=-1, keepdims=True)
                gs = (probs * (grad_probs - spread) * HEAD ** (-0.5)).astype(bf)
                term = mm(gs, kh)
                gq = term if gq is None else gq + term
                ks_ref[:, cols] += across_rows(gs, qh)
                vs_ref[:, cols] += across_rows(probs.astype(bf), gh)
            gq_ref[:, cols] = gq.astype(bf)

        @pl.when(step == pl.num_programs(0) - 1)
        def _():
            gk_ref[...] = ks_ref[...].astype(bf)
            gv_ref[...] = vs_ref[...].astype(bf)


def attend_back_call(at, q, k, v, g, qid, kid, rows):
    total, width = q.shape
    part = pl.BlockSpec((rows, width), lambda i, s: (i, 0))
    whole = pl.BlockSpec((total, width), lambda i, s: (0, 0))
    shape = jax.ShapeDtypeStruct((total, width), bf)
    return pl.pallas_call(
        attend_back_kernel,
        grid_spec=pltpu.PrefetchScalarGridSpec(
            num_scalar_prefetch=1,
            grid=(total // rows,),
            in_specs=[part, whole, whole, part, pl.BlockSpec((rows, 2), lambda i, s: (i, 0)), pl.BlockSpec(kid.shape, lambda i, s: (0, 0))],
            out_specs=(part, whole, whole),
            scratch_shapes=[pltpu.VMEM((total, width), f32)] * 2,
        ),
        out_shape=(shape, shape, shape),
        compiler_params=pltpu.CompilerParams(vmem_limit_bytes=60 * 1024 * 1024),
        cost_estimate=lasting(0.01),
        name="frame_attention_back",
    )(at, q, k, v, g, qid, kid)


def front_kernel(at_ref, x_ref, ao_ref, ax_ref, gain_ref, oo_ref, ox_ref, uo_ref, ux_ref, do_ref, dx_ref,
                 resid_ref, mid_ref, act_o, act_x, slope_o, slope_x, out_ref, total_ref):
    @pl.when(at_ref[0] == 0)
    def _():
        step = pl.program_id(0)
        turn = pl.num_programs(0) // 2

        @pl.when(step == 0)
        def _():
            resid = x_ref[...].astype(f32) + mm(ao_ref[...], oo_ref[...]) + mm(ax_ref[...], ox_ref[...])
            resid_ref[...] = resid
            scale = lax.rsqrt(jnp.mean(resid * resid, axis=-1, keepdims=True) + eps)
            mid_ref[...] = (resid * scale * gain_ref[1:2, :]).astype(bf)
            total_ref[...] = resid

        def part(up, down, act_ref, slope_ref):
            act, slope = gelu_both(mm(mid_ref[...], up[...]))
            act = act.astype(bf)
            act_ref[...] = act
            slope_ref[...] = slope.astype(bf)
            total_ref[...] += mm(act, down[...])

        @pl.when(step < turn)
        def _():
            part(uo_ref, do_ref, act_o, slope_o)

        @pl.when(step >= turn)
        def _():
            part(ux_ref, dx_ref, act_x, slope_x)

        @pl.when(step == pl.num_programs(0) - 1)
        def _():
            out_ref[...] = total_ref[...].astype(bf)


def halves_specs(turn, chunk, width, rows):
    first = lambda i, s: jnp.minimum(i, turn - 1) * (1 - s[0])
    later = lambda i, s: jnp.maximum(i - turn, 0) * (1 - s[0])
    ups = [pl.BlockSpec((width, chunk), lambda i, s, f=f: (0, f(i, s))) for f in (first, later)]
    downs = [pl.BlockSpec((chunk, width), lambda i, s, f=f: (f(i, s), 0)) for f in (first, later)]
    cols = [pl.BlockSpec((rows, chunk), lambda i, s, f=f: (0, f(i, s))) for f in (first, later)]
    return ups, downs, cols


def front_call(at, x, att_own, att_oth, gains, out_own, out_oth, up_own, up_oth, down_own, down_oth, chunk=512):
    rows, width = x.shape
    hidden = up_own.shape[1]
    turn = hidden // chunk
    ups, downs, cols = halves_specs(turn, chunk, width, rows)
    whole = lambda a: pl.BlockSpec(a.shape, lambda i, s: (0,) * a.ndim)
    sd = jax.ShapeDtypeStruct
    full = pl.BlockSpec((rows, width), lambda i, s: (0, 0))
    hid = sd((rows, hidden), bf)
    return pl.pallas_call(
        front_kernel,
        grid_spec=pltpu.PrefetchScalarGridSpec(
            num_scalar_prefetch=1,
            grid=(2 * turn,),
            in_specs=[full, whole(att_own), whole(att_oth), whole(gains), whole(out_own), whole(out_oth), *ups, *downs],
            out_specs=(full, full, cols[0], cols[1], cols[0], cols[1], full),
            scratch_shapes=[pltpu.VMEM((rows, width), f32)],
        ),
        out_shape=(sd((rows, width), f32), sd((rows, width), bf), hid, hid, hid, hid, sd((rows, width), bf)),
        compiler_params=pltpu.CompilerParams(vmem_limit_bytes=60 * 1024 * 1024),
        cost_estimate=lasting(15),
        name="global_forward",
    )(at, x, att_own, att_oth, gains, out_own, out_oth, up_own, up_oth, down_own, down_oth)


def back_kernel(at_ref, g_ref, resid_ref, gain_ref, so_ref, sx_ref, uo_ref, ux_ref, do_ref, dx_ref,
                rise_o, rise_x, grad_ref, low_ref, gsum_ref, total_ref):
    @pl.when(at_ref[0] == 0)
    def _():
        step = pl.program_id(0)
        turn = pl.num_programs(0) // 2

        def part(up, down, slope_ref, rise_ref):
            rise = (mm_nt(g_ref[...], down[...]) * slope_ref[...].astype(f32)).astype(bf)
            rise_ref[...] = rise
            return mm_nt(rise, up[...])

        @pl.when(step == 0)
        def _():
            total_ref[...] = part(uo_ref, do_ref, so_ref, rise_o)

        @pl.when((step > 0) & (step < turn))
        def _():
            total_ref[...] += part(uo_ref, do_ref, so_ref, rise_o)

        @pl.when(step >= turn)
        def _():
            total_ref[...] += part(ux_ref, dx_ref, sx_ref, rise_x)

        @pl.when(step == pl.num_programs(0) - 1)
        def _():
            resid = resid_ref[...]
            scale = lax.rsqrt(jnp.mean(resid * resid, axis=-1, keepdims=True) + eps)
            normal = resid * scale
            total = total_ref[...]
            unit = total * gain_ref[1:2, :]
            grad = g_ref[...].astype(f32) + scale * (unit - normal * jnp.mean(unit * normal, axis=-1, keepdims=True))
            grad_ref[...] = grad
            low_ref[...] = grad.astype(bf)
            gsum_ref[...] = jnp.sum(total * normal, axis=0, keepdims=True)


def back_call(at, g, resid, gains, slope_own, slope_oth, up_own, up_oth, down_own, down_oth, chunk=512):
    rows, width = g.shape
    hidden = up_own.shape[1]
    turn = hidden // chunk
    ups, downs, cols = halves_specs(turn, chunk, width, rows)
    sd = jax.ShapeDtypeStruct
    full = pl.BlockSpec((rows, width), lambda i, s: (0, 0))
    hid = sd((rows, hidden), bf)
    line = pl.BlockSpec((1, width), lambda i, s: (0, 0))
    return pl.pallas_call(
        back_kernel,
        grid_spec=pltpu.PrefetchScalarGridSpec(
            num_scalar_prefetch=1,
            grid=(2 * turn,),
            in_specs=[full, full, pl.BlockSpec(gains.shape, lambda i, s: (0, 0)), *cols, *ups, *downs],
            out_specs=(*cols, full, full, line),
            scratch_shapes=[pltpu.VMEM((rows, width), f32)],
        ),
        out_shape=(hid, hid, sd((rows, width), f32), sd((rows, width), bf), sd((1, width), f32)),
        compiler_params=pltpu.CompilerParams(vmem_limit_bytes=60 * 1024 * 1024),
        cost_estimate=lasting(13),
        name="global_backward",
    )(at, g, resid, gains, slope_own, slope_oth, up_own, up_oth, down_own, down_oth)


def split_sides(total, side, mine_ref, theirs_ref, at):
    half = total.shape[0] // 2
    top, bottom = total[:half].astype(bf), total[half:].astype(bf)
    mine_ref[at] = jnp.where(side == 0, top, bottom)
    theirs_ref[at] = jnp.where(side == 0, bottom, top)


def weight_kernel(at_ref, gl, gli, gr, gri, ll, lli, lr, lri, mine_ref, theirs_ref, *, plane_first):
    step = pl.program_id(0)

    def store(total):
        if not plane_first:
            split_sides(total, at_ref[2], mine_ref, theirs_ref, 0)
            return
        half = total.shape[0] // 2
        top, bottom = total[:half].astype(bf), total[half:].astype(bf)
        flip = at_ref[2] == 0
        near, far_side = jnp.where(flip, top, bottom), jnp.where(flip, bottom, top)

        @pl.when(step < 2)
        def _():
            theirs_ref[0, 0] = near
            theirs_ref[1, 0] = far_side

        @pl.when(step >= 2)
        def _():
            mine_ref[0, 0] = near
            mine_ref[1, 0] = far_side

    @pl.when(at_ref[0] == 0)
    def _():
        store(across_rows(gl[...], gr[...]) + across_rows(gli[...], gri[...]))

    @pl.when(at_ref[0] == 1)
    def _():
        store(across_rows(ll[...], lr[...]) + across_rows(lli[...], lri[...]))


def weight_call(at, four_global, four_local, plane_first, name):
    width = four_global[0].shape[1]
    cols = four_global[2].shape[1]
    piece = width // 8
    once = pl.Buffered(1)

    def turn(i):
        return jnp.where(i < 2, 2 * i + 1, 2 * i - 4) if plane_first else i

    def left(a, here):
        return pl.BlockSpec((a.shape[0], 2 * piece), lambda i, s: (0, jnp.where(s[0] == here, s[1] ^ turn(i), 0)))

    def right(a):
        return pl.BlockSpec(a.shape, lambda i, s: (0, 0), pipeline_mode=once)

    def specs(four, here):
        return [left(four[0], here), left(four[1], here), right(four[2]), right(four[3])]

    if plane_first:
        shape = jax.ShapeDtypeStruct((2, 2, piece, cols), bf)
        outs = (
            pl.BlockSpec((2, 1, piece, cols), lambda i, s: (0, jnp.maximum(i - 2, 0), 0, 0)),
            pl.BlockSpec((2, 1, piece, cols), lambda i, s: (0, jnp.minimum(i, 1), 0, 0)),
        )
    else:
        shape = jax.ShapeDtypeStruct((4, piece, cols), bf)
        outs = (pl.BlockSpec((1, piece, cols), lambda i, s: ((i % 2) * 2 + i // 2, 0, 0)),) * 2
    return pl.pallas_call(
        functools.partial(weight_kernel, plane_first=plane_first),
        grid_spec=pltpu.PrefetchScalarGridSpec(
            num_scalar_prefetch=1,
            grid=(4,),
            in_specs=specs(four_global, 0) + specs(four_local, 1),
            out_specs=outs,
        ),
        out_shape=(shape, shape),
        compiler_params=pltpu.CompilerParams(vmem_limit_bytes=60 * 1024 * 1024),
        cost_estimate=lasting(10),
        name=name,
    )(at, *four_global, *four_local)


def rest_kernel(at_ref, gl, gn, ga, gq, gk, gv, ll, lli, ln, lni, la, lai, lp, lpi, mine_ref, theirs_ref):
    size = la.shape[1]
    side = at_ref[2]

    def put(block, total):
        half = total.shape[0] // 2
        cols = slice(block, block + total.shape[1])
        top, bottom = total[:half].astype(bf), total[half:].astype(bf)
        mine_ref[0, :, cols] = jnp.where(side == 0, top, bottom)
        theirs_ref[0, :, cols] = jnp.where(side == 0, bottom, top)

    for which in range(2):

        @pl.when((at_ref[0] == 0) & (side == which))
        def _():
            for j, (left, right) in enumerate(((gl, ga), (gn, gq), (gn, gk), (gn, gv))):
                total = across_rows(left[...], right[...])
                start = j * size
                put(start + which * (size // 2), total)
                put(start + (1 - which) * (size // 2), jnp.zeros_like(total))

    @pl.when(at_ref[0] == 1)
    def _():
        put(0, across_rows(ll[...], la[...]) + across_rows(lli[...], lai[...]))
        for j in range(3):
            put((j + 1) * size, across_rows(ln[...], lp[j]) + across_rows(lni[...], lpi[j]))


def rest_call(at, g_low, g_normed, g_att, g_packs, l_low, l_low_in, l_normed, l_normed_in, l_att, l_att_in, l_pack, l_pack_in):
    piece = g_low.shape[1] // 8
    cols = 4 * l_att.shape[1]
    once = pl.Buffered(1)
    left = lambda a: pl.BlockSpec((a.shape[0], 2 * piece), lambda i, s: (0, s[1] ^ i))
    right = lambda a: pl.BlockSpec(a.shape, lambda i, s: (0,) * a.ndim, pipeline_mode=once)
    lefts, rights = (l_low, l_low_in, l_normed, l_normed_in), (l_att, l_att_in, l_pack, l_pack_in)
    shape = jax.ShapeDtypeStruct((4, piece, cols), bf)
    return pl.pallas_call(
        rest_kernel,
        grid_spec=pltpu.PrefetchScalarGridSpec(
            num_scalar_prefetch=1,
            grid=(4,),
            in_specs=[left(g_low), left(g_normed), right(g_att), *map(right, g_packs), *map(left, lefts), *map(right, rights)],
            out_specs=(pl.BlockSpec((1, piece, cols), lambda i, s: ((i % 2) * 2 + i // 2, 0, 0)),) * 2,
        ),
        out_shape=(shape, shape),
        compiler_params=pltpu.CompilerParams(vmem_limit_bytes=60 * 1024 * 1024),
        cost_estimate=lasting(0.01),
        name="rest_gradient",
    )(at, g_low, g_normed, g_att, *g_packs, *lefts, *rights)


def fall_kernel(at_ref, resid_ref, ao_ref, ax_ref, do_ref, dx_ref, out_ref, total_ref):
    step = pl.program_id(0)
    turn = pl.num_programs(0) // 2
    books, planes, half = out_ref.shape[1], out_ref.shape[0], out_ref.shape[2]

    @pl.when(at_ref[0] == 1)
    def _():
        @pl.when(step == 0)
        def _():
            total_ref[...] = resid_ref[...]

        @pl.when(step < turn)
        def _():
            total_ref[...] += mm(ao_ref[...], do_ref[...])

        @pl.when(step >= turn)
        def _():
            total_ref[...] += mm(ax_ref[...], dx_ref[...])

        @pl.when(step == pl.num_programs(0) - 1)
        def _():
            for c in range(books):
                for z in range(planes):
                    first = (c * planes + z) * half
                    out_ref[z, c] = total_ref[first : first + half, :].astype(bf)


def fall_call(at, resid, act_own, act_oth, down_own, down_oth, planes, books, chunk=512):
    rows, width = resid.shape
    turn = down_own.shape[0] // chunk
    first = lambda i, s: jnp.minimum(i, turn - 1) * s[0]
    later = lambda i, s: jnp.maximum(i - turn, 0) * s[0]
    col = lambda f: pl.BlockSpec((rows, chunk), lambda i, s: (0, f(i, s)))
    row = lambda f: pl.BlockSpec((chunk, width), lambda i, s: (f(i, s), 0))
    shape = (planes, books, rows // planes // books, width)
    return pl.pallas_call(
        fall_kernel,
        grid_spec=pltpu.PrefetchScalarGridSpec(
            num_scalar_prefetch=1,
            grid=(2 * turn,),
            in_specs=[pl.BlockSpec((rows, width), lambda i, s: (0, 0), pipeline_mode=pl.Buffered(1)), col(first), col(later), row(first), row(later)],
            out_specs=pl.BlockSpec(shape, lambda i, s: (0, 0, 0, 0)),
            scratch_shapes=[pltpu.VMEM((rows, width), f32)],
        ),
        out_shape=jax.ShapeDtypeStruct(shape, bf),
        compiler_params=pltpu.CompilerParams(vmem_limit_bytes=60 * 1024 * 1024),
        cost_estimate=lasting(7),
        name="local_output",
    )(at, resid, act_own, act_oth, down_own, down_oth)


def table_kernel(at_ref, code_ref, code_in_ref, own_ref, got_ref, low_ref, high_ref, total_ref):
    entries = total_ref.shape[0]
    slots = lax.broadcasted_iota(jnp.int32, (entries, code_ref.shape[2]), 0)
    piece = low_ref.shape[3]

    @pl.when(at_ref[0] == 1)
    def _():
        hot = (slots == code_ref[0]).astype(f32).astype(bf)
        hot_in = (slots == code_in_ref[0]).astype(f32).astype(bf)
        total_ref[...] = mm(hot, own_ref[0]) + mm(hot_in, got_ref[0])
        for jz in range(4):
            for jy in range(2):
                place = (at_ref[1] ^ jz) * 2 + (at_ref[2] ^ jy)
                spot = (jz % 2) * 2 + jz // 2
                for ref, base in ((low_ref, 0), (high_ref, entries // 2)):
                    rows = pl.ds(pl.multiple_of(base + place * piece, piece), piece)
                    ref[jy, spot, 0] = total_ref[rows, :].astype(bf)


def table_call(at, codes, codes_in, own, got, entries):
    books, rows = codes.shape
    width = own.shape[2]
    line = pl.BlockSpec((1, 1, rows), lambda c, s: (c, 0, 0))
    block = pl.BlockSpec((1, rows, width), lambda c, s: (c, 0, 0))
    shape = (2, 4, books, entries // 16, width)
    out = pl.BlockSpec((2, 4, 1, entries // 16, width), lambda c, s: (0, 0, c, 0, 0))
    return pl.pallas_call(
        table_kernel,
        grid_spec=pltpu.PrefetchScalarGridSpec(
            num_scalar_prefetch=1,
            grid=(books,),
            in_specs=[line, line, block, block],
            out_specs=(out, out),
            scratch_shapes=[pltpu.VMEM((entries, width), f32)],
        ),
        out_shape=(jax.ShapeDtypeStruct(shape, bf),) * 2,
        compiler_params=pltpu.CompilerParams(vmem_limit_bytes=60 * 1024 * 1024),
        cost_estimate=lasting(4),
        name="table_gradient",
    )(at, codes[:, None, :], codes_in[:, None, :], own, got)


def prepare_kernel(at_ref, code_ref, cot_ref, do_ref, dx_ref, table_ref, look_ref, po_ref, px_ref):
    step = pl.program_id(0)
    turn = pl.num_programs(0) // 2
    books, rows, chunk = po_ref.shape

    @pl.when(at_ref[0] == 1)
    def _():
        @pl.when(step < look_ref.shape[0])
        def _():
            slots = lax.broadcasted_iota(jnp.int32, (rows, table_ref.shape[1]), 1)
            hot = (slots == code_ref[jnp.minimum(step, look_ref.shape[0] - 1)]).astype(f32).astype(bf)
            look_ref[jnp.minimum(step, look_ref.shape[0] - 1)] = mm(hot, table_ref[0]).astype(bf)

        @pl.when(step < turn)
        def _():
            po_ref[...] = mm_nt(cot_ref[...], do_ref[...]).astype(bf).reshape(books, rows, chunk)

        @pl.when(step >= turn)
        def _():
            px_ref[...] = mm_nt(cot_ref[...], dx_ref[...]).astype(bf).reshape(books, rows, chunk)


def prepare_call(at, codes, cot, down_own, down_oth, table, chunk=512):
    books, rows = codes.shape
    width = cot.shape[1]
    hidden = down_own.shape[0]
    turn = hidden // chunk
    first = lambda i, s: jnp.minimum(i, turn - 1) * s[0]
    later = lambda i, s: jnp.maximum(i - turn, 0) * s[0]
    down = lambda f: pl.BlockSpec((chunk, width), lambda i, s: (f(i, s), 0))
    out = lambda f: pl.BlockSpec((books, rows, chunk), lambda i, s: (0, 0, f(i, s)))
    sd = jax.ShapeDtypeStruct
    return pl.pallas_call(
        prepare_kernel,
        grid_spec=pltpu.PrefetchScalarGridSpec(
            num_scalar_prefetch=1,
            grid=(2 * turn,),
            in_specs=[
                pl.BlockSpec((books, rows, 1), lambda i, s: (0, 0, 0)),
                pl.BlockSpec(cot.shape, lambda i, s: (0, 0)),
                down(first),
                down(later),
                pl.BlockSpec((1,) + table.shape[1:], lambda i, s: (jnp.minimum(i, books - 1) * s[0], 0, 0)),
            ],
            out_specs=(pl.BlockSpec((books, rows, width), lambda i, s: (0, 0, 0)), out(first), out(later)),
        ),
        out_shape=(sd((books, rows, width), bf), sd((books, rows, hidden), bf), sd((books, rows, hidden), bf)),
        compiler_params=pltpu.CompilerParams(vmem_limit_bytes=60 * 1024 * 1024),
        cost_estimate=lasting(5),
        name="local_prepare",
    )(at, codes[:, :, None], cot, down_own, down_oth, table)


def fence(*groups):
    return lax.optimization_barrier(groups)


def body(frames, codes, lengths, gains, w_qkv, w_out, w_up, w_down, table, cotangent):
    batches, share, width = frames.shape
    members = lax.axis_size("dp") // batches
    if (
        lax.axis_size("section") != 2
        or lax.axis_size("tensor") != 2
        or members != 2
        or lax.axis_size("dp") != 2 * batches
        or batches & (batches - 1)
        or share % 32
        or table.shape[1] != width
    ):
        return plain_body(frames, codes, lengths, gains, w_qkv, w_out, w_up, w_down, table, cotangent)
    place, core = lax.axis_index("dp"), lax.axis_index("tensor")
    plane, side = place // members, place % members
    on_first = lax.axis_index("section") == 0
    half = share // 2
    rows = batches * half
    count = 2 * batches
    at = jnp.stack([lax.axis_index("section"), plane, side]).astype(jnp.int32)

    everywhere, first, second = (0, 1), (0,), (1,)

    def linked(a, flip_place, flip_core, sections=everywhere):
        pairs = [
            ((z * count + i) * 2 + j, (z * count + (i ^ flip_place)) * 2 + (j ^ flip_core))
            for z in sections
            for i in range(count)
            for j in range(2)
        ]
        return lax.ppermute(a, ("section", "dp", "tensor"), pairs)

    def core_swap(a, sections=everywhere):
        return linked(a, 0, 1, sections)

    def side_swap(a, sections=everywhere):
        return linked(a, 1, 0, sections)

    def both_swap(a, sections=everywhere):
        return linked(a, 1, 1, sections)

    def to_local(a):
        return lax.ppermute(a, "section", [(0, 1)])

    def to_global(a):
        return lax.ppermute(a, "section", [(1, 0)])

    def planes_in(a, sections=everywhere):
        pieces = [lax.dynamic_slice_in_dim(a, plane ^ k, 1, 0) for k in range(batches)]
        return jnp.concatenate([pieces[0], *(linked(pieces[k], 2 * k, 0, sections) for k in range(1, batches))], 0)

    def planes_out(a, sections=everywhere):
        got = [a[:1], *(linked(a[k : k + 1], 2 * k, 0, sections) for k in range(1, batches))]
        out = jnp.zeros_like(a)
        for k in range(batches):
            out = lax.dynamic_update_slice_in_dim(out, got[k], plane ^ k, 0)
        return out

    def core_half(a, axis):
        return lax.dynamic_slice_in_dim(a, core * half, half, axis)

    def join_cores(a, axis):
        other = core_swap(a)
        return jnp.where(core == 0, jnp.concatenate([a, other], axis), jnp.concatenate([other, a], axis))

    def quarter(a, axis):
        size = a.shape[axis] // 2
        return lax.dynamic_slice_in_dim(a, side * size, size, axis)

    def by_side(mine, theirs, axis):
        return jnp.where(side == 0, jnp.concatenate([mine, theirs], axis), jnp.concatenate([theirs, mine], axis))

    x_own = planes_in(core_half(frames, 1), first).reshape(rows, width)
    x_side = side_swap(x_own, first)
    x_core, x_both = core_swap(x_own), core_swap(x_side)
    (x_core, x_both), (w_qkv, w_out, w_up, w_down, cotangent, codes) = fence(
        (x_core, x_both), (w_qkv, w_out, w_up, w_down, cotangent, codes)
    )
    x_all = jnp.concatenate([x_own, x_side, x_core, x_both], 0)

    gains_here = gains[0]
    proj_own = w_qkv[0].transpose(1, 0, 2)
    out_own, up_own, down_own = w_out[0], w_up[0], w_down[0]
    out_oth, up_oth, down_oth = (core_swap(w) for w in (out_own, up_own, down_own))
    proj_oth = core_swap(proj_own)

    def positions(jt, js):
        base = ((jnp.arange(batches)[:, None] ^ plane) * 2 + (side ^ js)) * share + (core ^ jt) * half
        return (base + jnp.arange(half)[None, :]).reshape(-1)

    pos = jnp.concatenate([positions(0, 0), positions(0, 1), positions(1, 0), positions(1, 1)]).astype(jnp.int32)
    doc_ends = jnp.cumsum(lax.dynamic_index_in_dim(lengths, plane, 0, keepdims=False))
    doc = doc_index(pos, doc_ends)
    qid = jnp.stack([pos, doc], 1)
    kid = jnp.stack([pos, jnp.where(pos < doc_ends[-1], doc, -1)], 0)

    x_all32 = x_all.astype(f32)
    all_scale = rms_scale(x_all32)
    normed_all = (x_all32 * all_scale * gains_here[0]).astype(bf)
    proj_mine = quarter(proj_own, 2)
    q, k, v = (matmul(normed_all, proj_mine[j]).astype(bf) for j in range(3))
    attended = attend_call(at, q, k, v, qid, kid, rows)
    parts = attended.reshape(4, rows, -1)
    att_own = by_side(parts[0], side_swap(parts[1], first), 1)
    att_oth = by_side(core_swap(parts[2]), both_swap(parts[3], first), 1)
    x32 = x_own.astype(f32)
    resid, mid, act_own, act_oth, slope_own, slope_oth, global_low = front_call(
        at, x_own, att_own, att_oth, gains_here, out_own, out_oth, up_own, up_oth, down_own, down_oth
    )
    mid_in, act_in = core_swap(mid), core_swap(act_oth)

    arrived = to_local(global_low)
    cot = planes_in(core_half(cotangent.transpose(0, 2, 1, 3), 2), second).transpose(1, 0, 2, 3).reshape(CODEBOOKS, rows, width)
    codes_own = planes_in(core_half(codes.transpose(0, 2, 1), 2), second).transpose(1, 0, 2).reshape(CODEBOOKS, rows)
    slots = jnp.arange(table.shape[1], dtype=jnp.int32)
    cot_rows = cot.reshape(-1, width)
    cot_in = core_swap(cot_rows)

    looked_up, pull_own, pull_oth = prepare_call(at, codes_own, cot_rows, down_own, down_oth, table)
    (
        l_normed, l_att_own, l_att_oth, l_resid, l_mid, l_act_own, l_act_oth, l_rise_own, l_rise_oth,
        l_low, l_pack_own, l_pack_oth, l_grad, l_frame, l_gains,
    ) = local_call(
        arrived, looked_up, cot, pull_own, pull_oth, gains_here, proj_own, proj_oth, out_own, out_oth, up_own, up_oth
    )
    global_moved = planes_out(jnp.where(on_first, global_low, arrived).reshape(batches, half, width))
    grad_low = to_global(l_frame.astype(bf))

    flat = lambda a: a.reshape(-1, a.shape[-1])

    def swap(a, bit):
        return lax.ppermute(a, "dp", [(i, i ^ (1 << bit)) for i in range(count)])

    def meet(mine, got):
        return (mine.astype(f32) + got.astype(f32)).astype(bf)

    def cols_of(a, which):
        return lax.dynamic_slice_in_dim(a, which * (width // 2), width // 2, 2)

    l_act_in = core_swap(flat(l_act_oth))
    l_got, codes_oth = core_swap(cols_of(l_grad, 1 - core)), core_swap(codes_own)
    l_rise_in, l_mid_in = core_swap(flat(l_rise_oth)), core_swap(flat(l_mid))
    l_low_in, l_att_in = core_swap(flat(l_low)), core_swap(flat(l_att_oth))
    l_normed_in, l_pack_in = core_swap(flat(l_normed)), core_swap(l_pack_oth)
    local_low = fall_call(at, flat(l_resid), flat(l_act_own), flat(l_act_oth), down_own, down_oth, batches, CODEBOOKS)
    table_low, table_high = table_call(at, codes_own, codes_oth, cols_of(l_grad, core), l_got, table.shape[1])
    (local_low, table_low, table_high), (grad_low,) = fence((local_low, table_low, table_high), (grad_low,))

    grad_in_low = core_swap(grad_low)
    rise_own, rise_oth, grad_resid, low_own, gain_mid = back_call(
        at, grad_low, resid, gains_here, slope_own, slope_oth, up_own, up_oth, down_own, down_oth
    )
    rise_in = core_swap(rise_oth)
    (low_own, grad_in_low, table_low, local_low), = fence((low_own, grad_in_low, table_low, local_low))
    low_side = side_swap(low_own, first)
    down_mine, down_theirs = weight_call(
        at, (grad_low, grad_in_low, act_own, act_in), (cot_rows, cot_in, flat(l_act_own), l_act_in), True, "down_gradient"
    )
    (down_theirs,), (rise_in,) = fence((down_theirs,), (rise_in,))
    down_got = swap(down_theirs, 1)
    up_mine, up_theirs = weight_call(
        at, (mid, mid_in, rise_own, rise_in), (flat(l_mid), l_mid_in, flat(l_rise_own), l_rise_in), False, "up_gradient"
    )
    (up_theirs, low_side, local_low, table_low), = fence((up_theirs, low_side, local_low, table_low))
    up_got = swap(up_theirs, 0)
    table_moved = to_global(table_low)
    local_moved = planes_out(local_low, second)
    low_all = jnp.concatenate([low_own, low_side, core_swap(low_own), core_swap(low_side)], 0)
    grad_att = against_rows(low_all, quarter(out_own, 0)).astype(bf)
    grad_packs = attend_back_call(at, q, k, v, grad_att, qid, kid, rows)
    part_normed = sum(against_rows(g, proj_mine[j]) for j, g in enumerate(grad_packs))
    pair = part_normed[: 2 * rows] + core_swap(part_normed[2 * rows :].astype(bf)).astype(f32)
    pair_side = side_swap(pair[rows:].astype(bf), first)
    rest_mine, rest_theirs = rest_call(
        at, low_all, normed_all, attended, grad_packs, flat(l_low), l_low_in, flat(l_normed), l_normed_in,
        flat(l_att_own), l_att_in, *(a.reshape(3, CODEBOOKS * rows, -1) for a in (l_pack_own, l_pack_in)),
    )
    (rest_theirs, down_got, up_got, pair_side, local_moved, global_moved), = fence(
        (rest_theirs, down_got, up_got, pair_side, local_moved, global_moved)
    )
    rest_got = swap(rest_theirs, 0)
    local_sent = to_global(local_moved)
    up_now = meet(up_mine, up_got)
    up_got = swap(up_now[2:], 1)
    grad_normed = pair[:rows] + pair_side.astype(f32)
    back_in, gain_in = rms_back(x32, gains_here[0], grad_normed)
    grad_frames = grad_resid + back_in
    inner = planes_out(jnp.where(on_first, grad_frames, l_frame).astype(bf).reshape(batches, half, width))
    gain_sum = jnp.where(on_first, jnp.concatenate([gain_in[None], gain_mid]), l_gains)
    gain_sum = (gain_sum + core_swap(gain_sum)).reshape(2, batches, 2, -1)
    down_now = meet(down_mine, down_got)
    (rest_got, up_got, down_now, inner, table_moved, gain_sum), = fence(
        (rest_got, up_got, down_now, inner, table_moved, gain_sum)
    )
    down_got = swap(down_now[1], 0)
    piece = width // count
    gain_rows = [
        [
            lax.dynamic_slice(gain_sum, (0, plane ^ (2 * j + i), side ^ y, 0), (2, 1, 1, piece)).reshape(1, -1)
            for i in range(2)
            for j in range(2)
        ]
        for y in range(2)
    ]
    table_now = jnp.where(on_first, table_moved, table_high).reshape(2, batches, -1, width // 2)
    filler = ((0, 15), (0, width // 2 - 2 * piece))
    table_now = jnp.concatenate(
        [table_now, jnp.stack([jnp.stack([jnp.pad(g.astype(bf), filler) for g in four]) for four in gain_rows])], 2
    )
    table_got = swap(table_now[1], 0)
    up_now = meet(up_now[:2], up_got)
    up_got = swap(up_now[1], 2)
    rest_now = meet(rest_mine, rest_got)
    rest_got = swap(rest_now[2:], 1)
    (rest_got, up_got, down_got, table_got, local_sent), = fence((rest_got, up_got, down_got, table_got, local_sent))
    down_now = meet(down_now[0], down_got)
    down_got = swap(down_now[1], 2)
    rest_now = meet(rest_now[:2], rest_got)
    rest_got = swap(rest_now[1], 2)
    table_now = meet(table_now[0], table_got)
    table_got = swap(table_now[2:], 1)
    up_share = up_now[0].astype(f32) + up_got.astype(f32)
    table_now = meet(table_now[:2], table_got)
    table_got = swap(table_now[1], 2)
    down_share = down_now[0].astype(f32) + down_got.astype(f32)
    rest_share = rest_now[0].astype(f32) + rest_got.astype(f32)
    table_now = table_now[0].astype(f32) + table_got.astype(f32)
    gain_share = table_now[-16, : 2 * piece].reshape(2, piece)
    grad_table = join_cores(table_now[:-16].reshape(CODEBOOKS, -1, width // 2).astype(bf), 2).astype(f32)

    global_out = join_cores(global_moved, 1)
    local_out = join_cores(jnp.where(on_first, local_sent, local_moved), 2).transpose(0, 2, 1, 3)
    input_grads = join_cores(inner, 1)
    hidden = out_own.shape[0]
    proj_share = rest_share[:, hidden:].reshape(piece, 3, hidden)
    return (
        global_out,
        local_out,
        input_grads.astype(f32)[None],
        proj_share[None],
        rest_share[:, :hidden].T[None],
        up_share[None],
        down_share.T[None],
        gain_share[None],
        grad_table,
    )


def solution(mesh):
    in_specs = (
        P(None, "dp", None),
        P(None, "dp", None),
        P(),
        P("section", None, None),
        P("section", None, None, "tensor"),
        P("section", "tensor", None),
        P("section", None, "tensor"),
        P("section", "tensor", None),
        P(),
        P(None, "dp", None, None),
    )
    out_specs = (
        P(None, "dp", None),
        P(None, "dp", None, None),
        P("section", None, "dp", None),
        P("section", "dp", None, "tensor"),
        P("section", "tensor", "dp"),
        P("section", "dp", "tensor"),
        P("section", "tensor", "dp"),
        P("section", None, "dp"),
        P(None, ("section", "dp"), None),
    )
    return jax.shard_map(body, mesh=mesh, in_specs=in_specs, out_specs=out_specs, check_vma=False)
```

```python
import functools

import jax
import jax.numpy as jnp
from jax import lax
from jax.experimental import pallas as pl
from jax.experimental.pallas import tpu as pltpu
from jax.sharding import PartitionSpec as P

HEAD = 64
CODEBOOKS = 3


eps = 1e-05
far = -1e30


def from_behind(block, axis, distance):
    devices = range(lax.axis_size(axis))
    route = [(i - distance, i) for i in devices if i - distance in devices]
    return lax.ppermute(block, axis, route)


def rms_scale(values):
    return lax.rsqrt(jnp.mean(values * values, axis=-1, keepdims=True) + eps)


def rms_back(values, gain_row, grad_normed):
    factor = rms_scale(values)
    normal = values * factor
    grad_unit = grad_normed * gain_row
    grad_values = factor * (
        grad_unit - normal * jnp.mean(grad_unit * normal, axis=-1, keepdims=True)
    )
    return (grad_values, jnp.sum(grad_normed * normal, axis=0))


def head_total(partial_sum):
    return lax.psum(partial_sum, "tensor")


def matmul(left, right):
    return jnp.dot(left, right, preferred_element_type=jnp.float32)


def across_rows(left, right):
    return lax.dot_general(
        left, right, (((0,), (0,)), ((), ())), preferred_element_type=jnp.float32
    )


def against_rows(left, right):
    return lax.dot_general(
        left, right, (((1,), (1,)), ((), ())), preferred_element_type=jnp.float32
    )


def smooth_gate(values):
    return jax.nn.gelu(values, approximate=True)


def doc_index(positions, doc_ends):
    return jnp.sum((positions[:, None] >= doc_ends[None, :]).astype(jnp.int32), axis=1)


def allowed_mask(query_pos, key_pos, doc_ends):
    same_doc = doc_index(query_pos, doc_ends)[:, None] == doc_index(key_pos, doc_ends)[None, :]
    earlier = key_pos[None, :] <= query_pos[:, None]
    live = (key_pos < doc_ends[-1])[None, :]
    return same_doc & earlier & live | (key_pos[None, :] == query_pos[:, None])


def masked_softmax(scores, mask, factor):
    logits = jnp.where(mask, scores * factor, far)
    top = jnp.max(logits, axis=-1, keepdims=True)
    weights = jnp.exp(logits - top)
    mass = jnp.sum(weights, axis=-1, keepdims=True)
    return (weights / mass, (top + jnp.log(mass))[..., 0])


def frame_forward(packed, query_pos, doc_ends, head_count):
    row_count = packed.shape[0]
    width = packed.shape[1] // 3
    factor = HEAD ** (-0.5)
    parts = packed.reshape(row_count, 3, width)
    all_keys, all_values = (
        lax.all_gather(parts[:, 1], "dp", axis=0, tiled=True),
        lax.all_gather(parts[:, 2], "dp", axis=0, tiled=True),
    )
    key_count = all_keys.shape[0]
    key_pos = jnp.arange(key_count, dtype=jnp.int32)
    mask = allowed_mask(query_pos, key_pos, doc_ends)
    queries = parts[:, 0].reshape(row_count, head_count, -1)
    scores = jnp.einsum(
        "qhe,khe->hqk",
        queries,
        all_keys.reshape(key_count, head_count, -1),
        preferred_element_type=jnp.float32,
    )
    probs, log_mass = masked_softmax(scores, mask[None], factor)
    attended = jnp.einsum(
        "hqk,khe->qhe",
        probs.astype(jnp.bfloat16),
        all_values.reshape(key_count, head_count, -1),
        preferred_element_type=jnp.float32,
    )
    return (attended.reshape(row_count, width), log_mass)


def frame_backward(packed, grad_att, log_mass, query_pos, doc_ends, head_count):
    row_count = packed.shape[0]
    width = packed.shape[1] // 3
    factor = HEAD ** (-0.5)
    parts = packed.reshape(row_count, 3, width)
    all_keys, all_values = (
        lax.all_gather(parts[:, 1], "dp", axis=0, tiled=True),
        lax.all_gather(parts[:, 2], "dp", axis=0, tiled=True),
    )
    key_count = all_keys.shape[0]
    key_pos = jnp.arange(key_count, dtype=jnp.int32)
    queries = parts[:, 0].reshape(row_count, head_count, -1)
    grad_heads = grad_att.reshape(row_count, head_count, -1)
    keys_heads = all_keys.reshape(key_count, head_count, -1)
    scores = jnp.einsum("qhe,khe->hqk", queries, keys_heads, preferred_element_type=jnp.float32)
    mask = allowed_mask(query_pos, key_pos, doc_ends)
    probs = jnp.exp(jnp.where(mask[None], scores * factor, far) - log_mass[:, :, None])
    grad_probs = jnp.einsum(
        "qhe,khe->hqk",
        grad_heads,
        all_values.reshape(key_count, head_count, -1),
        preferred_element_type=jnp.float32,
    )
    spread = jnp.sum(probs * grad_probs, axis=-1)
    grad_scores = (probs * (grad_probs - spread[:, :, None]) * factor).astype(jnp.bfloat16)
    grad_queries = jnp.einsum(
        "hqk,khe->qhe", grad_scores, keys_heads, preferred_element_type=jnp.float32
    ).reshape(row_count, width)
    keys_term = jnp.einsum(
        "hqk,qhe->khe", grad_scores, queries, preferred_element_type=jnp.float32
    ).reshape(key_count, width)
    values_term = jnp.einsum(
        "hqk,qhe->khe", probs.astype(jnp.bfloat16), grad_heads, preferred_element_type=jnp.float32
    ).reshape(key_count, width)
    grad_keys, grad_values = (
        lax.psum_scatter(keys_term, "dp", scatter_dimension=0, tiled=True),
        lax.psum_scatter(values_term, "dp", scatter_dimension=0, tiled=True),
    )
    return jnp.stack([grad_queries, grad_keys, grad_values], axis=1).reshape(row_count, 3 * width)


def codebook_forward(packed, head_count):
    row_count = packed.shape[0]
    width = packed.shape[1] // 3
    factor = HEAD ** (-0.5)
    parts = packed.reshape(row_count // CODEBOOKS, CODEBOOKS, 3, head_count, -1)
    scores = jnp.einsum(
        "nche,ndhe->nhcd", parts[:, :, 0], parts[:, :, 1], preferred_element_type=jnp.float32
    )
    order = jnp.arange(CODEBOOKS, dtype=jnp.int32)
    mask = order[None, :] <= order[:, None]
    probs, log_mass = masked_softmax(scores, mask, factor)
    attended = jnp.einsum(
        "nhcd,ndhe->nche",
        probs.astype(jnp.bfloat16),
        parts[:, :, 2],
        preferred_element_type=jnp.float32,
    )
    return (attended.reshape(row_count, width), probs)


def codebook_backward(packed, grad_att, probs, head_count):
    row_count = packed.shape[0]
    width = packed.shape[1] // 3
    factor = HEAD ** (-0.5)
    parts = packed.reshape(row_count // CODEBOOKS, CODEBOOKS, 3, head_count, -1)
    grad_heads = grad_att.reshape(row_count // CODEBOOKS, CODEBOOKS, head_count, -1)
    grad_probs = jnp.einsum(
        "nche,ndhe->nhcd", grad_heads, parts[:, :, 2], preferred_element_type=jnp.float32
    )
    spread = jnp.sum(probs * grad_probs, axis=-1, keepdims=True)
    grad_scores = (probs * (grad_probs - spread) * factor).astype(jnp.bfloat16)
    grad_queries = jnp.einsum(
        "nhcd,ndhe->nche", grad_scores, parts[:, :, 1], preferred_element_type=jnp.float32
    )
    grad_keys = jnp.einsum(
        "nhcd,nche->ndhe", grad_scores, parts[:, :, 0], preferred_element_type=jnp.float32
    )
    grad_values = jnp.einsum(
        "nhcd,nche->ndhe",
        probs.astype(jnp.bfloat16),
        grad_heads,
        preferred_element_type=jnp.float32,
    )
    return jnp.stack([grad_queries, grad_keys, grad_values], axis=2).reshape(row_count, 3 * width)


def layer_forward(inputs, gain_pair, layer_weights, attend):
    w_proj, w_mix, w_rise, w_fall = layer_weights
    normed = (inputs * rms_scale(inputs) * gain_pair[0]).astype(jnp.bfloat16)
    packed = matmul(normed, w_proj.reshape(w_proj.shape[0], -1)).astype(jnp.bfloat16)
    attended, saved = attend(packed)
    attended_low = attended.astype(jnp.bfloat16)
    resid = inputs + head_total(matmul(attended_low, w_mix))
    normed_mid = (resid * rms_scale(resid) * gain_pair[1]).astype(jnp.bfloat16)
    rise = matmul(normed_mid, w_rise)
    active = smooth_gate(rise).astype(jnp.bfloat16)
    result = resid + head_total(matmul(active, w_fall))
    return (result, (normed, packed, attended_low, saved, resid, normed_mid, rise, active))


def layer_backward(inputs, gain_pair, layer_weights, kept, grad_result, attend_back):
    w_proj, w_mix, w_rise, w_fall = layer_weights
    normed, packed, attended_low, saved, resid, normed_mid, rise, active = kept
    grad_fall_low = grad_result.astype(jnp.bfloat16)
    grad_fall_w = across_rows(active, grad_fall_low)
    grad_active = against_rows(grad_fall_low, w_fall)
    grad_rise = jax.vjp(smooth_gate, rise)[1](grad_active)[0].astype(jnp.bfloat16)
    grad_rise_w = across_rows(normed_mid, grad_rise)
    grad_mid = head_total(against_rows(grad_rise, w_rise))
    back_mid, gain_mid = rms_back(resid, gain_pair[1], grad_mid)
    grad_resid = grad_result + back_mid
    resid_low = grad_resid.astype(jnp.bfloat16)
    grad_mix_w = across_rows(attended_low, resid_low)
    grad_att = against_rows(resid_low, w_mix).astype(jnp.bfloat16)
    grad_packed = attend_back(packed, grad_att, saved).astype(jnp.bfloat16)
    flat_proj = w_proj.reshape(w_proj.shape[0], -1)
    grad_proj_w = across_rows(normed, grad_packed).reshape(w_proj.shape)
    grad_normed = head_total(against_rows(grad_packed, flat_proj))
    back_in, gain_in = rms_back(inputs, gain_pair[0], grad_normed)
    return (
        grad_resid + back_in,
        (grad_proj_w, grad_mix_w, grad_rise_w, grad_fall_w, jnp.stack([gain_in, gain_mid])),
    )


def plain_body(frames, codes, lengths, gains, w_qkv, w_out, w_up, w_down, table, cotangent):
    on_first = lax.axis_index("section") == 0
    head_count = w_qkv.shape[3] // HEAD
    layer_weights = (w_qkv[0], w_out[0], w_up[0], w_down[0])
    gains_here = gains[0]
    frame_count = frames.shape[1]
    query_pos = lax.axis_index("dp") * frame_count + jnp.arange(frame_count, dtype=jnp.int32)
    zero_grads = (
        jnp.zeros(w_qkv.shape[1:], jnp.float32),
        jnp.zeros(w_out.shape[1:], jnp.float32),
        jnp.zeros(w_up.shape[1:], jnp.float32),
        jnp.zeros(w_down.shape[1:], jnp.float32),
        jnp.zeros(gains.shape[1:], jnp.float32),
    )

    def global_forward_rows(frame_rows, slot_lengths):
        doc_ends = jnp.cumsum(slot_lengths)
        return (
            doc_ends,
            layer_forward(
                frame_rows.astype(jnp.float32),
                gains_here,
                layer_weights,
                lambda packed: frame_forward(packed, query_pos, doc_ends, head_count),
            ),
        )

    def global_step(carry, inputs):
        doc_ends, (result, kept) = global_forward_rows(inputs[0], inputs[1])
        return (carry, result.astype(jnp.bfloat16))

    global_low = lax.scan(global_step, jnp.zeros((), jnp.int32), (frames, lengths))[1]
    arrived = from_behind(global_low, "section", 1)
    books = jnp.arange(CODEBOOKS, dtype=jnp.int32)
    looked_up = table[books[None, None, :], codes]
    local_in = arrived.astype(jnp.float32)[:, :, None, :] + looked_up.astype(jnp.float32)
    local_rows = local_in.reshape(-1, local_in.shape[-1])
    local_result, local_kept = layer_forward(
        local_rows, gains_here, layer_weights, lambda packed: codebook_forward(packed, head_count)
    )
    grad_rows, local_grads = layer_backward(
        local_rows,
        gains_here,
        layer_weights,
        local_kept,
        cotangent.astype(jnp.float32).reshape(local_rows.shape),
        lambda packed, grad_att, saved: codebook_backward(packed, grad_att, saved, head_count),
    )
    grad_frame = jnp.sum(grad_rows.reshape(local_in.shape), axis=2)
    table_slots = (books[None, None, :] * table.shape[1] + codes).reshape(-1)
    table_term = jax.ops.segment_sum(
        grad_rows, table_slots, num_segments=table.shape[0] * table.shape[1]
    ).reshape(table.shape)
    local_low = local_result.astype(jnp.bfloat16).reshape(cotangent.shape)
    table_part = jnp.where(on_first, jnp.zeros(table.shape, jnp.float32), table_term)
    grad_frame = jnp.where(on_first, jnp.zeros(frames.shape, jnp.float32), grad_frame)
    grad_table = lax.psum_scatter(table_part, ("section", "dp"), scatter_dimension=1, tiled=True)
    grad_back, local_copy = from_behind((grad_frame.astype(jnp.bfloat16), local_low), "section", -1)

    def global_back(totals, inputs):
        frame_rows, slot_lengths, grad_low = inputs
        doc_ends, (result, kept) = global_forward_rows(frame_rows, slot_lengths)
        grad_in, grads = layer_backward(
            frame_rows.astype(jnp.float32),
            gains_here,
            layer_weights,
            kept,
            grad_low.astype(jnp.float32),
            lambda packed, grad_att, saved: frame_backward(
                packed, grad_att, saved, query_pos, doc_ends, head_count
            ),
        )
        return (jax.tree.map(jnp.add, totals, grads), grad_in)

    global_grads, grad_frames = lax.scan(global_back, zero_grads, (frames, lengths, grad_back))

    def pick(global_part, local_part):
        return jnp.where(on_first, global_part, local_part)

    proj_sum, mix_sum, rise_sum, fall_sum, gain_sum = jax.tree.map(pick, global_grads, local_grads)
    proj_share, mix_share, rise_share, fall_share, gain_share = (
        lax.psum_scatter(proj_sum, "dp", scatter_dimension=0, tiled=True),
        lax.psum_scatter(mix_sum, "dp", scatter_dimension=1, tiled=True),
        lax.psum_scatter(rise_sum, "dp", scatter_dimension=0, tiled=True),
        lax.psum_scatter(fall_sum, "dp", scatter_dimension=1, tiled=True),
        lax.psum_scatter(gain_sum, "dp", scatter_dimension=1, tiled=True),
    )
    global_out = jnp.where(on_first, global_low, arrived)
    local_out = jnp.where(on_first, local_copy, local_low)
    input_grads = jnp.where(on_first, grad_frames, grad_frame)[None]
    return (
        global_out,
        local_out,
        input_grads,
        proj_share[None],
        mix_share[None],
        rise_share[None],
        fall_share[None],
        gain_share[None],
        grad_table,
    )


def lasting(us):
    return pl.CostEstimate(flops=int(us * 1.1e9), bytes_accessed=int(us * 1e6), transcendentals=0)

f32=jnp.float32; bf=jnp.bfloat16

def mm(a,b): return jnp.dot(a,b,preferred_element_type=f32)
def mm_nt(a,b): return lax.dot_general(a,b,(((1,),(1,)),((),())),preferred_element_type=f32)

def gelu_both(v):
    c0 = 0.7978845608028654
    c1 = c0 * 0.044715
    sq = v * v
    half = 0.5 + 0.5 * jnp.tanh(v * (c0 + c1 * sq))
    act = v * half
    return act, half + act * (1.0 - half) * (2.0 * c0 + 6.0 * c1 * sq)


def local_kernel(g_ref, emb_ref, cot_ref, gao_ref, gax_ref, gains_ref, e_ref, et_ref,
                 pqo, pqx, woo, wox, wuo, wux,
                 normed_o, resid_o, mid_o, acto_o, actx_o, griso_o, grisx_o, glow_o, gpo_o, gpx_o, dx_o, gframe_o, gg_o,
                 q_s, k_s, v_s, p_s, gp_s, prod_s, wide_s, r_s, gm_s, gatt_s):
    F=g_ref.shape[0]; R=3*F; D=g_ref.shape[1]; H2=D//2
    step=pl.program_id(0)
    gain0=gains_ref[0:1,:]; gain1=gains_ref[1:2,:]
    g=g_ref[...].astype(f32)
    scr=(q_s,k_s,v_s)
    r0s=[]
    for c in range(3):
        x=g+emb_ref[c].astype(f32)
        r0=lax.rsqrt(jnp.mean(x*x,axis=-1,keepdims=True)+eps)
        r0s.append(r0)
        normed_o[c]=(x*r0*gain0).astype(bf)
    normed=normed_o[...].reshape(R,D)
    for j in range(3):
        scr[j][:,0:H2]=mm(normed,pqo[j]).astype(bf)
        scr[j][:,H2:D]=mm(normed,pqx[j]).astype(bf)
    pairs=[(c,c2) for c in range(3) for c2 in range(c+1)]
    rows=lambda ref,c: ref[c*F:(c+1)*F,:]
    for n,(c,c2) in enumerate(pairs):
        prod_s[n*F:(n+1)*F,:]=(rows(q_s,c).astype(f32)*rows(k_s,c2).astype(f32)).astype(bf)
    p_s[...]=mm(prod_s[...],e_ref[...])*0.125
    for c in range(3):
        own=[n for n,pr in enumerate(pairs) if pr[0]==c]
        ss=[rows(p_s,n) for n in own]
        top=functools.reduce(jnp.maximum,ss)
        ws=[jnp.exp(s-top) for s in ss]
        inv=1.0/functools.reduce(jnp.add,ws)
        for n,w in zip(own,ws): p_s[n*F:(n+1)*F,:]=w*inv
    wide_s[...]=mm(p_s[...].astype(bf),et_ref[...]).astype(bf)
    for c in range(3):
        acc=functools.reduce(jnp.add,[rows(wide_s,n).astype(f32)*rows(v_s,pr[1]).astype(f32) for n,pr in enumerate(pairs) if pr[0]==c])
        att=acc.astype(bf)
        gpo_o[0,c]=att[:,0:H2]; gpx_o[0,c]=att[:,H2:D]
    xs=(g_ref[...].astype(f32)[None]+emb_ref[...].astype(f32)).reshape(R,D)
    resid=xs+mm(gpo_o[0].reshape(R,H2),woo[...])+mm(gpx_o[0].reshape(R,H2),wox[...])
    r1=lax.rsqrt(jnp.mean(resid*resid,axis=-1,keepdims=True)+eps)
    resid_o[...]=resid.reshape(3,F,D)
    nm=(resid*r1*gain1).astype(bf)
    mid_o[...]=nm.reshape(3,F,D)
    ch=512
    gm=None
    for (wu,act_o,gris_o,ga_ref) in ((wuo,acto_o,griso_o,gao_ref),(wux,actx_o,grisx_o,gax_ref)):
        for j in range(wu.shape[1]//ch):
            sl=slice(j*ch,(j+1)*ch)
            w=wu[:,sl]
            act,gr=gelu_both(mm(nm,w))
            act_o[:,:,sl]=act.astype(bf).reshape(3,F,ch)
            gl=(ga_ref[:,:,sl].reshape(R,ch).astype(f32)*gr).astype(bf)
            gris_o[:,:,sl]=gl.reshape(3,F,ch)
            t=mm_nt(gl,w)
            if gm is None:
                gm_s[...]=t; gm=1
            else:
                gm_s[...]+=t
    gmid=gm_s[...]
    n1=resid_o[...].reshape(R,D)*r1
    u=gmid*gain1
    gres=cot_ref[...].reshape(R,D).astype(f32)+r1*(u-n1*jnp.mean(u*n1,axis=-1,keepdims=True))
    gsum1=jnp.sum(gmid*n1,axis=0,keepdims=True)
    r_s[...]=gres
    glow=gres.astype(bf)
    glow_o[...]=glow.reshape(3,F,D)
    gatt_s[:,0:H2]=mm_nt(glow,woo[...]).astype(bf)
    gatt_s[:,H2:D]=mm_nt(glow,wox[...]).astype(bf)
    def add(a,b): return b if a is None else a+b
    for n,(c,c2) in enumerate(pairs):
        prod_s[n*F:(n+1)*F,:]=(rows(gatt_s,c).astype(f32)*rows(v_s,c2).astype(f32)).astype(bf)
    gp_s[...]=mm(prod_s[...],e_ref[...])
    for c in range(3):
        own=[n for n,pr in enumerate(pairs) if pr[0]==c]
        ps=[rows(p_s,n) for n in own]
        gps=[rows(gp_s,n) for n in own]
        spread=functools.reduce(jnp.add,[p*gp for p,gp in zip(ps,gps)])
        for n,p,gp in zip(own,ps,gps): gp_s[n*F:(n+1)*F,:]=p*(gp-spread)*0.125
    prod_s[...]=mm(gp_s[...].astype(bf),et_ref[...]).astype(bf)
    for c in range(3):
        take=lambda which,left,right,at: functools.reduce(jnp.add,[rows(left,n).astype(f32)*rows(right,pr[1-which]).astype(f32) for n,pr in enumerate(pairs) if pr[which]==at]).astype(bf)
        for j,a in ((1,take(0,prod_s,k_s,c)),(2,take(1,prod_s,q_s,c)),(3,take(1,wide_s,gatt_s,c))):
            gpo_o[j,c]=a[:,0:H2]; gpx_o[j,c]=a[:,H2:D]
    gn=None
    for j in range(3):
        gn=add(gn,mm_nt(gpo_o[j+1].reshape(R,H2),pqo[j]))
        gn=gn+mm_nt(gpx_o[j+1].reshape(R,H2),pqx[j])
    gm_s[...]=gn
    tot=None; gsum0=None
    for c in range(3):
        gn=gm_s[c*F:(c+1)*F,:]
        n0=(g_ref[...].astype(f32)+emb_ref[c].astype(f32))*r0s[c]
        w=gn*gain0
        dx=r_s[c*F:(c+1)*F,:]+r0s[c]*(w-n0*jnp.mean(w*n0,axis=-1,keepdims=True))
        gsum0=add(gsum0,jnp.sum(gn*n0,axis=0,keepdims=True))
        dx_o[c]=dx.astype(bf)
        tot=add(tot,dx)
    gframe_o[...]=tot
    @pl.when(step==0)
    def _(): gg_o[...]=jnp.zeros_like(gg_o)
    gg_o[0:1,:]+=gsum0
    gg_o[1:2,:]+=gsum1

def local_call(g,emb,cot,gao,gax,gains,pqo,pqx,woo,wox,wuo,wux,tile=128):
    N,D=g.shape; H2=D//2; FH=wuo.shape[1]; F=tile
    E=(jnp.arange(D)[:,None]//HEAD==jnp.arange(128)[None,:]).astype(bf)
    ET=E.T
    c3=lambda w: pl.BlockSpec((3,F,w),lambda i:(0,i,0))
    whole=lambda shp: pl.BlockSpec(shp,lambda i:(0,)*len(shp),pipeline_mode=pl.Buffered(1))
    sd=jax.ShapeDtypeStruct
    out_shape=(sd((3,N,D),bf),sd((3,N,D),f32),sd((3,N,D),bf),
       sd((3,N,FH),bf),sd((3,N,FH),bf),sd((3,N,FH),bf),sd((3,N,FH),bf),sd((3,N,D),bf),
       sd((4,3,N,H2),bf),sd((4,3,N,H2),bf),sd((3,N,D),bf),sd((N,D),f32),sd((2,D),f32))
    gp=pl.BlockSpec((4,3,F,H2),lambda i:(0,0,i,0))
    return pl.pallas_call(local_kernel, grid=(N//F,),
      in_specs=[pl.BlockSpec((F,D),lambda i:(i,0)),c3(D),c3(D),c3(FH),c3(FH),whole((2,D)),whole(E.shape),whole(ET.shape),
        whole(pqo.shape),whole(pqx.shape),whole(woo.shape),whole(wox.shape),whole(wuo.shape),whole(wux.shape)],
      out_specs=(c3(D),c3(D),c3(D),c3(FH),c3(FH),c3(FH),c3(FH),c3(D),gp,gp,c3(D),pl.BlockSpec((F,D),lambda i:(i,0)),pl.BlockSpec((2,D),lambda i:(0,0))),
      out_shape=out_shape,
      scratch_shapes=[pltpu.VMEM((3*F,D),bf)]*3+[pltpu.VMEM((6*F,128),f32)]*2+[pltpu.VMEM((6*F,D),bf)]*2+[pltpu.VMEM((3*F,D),f32),pltpu.VMEM((3*F,D),f32),pltpu.VMEM((3*F,D),bf)],
      compiler_params=pltpu.CompilerParams(vmem_limit_bytes=65400 * 1024),
      cost_estimate=lasting(57),
      name="local_layer",
    )(g,emb,cot,gao,gax,gains,E,ET,pqo,pqx,woo,wox,wuo,wux)

def attend_kernel(at_ref, xo_ref, xs_ref, xc_ref, xb_ref, gain_ref, proj_ref, qid_ref, kid_ref,
                  normed_ref, q_ref, k_ref, v_ref, near_ref, off_ref):
    step = pl.program_id(0)
    rows = xo_ref.shape[0]

    @pl.when((at_ref[0] == 0) & (step == 0))
    def _():
        for j, x_ref in enumerate((xo_ref, xs_ref, xc_ref, xb_ref)):
            part = slice(j * rows, (j + 1) * rows)
            x = x_ref[...].astype(f32)
            scale = lax.rsqrt(jnp.mean(x * x, axis=-1, keepdims=True) + eps)
            normed_ref[part, :] = (x * scale * gain_ref[0:1, :]).astype(bf)
        for j, ref in enumerate((q_ref, k_ref, v_ref)):
            ref[...] = mm(normed_ref[...], proj_ref[j]).astype(bf)

    @pl.when(at_ref[0] == 0)
    def _():
        bias = jnp.where(
            ((qid_ref[:, 1:2] == kid_ref[1:2, :]) & (kid_ref[0:1, :] <= qid_ref[:, 0:1]))
            | (kid_ref[0:1, :] == qid_ref[:, 0:1]),
            0.0,
            far,
        )
        lane = lax.broadcasted_iota(jnp.int32, (1, 2 * HEAD), 1) // HEAD
        here_rows = pl.ds(pl.multiple_of(step * rows, rows), rows)
        for pair in range(q_ref.shape[1] // (2 * HEAD)):
            cols = slice(pair * 2 * HEAD, (pair + 1) * 2 * HEAD)
            q, k, v = q_ref[here_rows, cols], k_ref[:, cols], v_ref[:, cols]
            total = None
            for side in range(2):
                here = lane == side
                scores = mm_nt(jnp.where(here, q * HEAD ** (-0.5), jnp.zeros_like(q)), k) + bias
                top = jnp.max(scores, axis=-1, keepdims=True)
                weights = jnp.exp(scores - top)
                mass = jnp.sum(weights, axis=-1, keepdims=True)
                probs = (weights * (1.0 / mass)).astype(bf)
                term = mm(probs, jnp.where(here, v, jnp.zeros_like(v)))
                total = term if total is None else total + term
            for odd, ref in ((0, near_ref), (1, off_ref)):

                @pl.when(step % 2 == odd)
                def _():
                    ref[0, :, cols] = total.astype(bf)


def attend_call(at, blocks, gains, proj, qid, kid):
    rows, width = blocks[0].shape
    cols = proj.shape[2] // 2
    total = 4 * rows
    whole = lambda shape: pl.BlockSpec(shape, lambda i, s: (0,) * len(shape))
    sd = jax.ShapeDtypeStruct
    half = pl.BlockSpec((1, rows, cols), lambda i, s: (i // 2, 0, 0))
    return pl.pallas_call(
        attend_kernel,
        grid_spec=pltpu.PrefetchScalarGridSpec(
            num_scalar_prefetch=1,
            grid=(4,),
            in_specs=[whole((rows, width))] * 4
            + [
                whole(gains.shape),
                pl.BlockSpec((3, width, cols), lambda i, s: (0, 0, s[2])),
                pl.BlockSpec((rows, 2), lambda i, s: (i, 0)),
                whole(kid.shape),
            ],
            out_specs=(whole((total, width)), *[whole((total, cols))] * 3, half, half),
        ),
        out_shape=(sd((total, width), bf), *[sd((total, cols), bf)] * 3, *[sd((2, rows, cols), bf)] * 2),
        compiler_params=pltpu.CompilerParams(vmem_limit_bytes=60 * 1024 * 1024),
        cost_estimate=lasting(18),
        name="frame_attention",
    )(at, *blocks, gains, proj, qid, kid)


def attend_back_kernel(at_ref, q_ref, k_ref, v_ref, g_ref, qid_ref, kid_ref, gq_ref, gk_ref, gv_ref, ks_ref, vs_ref):
    @pl.when(at_ref[0] == 0)
    def _():
        step = pl.program_id(0)

        @pl.when(step == 0)
        def _():
            ks_ref[...] = jnp.zeros_like(ks_ref)
            vs_ref[...] = jnp.zeros_like(vs_ref)

        bias = jnp.where(
            ((qid_ref[:, 1:2] == kid_ref[1:2, :]) & (kid_ref[0:1, :] <= qid_ref[:, 0:1]))
            | (kid_ref[0:1, :] == qid_ref[:, 0:1]),
            0.0,
            far,
        )
        lane = lax.broadcasted_iota(jnp.int32, (1, 2 * HEAD), 1) // HEAD
        for pair in range(q_ref.shape[1] // (2 * HEAD)):
            cols = slice(pair * 2 * HEAD, (pair + 1) * 2 * HEAD)
            q, k, v, g = q_ref[:, cols], k_ref[:, cols], v_ref[:, cols], g_ref[:, cols]
            gq = None
            for side in range(2):
                here = lane == side
                qh = jnp.where(here, q, jnp.zeros_like(q))
                gh = jnp.where(here, g, jnp.zeros_like(g))
                kh = jnp.where(here, k, jnp.zeros_like(k))
                scores = mm_nt(qh * HEAD ** (-0.5), k) + bias
                top = jnp.max(scores, axis=-1, keepdims=True)
                weights = jnp.exp(scores - top)
                mass = jnp.sum(weights, axis=-1, keepdims=True)
                probs = weights * (1.0 / mass)
                grad_probs = mm_nt(gh, v)
                spread = jnp.sum(probs * grad_probs, axis=-1, keepdims=True)
                gs = (probs * (grad_probs - spread) * HEAD ** (-0.5)).astype(bf)
                term = mm(gs, kh)
                gq = term if gq is None else gq + term
                ks_ref[:, cols] += across_rows(gs, qh)
                vs_ref[:, cols] += across_rows(probs.astype(bf), gh)
            gq_ref[:, cols] = gq.astype(bf)

        @pl.when(step == pl.num_programs(0) - 1)
        def _():
            gk_ref[...] = ks_ref[...].astype(bf)
            gv_ref[...] = vs_ref[...].astype(bf)


def attend_back_call(at, q, k, v, g, qid, kid, rows):
    total, width = q.shape
    part = pl.BlockSpec((rows, width), lambda i, s: (i, 0))
    whole = pl.BlockSpec((total, width), lambda i, s: (0, 0))
    shape = jax.ShapeDtypeStruct((total, width), bf)
    return pl.pallas_call(
        attend_back_kernel,
        grid_spec=pltpu.PrefetchScalarGridSpec(
            num_scalar_prefetch=1,
            grid=(total // rows,),
            in_specs=[part, whole, whole, part, pl.BlockSpec((rows, 2), lambda i, s: (i, 0)), pl.BlockSpec(kid.shape, lambda i, s: (0, 0))],
            out_specs=(part, whole, whole),
            scratch_shapes=[pltpu.VMEM((total, width), f32)] * 2,
        ),
        out_shape=(shape, shape, shape),
        compiler_params=pltpu.CompilerParams(vmem_limit_bytes=60 * 1024 * 1024),
        cost_estimate=lasting(0.01),
        name="frame_attention_back",
    )(at, q, k, v, g, qid, kid)


def front_kernel(at_ref, x_ref, near_ref, off_ref, core_ref, gain_ref, oo_ref, ox_ref, uo_ref, ux_ref, do_ref, dx_ref,
                 resid_ref, mid_ref, act_o, act_x, slope_o, slope_x, out_ref, total_ref):
    @pl.when(at_ref[0] == 0)
    def _():
        step = pl.program_id(0)
        turn = pl.num_programs(0) // 2

        @pl.when(step == 0)
        def _():
            cols = near_ref.shape[2]
            resid = x_ref[...].astype(f32)
            for flip, part, out in ((0, near_ref, oo_ref), (1, off_ref, oo_ref), (0, core_ref, ox_ref), (1, core_ref, ox_ref)):
                spot = pl.ds(pl.multiple_of((at_ref[2] ^ flip) * cols, cols), cols)
                resid = resid + mm(part[flip if part is core_ref else 0], out[spot, :])
            resid_ref[...] = resid
            scale = lax.rsqrt(jnp.mean(resid * resid, axis=-1, keepdims=True) + eps)
            mid_ref[...] = (resid * scale * gain_ref[1:2, :]).astype(bf)
            total_ref[...] = resid

        def part(up, down, act_ref, slope_ref):
            act, slope = gelu_both(mm(mid_ref[...], up[...]))
            act = act.astype(bf)
            act_ref[...] = act
            slope_ref[...] = slope.astype(bf)
            total_ref[...] += mm(act, down[...])

        @pl.when(step < turn)
        def _():
            part(uo_ref, do_ref, act_o, slope_o)

        @pl.when(step >= turn)
        def _():
            part(ux_ref, dx_ref, act_x, slope_x)

        @pl.when(step == pl.num_programs(0) - 1)
        def _():
            out_ref[...] = total_ref[...].astype(bf)


def halves_specs(turn, chunk, width, rows):
    first = lambda i, s: jnp.minimum(i, turn - 1) * (1 - s[0])
    later = lambda i, s: jnp.maximum(i - turn, 0) * (1 - s[0])
    ups = [pl.BlockSpec((width, chunk), lambda i, s, f=f: (0, f(i, s))) for f in (first, later)]
    downs = [pl.BlockSpec((chunk, width), lambda i, s, f=f: (f(i, s), 0)) for f in (first, later)]
    cols = [pl.BlockSpec((rows, chunk), lambda i, s, f=f: (0, f(i, s))) for f in (first, later)]
    return ups, downs, cols


def front_call(at, x, near, off, from_core, gains, out_own, out_oth, up_own, up_oth, down_own, down_oth, chunk=1024):
    rows, width = x.shape
    hidden = up_own.shape[1]
    turn = hidden // chunk
    ups, downs, cols = halves_specs(turn, chunk, width, rows)
    whole = lambda a: pl.BlockSpec(a.shape, lambda i, s: (0,) * a.ndim)
    sd = jax.ShapeDtypeStruct
    full = pl.BlockSpec((rows, width), lambda i, s: (0, 0))
    hid = sd((rows, hidden), bf)
    return pl.pallas_call(
        front_kernel,
        grid_spec=pltpu.PrefetchScalarGridSpec(
            num_scalar_prefetch=1,
            grid=(2 * turn,),
            in_specs=[full, whole(near), whole(off), whole(from_core), whole(gains), whole(out_own), whole(out_oth), *ups, *downs],
            out_specs=(full, full, cols[0], cols[1], cols[0], cols[1], full),
            scratch_shapes=[pltpu.VMEM((rows, width), f32)],
        ),
        out_shape=(sd((rows, width), f32), sd((rows, width), bf), hid, hid, hid, hid, sd((rows, width), bf)),
        compiler_params=pltpu.CompilerParams(vmem_limit_bytes=60 * 1024 * 1024),
        cost_estimate=lasting(15),
        name="global_forward",
    )(at, x, near, off, from_core, gains, out_own, out_oth, up_own, up_oth, down_own, down_oth)


def back_kernel(at_ref, g_ref, resid_ref, gain_ref, so_ref, sx_ref, uo_ref, ux_ref, do_ref, dx_ref,
                rise_o, rise_x, grad_ref, low_ref, gsum_ref, total_ref):
    @pl.when(at_ref[0] == 0)
    def _():
        step = pl.program_id(0)
        turn = pl.num_programs(0) // 2

        def part(up, down, slope_ref, rise_ref):
            rise = (mm_nt(g_ref[...], down[...]) * slope_ref[...].astype(f32)).astype(bf)
            rise_ref[...] = rise
            return mm_nt(rise, up[...])

        @pl.when(step == 0)
        def _():
            total_ref[...] = part(uo_ref, do_ref, so_ref, rise_o)

        @pl.when((step > 0) & (step < turn))
        def _():
            total_ref[...] += part(uo_ref, do_ref, so_ref, rise_o)

        @pl.when(step >= turn)
        def _():
            total_ref[...] += part(ux_ref, dx_ref, sx_ref, rise_x)

        @pl.when(step == pl.num_programs(0) - 1)
        def _():
            resid = resid_ref[...]
            scale = lax.rsqrt(jnp.mean(resid * resid, axis=-1, keepdims=True) + eps)
            normal = resid * scale
            total = total_ref[...]
            unit = total * gain_ref[1:2, :]
            grad = g_ref[...].astype(f32) + scale * (unit - normal * jnp.mean(unit * normal, axis=-1, keepdims=True))
            grad_ref[...] = grad
            low_ref[...] = grad.astype(bf)
            gsum_ref[...] = jnp.sum(total * normal, axis=0, keepdims=True)


def back_call(at, g, resid, gains, slope_own, slope_oth, up_own, up_oth, down_own, down_oth, chunk=1024):
    rows, width = g.shape
    hidden = up_own.shape[1]
    turn = hidden // chunk
    ups, downs, cols = halves_specs(turn, chunk, width, rows)
    sd = jax.ShapeDtypeStruct
    full = pl.BlockSpec((rows, width), lambda i, s: (0, 0))
    hid = sd((rows, hidden), bf)
    line = pl.BlockSpec((1, width), lambda i, s: (0, 0))
    return pl.pallas_call(
        back_kernel,
        grid_spec=pltpu.PrefetchScalarGridSpec(
            num_scalar_prefetch=1,
            grid=(2 * turn,),
            in_specs=[full, full, pl.BlockSpec(gains.shape, lambda i, s: (0, 0)), *cols, *ups, *downs],
            out_specs=(*cols, full, full, line),
            scratch_shapes=[pltpu.VMEM((rows, width), f32)],
        ),
        out_shape=(hid, hid, sd((rows, width), f32), sd((rows, width), bf), sd((1, width), f32)),
        compiler_params=pltpu.CompilerParams(vmem_limit_bytes=60 * 1024 * 1024),
        cost_estimate=lasting(13),
        name="global_backward",
    )(at, g, resid, gains, slope_own, slope_oth, up_own, up_oth, down_own, down_oth)


def split_sides(total, side, mine_ref, theirs_ref, at):
    half = total.shape[0] // 2
    top, bottom = total[:half].astype(bf), total[half:].astype(bf)
    mine_ref[at] = jnp.where(side == 0, top, bottom)
    theirs_ref[at] = jnp.where(side == 0, bottom, top)


def deal(total_ref, at_ref, mine_ref, theirs_ref, plane_first):
    piece = total_ref.shape[0] // 8
    for jz in range(4):
        for jy in range(2):
            place = (at_ref[1] ^ jz) * 2 + (at_ref[2] ^ jy)
            rows = pl.ds(pl.multiple_of(place * piece, piece), piece)
            low, high = jz % 2, jz // 2
            part = total_ref[rows, :].astype(bf)
            if plane_first:
                (theirs_ref if low else mine_ref)[high, jy] = part
            else:
                (theirs_ref if jy else mine_ref)[low * 2 + high] = part


def weight_kernel(at_ref, gl, gli, gr, gri, ll, lli, lr, lri, mine_ref, theirs_ref, total_ref, gt, gti, lt, lti, *, plane_first):
    step = pl.program_id(0)
    for here, lefts, turned, rights in ((0, (gl, gli), (gt, gti), (gr, gri)), (1, (ll, lli), (lt, lti), (lr, lri))):

        @pl.when(at_ref[0] == here)
        def _():
            @pl.when(step == 0)
            def _():
                for left, turn in zip(lefts, turned):
                    turn[...] = left[...].T

            total_ref[...] = mm(turned[0][...], rights[0][...]) + mm(turned[1][...], rights[1][...])

    deal(total_ref, at_ref, mine_ref, theirs_ref, plane_first)


def weight_call(at, four_global, four_local, plane_first, name, chunk=512):
    width = four_global[0].shape[1]
    cols = four_global[2].shape[1]
    piece = width // 8

    def specs(four, here):
        whole = [pl.BlockSpec(a.shape, lambda i, s: (0, 0), pipeline_mode=pl.Buffered(1)) for a in four[:2]]
        part = [pl.BlockSpec((a.shape[0], chunk), lambda i, s: (0, jnp.where(s[0] == here, i, 0))) for a in four[2:]]
        return whole + part

    if plane_first:
        shape = jax.ShapeDtypeStruct((2, 2, piece, cols), bf)
        out = pl.BlockSpec((2, 2, piece, chunk), lambda i, s: (0, 0, 0, i))
    else:
        shape = jax.ShapeDtypeStruct((4, piece, cols), bf)
        out = pl.BlockSpec((4, piece, chunk), lambda i, s: (0, 0, i))
    return pl.pallas_call(
        functools.partial(weight_kernel, plane_first=plane_first),
        grid_spec=pltpu.PrefetchScalarGridSpec(
            num_scalar_prefetch=1,
            grid=(cols // chunk,),
            in_specs=specs(four_global, 0) + specs(four_local, 1),
            out_specs=(out, out),
            scratch_shapes=[pltpu.VMEM((width, chunk), f32)]
            + [pltpu.VMEM((width, a.shape[0]), bf) for a in (*four_global[:2], *four_local[:2])],
        ),
        out_shape=(shape, shape),
        compiler_params=pltpu.CompilerParams(vmem_limit_bytes=60 * 1024 * 1024),
        cost_estimate=lasting(8),
        name=name,
    )(at, *four_global, *four_local)


def rest_kernel(at_ref, gl, gn, gr, ll, lli, ln, lni, lr, lri, mine_ref, theirs_ref, total_ref, gt, lt, lti):
    step = pl.program_id(0)
    size = total_ref.shape[1] // 2

    @pl.when(at_ref[0] == 0)
    def _():
        for when, left in ((0, gl), (1, gn)):

            @pl.when(step == when)
            def _():
                gt[...] = left[...].T

        for which in range(2):

            @pl.when(at_ref[2] == which)
            def _():
                total_ref[:, which * size : (which + 1) * size] = mm(gt[...], gr[0])
                total_ref[:, (1 - which) * size : (2 - which) * size] = jnp.zeros((total_ref.shape[0], size), f32)

    @pl.when(at_ref[0] == 1)
    def _():
        for when, left, left_in in ((0, ll, lli), (1, ln, lni)):

            @pl.when(step == when)
            def _():
                lt[...] = left[...].T
                lti[...] = left_in[...].T

        total_ref[...] = mm(lt[...], lr[0]) + mm(lti[...], lri[0])

    deal(total_ref, at_ref, mine_ref, theirs_ref, False)


def rest_call(at, g_low, g_normed, g_rights, l_low, l_low_in, l_normed, l_normed_in, l_rights, l_rights_in):
    width = g_low.shape[1]
    piece = width // 8
    count, rows, size = l_rights.shape
    whole = lambda a: pl.BlockSpec(a.shape, lambda i, s: (0, 0), pipeline_mode=pl.Buffered(1))
    part = lambda a, here: pl.BlockSpec((1,) + a.shape[1:], lambda i, s: (jnp.where(s[0] == here, i, 0), 0, 0))
    shape = jax.ShapeDtypeStruct((4, piece, count * size), bf)
    out = pl.BlockSpec((4, piece, size), lambda i, s: (0, 0, i))
    lefts = (l_low, l_low_in, l_normed, l_normed_in)
    return pl.pallas_call(
        rest_kernel,
        grid_spec=pltpu.PrefetchScalarGridSpec(
            num_scalar_prefetch=1,
            grid=(count,),
            in_specs=[whole(g_low), whole(g_normed), part(g_rights, 0), *map(whole, lefts), part(l_rights, 1), part(l_rights_in, 1)],
            out_specs=(out, out),
            scratch_shapes=[pltpu.VMEM((width, size), f32), pltpu.VMEM(g_low.shape[::-1], bf)]
            + [pltpu.VMEM((width, rows), bf)] * 2,
        ),
        out_shape=(shape, shape),
        compiler_params=pltpu.CompilerParams(vmem_limit_bytes=60 * 1024 * 1024),
        cost_estimate=lasting(0.01),
        name="rest_gradient",
    )(at, g_low, g_normed, g_rights, *lefts, l_rights, l_rights_in)


def fall_kernel(at_ref, resid_ref, ao_ref, ax_ref, do_ref, dx_ref, out_ref, total_ref):
    step = pl.program_id(0)
    turn = pl.num_programs(0) // 2
    books, planes, half = out_ref.shape[1], out_ref.shape[0], out_ref.shape[2]

    @pl.when(at_ref[0] == 1)
    def _():
        @pl.when(step == 0)
        def _():
            total_ref[...] = resid_ref[...]

        @pl.when(step < turn)
        def _():
            total_ref[...] += mm(ao_ref[...], do_ref[...])

        @pl.when(step >= turn)
        def _():
            total_ref[...] += mm(ax_ref[...], dx_ref[...])

        @pl.when(step == pl.num_programs(0) - 1)
        def _():
            for c in range(books):
                for z in range(planes):
                    first = (c * planes + z) * half
                    out_ref[z, c] = total_ref[first : first + half, :].astype(bf)


def fall_call(at, resid, act_own, act_oth, down_own, down_oth, planes, books, chunk=1024):
    rows, width = resid.shape
    turn = down_own.shape[0] // chunk
    first = lambda i, s: jnp.minimum(i, turn - 1) * s[0]
    later = lambda i, s: jnp.maximum(i - turn, 0) * s[0]
    col = lambda f: pl.BlockSpec((rows, chunk), lambda i, s: (0, f(i, s)))
    row = lambda f: pl.BlockSpec((chunk, width), lambda i, s: (f(i, s), 0))
    shape = (planes, books, rows // planes // books, width)
    return pl.pallas_call(
        fall_kernel,
        grid_spec=pltpu.PrefetchScalarGridSpec(
            num_scalar_prefetch=1,
            grid=(2 * turn,),
            in_specs=[pl.BlockSpec((rows, width), lambda i, s: (0, 0), pipeline_mode=pl.Buffered(1)), col(first), col(later), row(first), row(later)],
            out_specs=pl.BlockSpec(shape, lambda i, s: (0, 0, 0, 0)),
            scratch_shapes=[pltpu.VMEM((rows, width), f32)],
        ),
        out_shape=jax.ShapeDtypeStruct(shape, bf),
        compiler_params=pltpu.CompilerParams(vmem_limit_bytes=60 * 1024 * 1024),
        cost_estimate=lasting(7),
        name="local_output",
    )(at, resid, act_own, act_oth, down_own, down_oth)


def table_kernel(at_ref, code_ref, code_in_ref, own_ref, got_ref, low_ref, high_ref, total_ref):
    entries = total_ref.shape[0]
    slots = lax.broadcasted_iota(jnp.int32, (entries, code_ref.shape[2]), 0)
    piece = low_ref.shape[3]

    @pl.when(at_ref[0] == 1)
    def _():
        hot = (slots == code_ref[0]).astype(f32).astype(bf)
        hot_in = (slots == code_in_ref[0]).astype(f32).astype(bf)
        total_ref[...] = mm(hot, own_ref[0]) + mm(hot_in, got_ref[0])
        for jz in range(4):
            for jy in range(2):
                place = (at_ref[1] ^ jz) * 2 + (at_ref[2] ^ jy)
                spot = (jz % 2) * 2 + jz // 2
                for ref, base in ((low_ref, 0), (high_ref, entries // 2)):
                    rows = pl.ds(pl.multiple_of(base + place * piece, piece), piece)
                    ref[jy, spot, 0] = total_ref[rows, :].astype(bf)


def table_call(at, codes, codes_in, own, got, entries):
    books, rows = codes.shape
    width = own.shape[2]
    line = pl.BlockSpec((1, 1, rows), lambda c, s: (c, 0, 0))
    block = pl.BlockSpec((1, rows, width), lambda c, s: (c, 0, 0))
    shape = (2, 4, books, entries // 16, width)
    out = pl.BlockSpec((2, 4, 1, entries // 16, width), lambda c, s: (0, 0, c, 0, 0))
    return pl.pallas_call(
        table_kernel,
        grid_spec=pltpu.PrefetchScalarGridSpec(
            num_scalar_prefetch=1,
            grid=(books,),
            in_specs=[line, line, block, block],
            out_specs=(out, out),
            scratch_shapes=[pltpu.VMEM((entries, width), f32)],
        ),
        out_shape=(jax.ShapeDtypeStruct(shape, bf),) * 2,
        compiler_params=pltpu.CompilerParams(vmem_limit_bytes=60 * 1024 * 1024),
        cost_estimate=lasting(4),
        name="table_gradient",
    )(at, codes[:, None, :], codes_in[:, None, :], own, got)


def prepare_kernel(at_ref, code_ref, cot_ref, do_ref, dx_ref, table_ref, look_ref, po_ref, px_ref):
    step = pl.program_id(0)
    turn = pl.num_programs(0) // 2
    books, rows, chunk = po_ref.shape

    @pl.when(at_ref[0] == 1)
    def _():
        @pl.when(step < look_ref.shape[0])
        def _():
            slots = lax.broadcasted_iota(jnp.int32, (rows, table_ref.shape[1]), 1)
            hot = (slots == code_ref[jnp.minimum(step, look_ref.shape[0] - 1)]).astype(f32).astype(bf)
            look_ref[jnp.minimum(step, look_ref.shape[0] - 1)] = mm(hot, table_ref[0]).astype(bf)

        @pl.when(step < turn)
        def _():
            po_ref[...] = mm_nt(cot_ref[...], do_ref[...]).astype(bf).reshape(books, rows, chunk)

        @pl.when(step >= turn)
        def _():
            px_ref[...] = mm_nt(cot_ref[...], dx_ref[...]).astype(bf).reshape(books, rows, chunk)


def prepare_call(at, codes, cot, down_own, down_oth, table, chunk=512):
    books, rows = codes.shape
    width = cot.shape[1]
    hidden = down_own.shape[0]
    turn = hidden // chunk
    first = lambda i, s: jnp.minimum(i, turn - 1) * s[0]
    later = lambda i, s: jnp.maximum(i - turn, 0) * s[0]
    down = lambda f: pl.BlockSpec((chunk, width), lambda i, s: (f(i, s), 0))
    out = lambda f: pl.BlockSpec((books, rows, chunk), lambda i, s: (0, 0, f(i, s)))
    sd = jax.ShapeDtypeStruct
    return pl.pallas_call(
        prepare_kernel,
        grid_spec=pltpu.PrefetchScalarGridSpec(
            num_scalar_prefetch=1,
            grid=(2 * turn,),
            in_specs=[
                pl.BlockSpec((books, rows, 1), lambda i, s: (0, 0, 0)),
                pl.BlockSpec(cot.shape, lambda i, s: (0, 0)),
                down(first),
                down(later),
                pl.BlockSpec((1,) + table.shape[1:], lambda i, s: (jnp.minimum(i, books - 1) * s[0], 0, 0)),
            ],
            out_specs=(pl.BlockSpec((books, rows, width), lambda i, s: (0, 0, 0)), out(first), out(later)),
        ),
        out_shape=(sd((books, rows, width), bf), sd((books, rows, hidden), bf), sd((books, rows, hidden), bf)),
        compiler_params=pltpu.CompilerParams(vmem_limit_bytes=60 * 1024 * 1024),
        cost_estimate=lasting(5),
        name="local_prepare",
    )(at, codes[:, :, None], cot, down_own, down_oth, table)


def fence(*groups):
    return lax.optimization_barrier(groups)


def body(frames, codes, lengths, gains, w_qkv, w_out, w_up, w_down, table, cotangent):
    batches, share, width = frames.shape
    members = lax.axis_size("dp") // batches
    if (
        lax.axis_size("section") != 2
        or lax.axis_size("tensor") != 2
        or members != 2
        or lax.axis_size("dp") != 2 * batches
        or batches & (batches - 1)
        or share % 32
        or table.shape[1] != width
    ):
        return plain_body(frames, codes, lengths, gains, w_qkv, w_out, w_up, w_down, table, cotangent)
    place, core = lax.axis_index("dp"), lax.axis_index("tensor")
    plane, side = place // members, place % members
    on_first = lax.axis_index("section") == 0
    half = share // 2
    rows = batches * half
    count = 2 * batches
    at = jnp.stack([lax.axis_index("section"), plane, side]).astype(jnp.int32)

    everywhere, first, second = (0, 1), (0,), (1,)

    def linked(a, flip_place, flip_core, sections=everywhere):
        pairs = [
            ((z * count + i) * 2 + j, (z * count + (i ^ flip_place)) * 2 + (j ^ flip_core))
            for z in sections
            for i in range(count)
            for j in range(2)
        ]
        return lax.ppermute(a, ("section", "dp", "tensor"), pairs)

    def core_swap(a, sections=everywhere):
        return linked(a, 0, 1, sections)

    def side_swap(a, sections=everywhere):
        return linked(a, 1, 0, sections)

    def both_swap(a, sections=everywhere):
        return linked(a, 1, 1, sections)

    def to_local(a):
        return lax.ppermute(a, "section", [(0, 1)])

    def to_global(a):
        return lax.ppermute(a, "section", [(1, 0)])

    def planes_in(a, sections=everywhere):
        pieces = [lax.dynamic_slice_in_dim(a, plane ^ k, 1, 0) for k in range(batches)]
        return jnp.concatenate([pieces[0], *(linked(pieces[k], 2 * k, 0, sections) for k in range(1, batches))], 0)

    def planes_out(a, sections=everywhere):
        got = [a[:1], *(linked(a[k : k + 1], 2 * k, 0, sections) for k in range(1, batches))]
        out = jnp.zeros_like(a)
        for k in range(batches):
            out = lax.dynamic_update_slice_in_dim(out, got[k], plane ^ k, 0)
        return out

    def core_half(a, axis):
        return lax.dynamic_slice_in_dim(a, core * half, half, axis)

    def join_cores(a, axis):
        other = core_swap(a)
        return jnp.where(core == 0, jnp.concatenate([a, other], axis), jnp.concatenate([other, a], axis))

    def quarter(a, axis):
        size = a.shape[axis] // 2
        return lax.dynamic_slice_in_dim(a, side * size, size, axis)

    def by_side(mine, theirs, axis):
        return jnp.where(side == 0, jnp.concatenate([mine, theirs], axis), jnp.concatenate([theirs, mine], axis))

    x_own = planes_in(core_half(frames, 1), first).reshape(rows, width)
    x_side = side_swap(x_own, first)
    x_core, x_both = core_swap(x_own), core_swap(x_side)
    (x_core, x_both), (w_qkv, w_out, w_up, w_down, cotangent, codes) = fence(
        (x_core, x_both), (w_qkv, w_out, w_up, w_down, cotangent, codes)
    )

    gains_here = gains[0]
    proj_own = w_qkv[0].transpose(1, 0, 2)
    out_own, up_own, down_own = w_out[0], w_up[0], w_down[0]
    out_oth, up_oth, down_oth = (core_swap(w) for w in (out_own, up_own, down_own))
    proj_oth = core_swap(proj_own)

    def positions(jt, js):
        base = ((jnp.arange(batches)[:, None] ^ plane) * 2 + (side ^ js)) * share + (core ^ jt) * half
        return (base + jnp.arange(half)[None, :]).reshape(-1)

    pos = jnp.concatenate([positions(0, 0), positions(0, 1), positions(1, 0), positions(1, 1)]).astype(jnp.int32)
    doc_ends = jnp.cumsum(lax.dynamic_index_in_dim(lengths, plane, 0, keepdims=False))
    doc = doc_index(pos, doc_ends)
    qid = jnp.stack([pos, doc], 1)
    kid = jnp.stack([pos, jnp.where(pos < doc_ends[-1], doc, -1)], 0)

    normed_all, q, k, v, near, off = attend_call(at, (x_own, x_side, x_core, x_both), gains_here, proj_own, qid, kid)
    proj_mine = quarter(proj_own, 2)
    off_got = side_swap(off, first)
    from_core = core_swap(jnp.concatenate([near[1:], off_got[1:]], 0))
    attended = jnp.stack([near[0], off[0], near[1], off[1]]).reshape(4 * rows, -1)
    x32 = x_own.astype(f32)
    resid, mid, act_own, act_oth, slope_own, slope_oth, global_low = front_call(
        at, x_own, near, off_got, from_core, gains_here, out_own, out_oth, up_own, up_oth, down_own, down_oth
    )
    mid_in, act_in = core_swap(mid), core_swap(act_oth)

    arrived = to_local(global_low)
    cot = planes_in(core_half(cotangent.transpose(0, 2, 1, 3), 2), second).transpose(1, 0, 2, 3).reshape(CODEBOOKS, rows, width)
    codes_own = planes_in(core_half(codes.transpose(0, 2, 1), 2), second).transpose(1, 0, 2).reshape(CODEBOOKS, rows)
    slots = jnp.arange(table.shape[1], dtype=jnp.int32)
    cot_rows = cot.reshape(-1, width)
    cot_in = core_swap(cot_rows)

    looked_up, pull_own, pull_oth = prepare_call(at, codes_own, cot_rows, down_own, down_oth, table)
    (
        l_normed, l_resid, l_mid, l_act_own, l_act_oth, l_rise_own, l_rise_oth,
        l_low, l_pack_own, l_pack_oth, l_grad, l_frame, l_gains,
    ) = local_call(
        arrived, looked_up, cot, pull_own, pull_oth, gains_here, proj_own, proj_oth, out_own, out_oth, up_own, up_oth
    )
    global_here = jnp.where(on_first, global_low, arrived).reshape(batches, half, width)
    grad_low = to_global(l_frame.astype(bf))

    flat = lambda a: a.reshape(-1, a.shape[-1])

    def swap(a, bit):
        return lax.ppermute(a, "dp", [(i, i ^ (1 << bit)) for i in range(count)])

    def meet(mine, got):
        return (mine.astype(f32) + got.astype(f32)).astype(bf)

    def cols_of(a, which):
        return lax.dynamic_slice_in_dim(a, which * (width // 2), width // 2, 2)

    l_act_in = core_swap(flat(l_act_oth))
    l_got, codes_oth = core_swap(cols_of(l_grad, 1 - core)), core_swap(codes_own)
    l_rise_in, l_mid_in = core_swap(flat(l_rise_oth)), core_swap(flat(l_mid))
    l_low_in = core_swap(flat(l_low))
    l_normed_in, l_pack_in = core_swap(flat(l_normed)), core_swap(l_pack_oth)
    local_low = fall_call(at, flat(l_resid), flat(l_act_own), flat(l_act_oth), down_own, down_oth, batches, CODEBOOKS)
    table_low, table_high = table_call(at, codes_own, codes_oth, cols_of(l_grad, core), l_got, table.shape[1])
    (local_low, table_low, table_high), (grad_low,) = fence((local_low, table_low, table_high), (grad_low,))

    grad_in_low = core_swap(grad_low)
    rise_own, rise_oth, grad_resid, low_own, gain_mid = back_call(
        at, grad_low, resid, gains_here, slope_own, slope_oth, up_own, up_oth, down_own, down_oth
    )
    rise_in = core_swap(rise_oth)
    (low_own, grad_in_low, table_low), (local_low, global_here) = fence(
        (low_own, grad_in_low, table_low), (local_low, global_here)
    )
    local_moved = planes_out(local_low, second)
    global_moved = planes_out(global_here)
    low_side = side_swap(low_own, first)
    down_mine, down_theirs = weight_call(
        at, (grad_low, grad_in_low, act_own, act_in), (cot_rows, cot_in, flat(l_act_own), l_act_in), True, "down_gradient"
    )
    (down_theirs,), (rise_in,) = fence((down_theirs,), (rise_in,))
    down_got = swap(down_theirs, 1)
    up_mine, up_theirs = weight_call(
        at, (mid, mid_in, rise_own, rise_in), (flat(l_mid), l_mid_in, flat(l_rise_own), l_rise_in), False, "up_gradient"
    )
    (up_theirs, low_side, table_low, local_moved, global_moved), = fence(
        (up_theirs, low_side, table_low, local_moved, global_moved)
    )
    up_got = swap(up_theirs, 0)
    table_moved = to_global(table_low)
    low_all = jnp.concatenate([low_own, low_side, core_swap(low_own), core_swap(low_side)], 0)
    grad_att = against_rows(low_all, quarter(out_own, 0)).astype(bf)
    grad_packs = attend_back_call(at, q, k, v, grad_att, qid, kid, rows)
    rest_mine, rest_theirs = rest_call(
        at, low_all, normed_all, jnp.stack([attended, *grad_packs]), flat(l_low), l_low_in, flat(l_normed), l_normed_in,
        l_pack_own.reshape(4, CODEBOOKS * rows, -1), l_pack_in.reshape(4, CODEBOOKS * rows, -1),
    )
    (rest_theirs, down_got, up_got), (grad_packs,) = fence((rest_theirs, down_got, up_got), (grad_packs,))
    rest_got = swap(rest_theirs, 0)
    up_now = meet(up_mine, up_got)
    up_got = swap(up_now[2:], 1)
    down_now = meet(down_mine, down_got)
    down_got = swap(down_now[1], 2)
    local_sent = to_global(local_moved)
    part_normed = sum(against_rows(g, proj_mine[j]) for j, g in enumerate(grad_packs))
    pair = part_normed[: 2 * rows] + core_swap(part_normed[2 * rows :].astype(bf)).astype(f32)
    pair_side = side_swap(pair[rows:].astype(bf), first)
    (rest_got, up_got, down_got, table_moved, pair_side), = fence((rest_got, up_got, down_got, table_moved, pair_side))
    rest_now = meet(rest_mine, rest_got)
    rest_got = swap(rest_now[2:], 1)
    down_now = meet(down_now[0], down_got)
    down_got = swap(down_now[1], 0)
    up_now = meet(up_now[:2], up_got)
    up_got = swap(up_now[1], 2)
    table_now = jnp.where(on_first, table_moved, table_high).reshape(2, batches, -1, width // 2)
    table_got = swap(table_now[1], 0)
    grad_normed = pair[:rows] + pair_side.astype(f32)
    back_in, gain_in = rms_back(x32, gains_here[0], grad_normed)
    grad_frames = grad_resid + back_in
    gain_sum = jnp.where(on_first, jnp.concatenate([gain_in[None], gain_mid]), l_gains)
    gain_sum = (gain_sum + core_swap(gain_sum)).reshape(2, batches, 2, -1)
    piece = width // count
    gain_rows = jnp.concatenate(
        [
            lax.dynamic_slice(gain_sum, (0, plane ^ (2 * j + i), side ^ y, 0), (2, 1, 1, piece)).reshape(1, -1)
            for y in range(2)
            for i in range(2)
            for j in range(2)
        ]
    ).reshape(2, batches, 2 * piece)
    gain_got = swap(gain_rows[1], 0)
    inner = planes_out(jnp.where(on_first, grad_frames, l_frame).astype(bf).reshape(batches, half, width))
    (rest_got, up_got, down_got, table_got, local_sent, gain_got, inner), = fence(
        (rest_got, up_got, down_got, table_got, local_sent, gain_got, inner)
    )
    rest_now = meet(rest_now[:2], rest_got)
    rest_got = swap(rest_now[1], 2)
    table_now = meet(table_now[0], table_got)
    gain_rows = jnp.pad((gain_rows[0] + gain_got).astype(bf)[:, None, :], ((0, 0), (0, 15), (0, width // 2 - 2 * piece)))
    table_now = jnp.concatenate([table_now, gain_rows], 1)
    table_got = swap(table_now[2:], 1)
    local_out = join_cores(jnp.where(on_first, local_sent, local_moved), 2).transpose(0, 2, 1, 3)
    global_out = join_cores(global_moved, 1)
    down_share = down_now[0].astype(f32) + down_got.astype(f32)
    up_share = up_now[0].astype(f32) + up_got.astype(f32)
    table_now = meet(table_now[:2], table_got)
    table_got = swap(table_now[1], 2)
    input_grads = join_cores(inner, 1).astype(f32)[None]
    hidden = out_own.shape[0]
    (local_out, global_out, input_grads, up_share, down_share), (rest_got, table_got) = fence(
        (local_out, global_out, input_grads, up_share, down_share.T), (rest_got, table_got)
    )
    rest_share = rest_now[0].astype(f32) + rest_got.astype(f32)
    table_now = table_now[0].astype(f32) + table_got.astype(f32)
    gain_share = table_now[-16, : 2 * piece].reshape(2, piece)
    grad_table = join_cores(table_now[:-16].reshape(CODEBOOKS, -1, width // 2).astype(bf), 2).astype(f32)

    hidden = out_own.shape[0]
    proj_share = rest_share[:, hidden:].reshape(piece, 3, hidden)
    return (
        global_out,
        local_out,
        input_grads,
        proj_share[None],
        rest_share[:, :hidden].T[None],
        up_share[None],
        down_share[None],
        gain_share[None],
        grad_table,
    )


def solution(mesh):
    in_specs = (
        P(None, "dp", None),
        P(None, "dp", None),
        P(),
        P("section", None, None),
        P("section", None, None, "tensor"),
        P("section", "tensor", None),
        P("section", None, "tensor"),
        P("section", "tensor", None),
        P(),
        P(None, "dp", None, None),
    )
    out_specs = (
        P(None, "dp", None),
        P(None, "dp", None, None),
        P("section", None, "dp", None),
        P("section", "dp", None, "tensor"),
        P("section", "tensor", "dp"),
        P("section", "dp", "tensor"),
        P("section", "tensor", "dp"),
        P("section", None, "dp"),
        P(None, ("section", "dp"), None),
    )
    return jax.shard_map(body, mesh=mesh, in_specs=in_specs, out_specs=out_specs, check_vma=False)
```

```python
import functools

import jax
import jax.numpy as jnp
from jax import lax
from jax.experimental import pallas as pl
from jax.experimental.pallas import tpu as pltpu
from jax.sharding import PartitionSpec as P

HEAD = 64
CODEBOOKS = 3


eps = 1e-05
far = -1e30


def from_behind(block, axis, distance):
    devices = range(lax.axis_size(axis))
    route = [(i - distance, i) for i in devices if i - distance in devices]
    return lax.ppermute(block, axis, route)


def rms_scale(values):
    return lax.rsqrt(jnp.mean(values * values, axis=-1, keepdims=True) + eps)


def rms_back(values, gain_row, grad_normed):
    factor = rms_scale(values)
    normal = values * factor
    grad_unit = grad_normed * gain_row
    grad_values = factor * (
        grad_unit - normal * jnp.mean(grad_unit * normal, axis=-1, keepdims=True)
    )
    return (grad_values, jnp.sum(grad_normed * normal, axis=0))


def head_total(partial_sum):
    return lax.psum(partial_sum, "tensor")


def matmul(left, right):
    return jnp.dot(left, right, preferred_element_type=jnp.float32)


def across_rows(left, right):
    return lax.dot_general(
        left, right, (((0,), (0,)), ((), ())), preferred_element_type=jnp.float32
    )


def against_rows(left, right):
    return lax.dot_general(
        left, right, (((1,), (1,)), ((), ())), preferred_element_type=jnp.float32
    )


def smooth_gate(values):
    return jax.nn.gelu(values, approximate=True)


def doc_index(positions, doc_ends):
    return jnp.sum((positions[:, None] >= doc_ends[None, :]).astype(jnp.int32), axis=1)


def allowed_mask(query_pos, key_pos, doc_ends):
    same_doc = doc_index(query_pos, doc_ends)[:, None] == doc_index(key_pos, doc_ends)[None, :]
    earlier = key_pos[None, :] <= query_pos[:, None]
    live = (key_pos < doc_ends[-1])[None, :]
    return same_doc & earlier & live | (key_pos[None, :] == query_pos[:, None])


def masked_softmax(scores, mask, factor):
    logits = jnp.where(mask, scores * factor, far)
    top = jnp.max(logits, axis=-1, keepdims=True)
    weights = jnp.exp(logits - top)
    mass = jnp.sum(weights, axis=-1, keepdims=True)
    return (weights / mass, (top + jnp.log(mass))[..., 0])


def frame_forward(packed, query_pos, doc_ends, head_count):
    row_count = packed.shape[0]
    width = packed.shape[1] // 3
    factor = HEAD ** (-0.5)
    parts = packed.reshape(row_count, 3, width)
    all_keys, all_values = (
        lax.all_gather(parts[:, 1], "dp", axis=0, tiled=True),
        lax.all_gather(parts[:, 2], "dp", axis=0, tiled=True),
    )
    key_count = all_keys.shape[0]
    key_pos = jnp.arange(key_count, dtype=jnp.int32)
    mask = allowed_mask(query_pos, key_pos, doc_ends)
    queries = parts[:, 0].reshape(row_count, head_count, -1)
    scores = jnp.einsum(
        "qhe,khe->hqk",
        queries,
        all_keys.reshape(key_count, head_count, -1),
        preferred_element_type=jnp.float32,
    )
    probs, log_mass = masked_softmax(scores, mask[None], factor)
    attended = jnp.einsum(
        "hqk,khe->qhe",
        probs.astype(jnp.bfloat16),
        all_values.reshape(key_count, head_count, -1),
        preferred_element_type=jnp.float32,
    )
    return (attended.reshape(row_count, width), log_mass)


def frame_backward(packed, grad_att, log_mass, query_pos, doc_ends, head_count):
    row_count = packed.shape[0]
    width = packed.shape[1] // 3
    factor = HEAD ** (-0.5)
    parts = packed.reshape(row_count, 3, width)
    all_keys, all_values = (
        lax.all_gather(parts[:, 1], "dp", axis=0, tiled=True),
        lax.all_gather(parts[:, 2], "dp", axis=0, tiled=True),
    )
    key_count = all_keys.shape[0]
    key_pos = jnp.arange(key_count, dtype=jnp.int32)
    queries = parts[:, 0].reshape(row_count, head_count, -1)
    grad_heads = grad_att.reshape(row_count, head_count, -1)
    keys_heads = all_keys.reshape(key_count, head_count, -1)
    scores = jnp.einsum("qhe,khe->hqk", queries, keys_heads, preferred_element_type=jnp.float32)
    mask = allowed_mask(query_pos, key_pos, doc_ends)
    probs = jnp.exp(jnp.where(mask[None], scores * factor, far) - log_mass[:, :, None])
    grad_probs = jnp.einsum(
        "qhe,khe->hqk",
        grad_heads,
        all_values.reshape(key_count, head_count, -1),
        preferred_element_type=jnp.float32,
    )
    spread = jnp.sum(probs * grad_probs, axis=-1)
    grad_scores = (probs * (grad_probs - spread[:, :, None]) * factor).astype(jnp.bfloat16)
    grad_queries = jnp.einsum(
        "hqk,khe->qhe", grad_scores, keys_heads, preferred_element_type=jnp.float32
    ).reshape(row_count, width)
    keys_term = jnp.einsum(
        "hqk,qhe->khe", grad_scores, queries, preferred_element_type=jnp.float32
    ).reshape(key_count, width)
    values_term = jnp.einsum(
        "hqk,qhe->khe", probs.astype(jnp.bfloat16), grad_heads, preferred_element_type=jnp.float32
    ).reshape(key_count, width)
    grad_keys, grad_values = (
        lax.psum_scatter(keys_term, "dp", scatter_dimension=0, tiled=True),
        lax.psum_scatter(values_term, "dp", scatter_dimension=0, tiled=True),
    )
    return jnp.stack([grad_queries, grad_keys, grad_values], axis=1).reshape(row_count, 3 * width)


def codebook_forward(packed, head_count):
    row_count = packed.shape[0]
    width = packed.shape[1] // 3
    factor = HEAD ** (-0.5)
    parts = packed.reshape(row_count // CODEBOOKS, CODEBOOKS, 3, head_count, -1)
    scores = jnp.einsum(
        "nche,ndhe->nhcd", parts[:, :, 0], parts[:, :, 1], preferred_element_type=jnp.float32
    )
    order = jnp.arange(CODEBOOKS, dtype=jnp.int32)
    mask = order[None, :] <= order[:, None]
    probs, log_mass = masked_softmax(scores, mask, factor)
    attended = jnp.einsum(
        "nhcd,ndhe->nche",
        probs.astype(jnp.bfloat16),
        parts[:, :, 2],
        preferred_element_type=jnp.float32,
    )
    return (attended.reshape(row_count, width), probs)


def codebook_backward(packed, grad_att, probs, head_count):
    row_count = packed.shape[0]
    width = packed.shape[1] // 3
    factor = HEAD ** (-0.5)
    parts = packed.reshape(row_count // CODEBOOKS, CODEBOOKS, 3, head_count, -1)
    grad_heads = grad_att.reshape(row_count // CODEBOOKS, CODEBOOKS, head_count, -1)
    grad_probs = jnp.einsum(
        "nche,ndhe->nhcd", grad_heads, parts[:, :, 2], preferred_element_type=jnp.float32
    )
    spread = jnp.sum(probs * grad_probs, axis=-1, keepdims=True)
    grad_scores = (probs * (grad_probs - spread) * factor).astype(jnp.bfloat16)
    grad_queries = jnp.einsum(
        "nhcd,ndhe->nche", grad_scores, parts[:, :, 1], preferred_element_type=jnp.float32
    )
    grad_keys = jnp.einsum(
        "nhcd,nche->ndhe", grad_scores, parts[:, :, 0], preferred_element_type=jnp.float32
    )
    grad_values = jnp.einsum(
        "nhcd,nche->ndhe",
        probs.astype(jnp.bfloat16),
        grad_heads,
        preferred_element_type=jnp.float32,
    )
    return jnp.stack([grad_queries, grad_keys, grad_values], axis=2).reshape(row_count, 3 * width)


def layer_forward(inputs, gain_pair, layer_weights, attend):
    w_proj, w_mix, w_rise, w_fall = layer_weights
    normed = (inputs * rms_scale(inputs) * gain_pair[0]).astype(jnp.bfloat16)
    packed = matmul(normed, w_proj.reshape(w_proj.shape[0], -1)).astype(jnp.bfloat16)
    attended, saved = attend(packed)
    attended_low = attended.astype(jnp.bfloat16)
    resid = inputs + head_total(matmul(attended_low, w_mix))
    normed_mid = (resid * rms_scale(resid) * gain_pair[1]).astype(jnp.bfloat16)
    rise = matmul(normed_mid, w_rise)
    active = smooth_gate(rise).astype(jnp.bfloat16)
    result = resid + head_total(matmul(active, w_fall))
    return (result, (normed, packed, attended_low, saved, resid, normed_mid, rise, active))


def layer_backward(inputs, gain_pair, layer_weights, kept, grad_result, attend_back):
    w_proj, w_mix, w_rise, w_fall = layer_weights
    normed, packed, attended_low, saved, resid, normed_mid, rise, active = kept
    grad_fall_low = grad_result.astype(jnp.bfloat16)
    grad_fall_w = across_rows(active, grad_fall_low)
    grad_active = against_rows(grad_fall_low, w_fall)
    grad_rise = jax.vjp(smooth_gate, rise)[1](grad_active)[0].astype(jnp.bfloat16)
    grad_rise_w = across_rows(normed_mid, grad_rise)
    grad_mid = head_total(against_rows(grad_rise, w_rise))
    back_mid, gain_mid = rms_back(resid, gain_pair[1], grad_mid)
    grad_resid = grad_result + back_mid
    resid_low = grad_resid.astype(jnp.bfloat16)
    grad_mix_w = across_rows(attended_low, resid_low)
    grad_att = against_rows(resid_low, w_mix).astype(jnp.bfloat16)
    grad_packed = attend_back(packed, grad_att, saved).astype(jnp.bfloat16)
    flat_proj = w_proj.reshape(w_proj.shape[0], -1)
    grad_proj_w = across_rows(normed, grad_packed).reshape(w_proj.shape)
    grad_normed = head_total(against_rows(grad_packed, flat_proj))
    back_in, gain_in = rms_back(inputs, gain_pair[0], grad_normed)
    return (
        grad_resid + back_in,
        (grad_proj_w, grad_mix_w, grad_rise_w, grad_fall_w, jnp.stack([gain_in, gain_mid])),
    )


def plain_body(frames, codes, lengths, gains, w_qkv, w_out, w_up, w_down, table, cotangent):
    on_first = lax.axis_index("section") == 0
    head_count = w_qkv.shape[3] // HEAD
    layer_weights = (w_qkv[0], w_out[0], w_up[0], w_down[0])
    gains_here = gains[0]
    frame_count = frames.shape[1]
    query_pos = lax.axis_index("dp") * frame_count + jnp.arange(frame_count, dtype=jnp.int32)
    zero_grads = (
        jnp.zeros(w_qkv.shape[1:], jnp.float32),
        jnp.zeros(w_out.shape[1:], jnp.float32),
        jnp.zeros(w_up.shape[1:], jnp.float32),
        jnp.zeros(w_down.shape[1:], jnp.float32),
        jnp.zeros(gains.shape[1:], jnp.float32),
    )

    def global_forward_rows(frame_rows, slot_lengths):
        doc_ends = jnp.cumsum(slot_lengths)
        return (
            doc_ends,
            layer_forward(
                frame_rows.astype(jnp.float32),
                gains_here,
                layer_weights,
                lambda packed: frame_forward(packed, query_pos, doc_ends, head_count),
            ),
        )

    def global_step(carry, inputs):
        doc_ends, (result, kept) = global_forward_rows(inputs[0], inputs[1])
        return (carry, result.astype(jnp.bfloat16))

    global_low = lax.scan(global_step, jnp.zeros((), jnp.int32), (frames, lengths))[1]
    arrived = from_behind(global_low, "section", 1)
    books = jnp.arange(CODEBOOKS, dtype=jnp.int32)
    looked_up = table[books[None, None, :], codes]
    local_in = arrived.astype(jnp.float32)[:, :, None, :] + looked_up.astype(jnp.float32)
    local_rows = local_in.reshape(-1, local_in.shape[-1])
    local_result, local_kept = layer_forward(
        local_rows, gains_here, layer_weights, lambda packed: codebook_forward(packed, head_count)
    )
    grad_rows, local_grads = layer_backward(
        local_rows,
        gains_here,
        layer_weights,
        local_kept,
        cotangent.astype(jnp.float32).reshape(local_rows.shape),
        lambda packed, grad_att, saved: codebook_backward(packed, grad_att, saved, head_count),
    )
    grad_frame = jnp.sum(grad_rows.reshape(local_in.shape), axis=2)
    table_slots = (books[None, None, :] * table.shape[1] + codes).reshape(-1)
    table_term = jax.ops.segment_sum(
        grad_rows, table_slots, num_segments=table.shape[0] * table.shape[1]
    ).reshape(table.shape)
    local_low = local_result.astype(jnp.bfloat16).reshape(cotangent.shape)
    table_part = jnp.where(on_first, jnp.zeros(table.shape, jnp.float32), table_term)
    grad_frame = jnp.where(on_first, jnp.zeros(frames.shape, jnp.float32), grad_frame)
    grad_table = lax.psum_scatter(table_part, ("section", "dp"), scatter_dimension=1, tiled=True)
    grad_back, local_copy = from_behind((grad_frame.astype(jnp.bfloat16), local_low), "section", -1)

    def global_back(totals, inputs):
        frame_rows, slot_lengths, grad_low = inputs
        doc_ends, (result, kept) = global_forward_rows(frame_rows, slot_lengths)
        grad_in, grads = layer_backward(
            frame_rows.astype(jnp.float32),
            gains_here,
            layer_weights,
            kept,
            grad_low.astype(jnp.float32),
            lambda packed, grad_att, saved: frame_backward(
                packed, grad_att, saved, query_pos, doc_ends, head_count
            ),
        )
        return (jax.tree.map(jnp.add, totals, grads), grad_in)

    global_grads, grad_frames = lax.scan(global_back, zero_grads, (frames, lengths, grad_back))

    def pick(global_part, local_part):
        return jnp.where(on_first, global_part, local_part)

    proj_sum, mix_sum, rise_sum, fall_sum, gain_sum = jax.tree.map(pick, global_grads, local_grads)
    proj_share, mix_share, rise_share, fall_share, gain_share = (
        lax.psum_scatter(proj_sum, "dp", scatter_dimension=0, tiled=True),
        lax.psum_scatter(mix_sum, "dp", scatter_dimension=1, tiled=True),
        lax.psum_scatter(rise_sum, "dp", scatter_dimension=0, tiled=True),
        lax.psum_scatter(fall_sum, "dp", scatter_dimension=1, tiled=True),
        lax.psum_scatter(gain_sum, "dp", scatter_dimension=1, tiled=True),
    )
    global_out = jnp.where(on_first, global_low, arrived)
    local_out = jnp.where(on_first, local_copy, local_low)
    input_grads = jnp.where(on_first, grad_frames, grad_frame)[None]
    return (
        global_out,
        local_out,
        input_grads,
        proj_share[None],
        mix_share[None],
        rise_share[None],
        fall_share[None],
        gain_share[None],
        grad_table,
    )


def lasting(us):
    return pl.CostEstimate(flops=int(us * 1.1e9), bytes_accessed=int(us * 1e6), transcendentals=0)

f32=jnp.float32; bf=jnp.bfloat16

def mm(a,b): return jnp.dot(a,b,preferred_element_type=f32)
def mm_nt(a,b): return lax.dot_general(a,b,(((1,),(1,)),((),())),preferred_element_type=f32)

def gelu_both(v):
    c0 = 0.7978845608028654
    c1 = c0 * 0.044715
    sq = v * v
    half = 0.5 + 0.5 * jnp.tanh(v * (c0 + c1 * sq))
    act = v * half
    return act, half + act * (1.0 - half) * (2.0 * c0 + 6.0 * c1 * sq)


def local_kernel(g_ref, emb_ref, cot_ref, gao_ref, gax_ref, gains_ref, e_ref, et_ref,
                 pqo, pqx, woo, wox, wuo, wux,
                 resid_o, acto_o, griso_o, gpo_o, actx_o, send_o, dx_o, gframe_o, gg_o,
                 q_s, k_s, v_s, p_s, gp_s, prod_s, wide_s, r_s, gm_s, gatt_s):
    F=g_ref.shape[0]; R=3*F; D=g_ref.shape[1]; H2=D//2
    W=acto_o.shape[2]
    grisx_o=send_o.at[:,:,0:W]
    mid_o,glow_o,normed_o=(send_o.at[:,:,W+j*D:W+(j+1)*D] for j in range(3))
    gpx_o=[send_o.at[:,:,W+3*D+j*H2:W+3*D+(j+1)*H2] for j in range(4)]
    step=pl.program_id(0)
    gain0=gains_ref[0:1,:]; gain1=gains_ref[1:2,:]
    g=g_ref[...].astype(f32)
    scr=(q_s,k_s,v_s)
    r0s=[]
    for c in range(3):
        x=g+emb_ref[c].astype(f32)
        r0=lax.rsqrt(jnp.mean(x*x,axis=-1,keepdims=True)+eps)
        r0s.append(r0)
        normed_o[c]=(x*r0*gain0).astype(bf)
    normed=normed_o[...].reshape(R,D)
    for j in range(3):
        scr[j][:,0:H2]=mm(normed,pqo[j]).astype(bf)
        scr[j][:,H2:D]=mm(normed,pqx[j]).astype(bf)
    pairs=[(c,c2) for c in range(3) for c2 in range(c+1)]
    rows=lambda ref,c: ref[c*F:(c+1)*F,:]
    for n,(c,c2) in enumerate(pairs):
        prod_s[n*F:(n+1)*F,:]=(rows(q_s,c).astype(f32)*rows(k_s,c2).astype(f32)).astype(bf)
    p_s[...]=mm(prod_s[...],e_ref[...])*0.125
    for c in range(3):
        own=[n for n,pr in enumerate(pairs) if pr[0]==c]
        ss=[rows(p_s,n) for n in own]
        top=functools.reduce(jnp.maximum,ss)
        ws=[jnp.exp(s-top) for s in ss]
        inv=1.0/functools.reduce(jnp.add,ws)
        for n,w in zip(own,ws): p_s[n*F:(n+1)*F,:]=w*inv
    wide_s[...]=mm(p_s[...].astype(bf),et_ref[...]).astype(bf)
    for c in range(3):
        acc=functools.reduce(jnp.add,[rows(wide_s,n).astype(f32)*rows(v_s,pr[1]).astype(f32) for n,pr in enumerate(pairs) if pr[0]==c])
        att=acc.astype(bf)
        gpo_o[0,c]=att[:,0:H2]; gpx_o[0][c]=att[:,H2:D]
    xs=(g_ref[...].astype(f32)[None]+emb_ref[...].astype(f32)).reshape(R,D)
    resid=xs+mm(gpo_o[0].reshape(R,H2),woo[...])+mm(gpx_o[0][...].reshape(R,H2),wox[...])
    r1=lax.rsqrt(jnp.mean(resid*resid,axis=-1,keepdims=True)+eps)
    resid_o[...]=resid.reshape(3,F,D)
    nm=(resid*r1*gain1).astype(bf)
    mid_o[...]=nm.reshape(3,F,D)
    ch=512
    gm=None
    for (wu,act_o,gris_o,ga_ref) in ((wuo,acto_o,griso_o,gao_ref),(wux,actx_o,grisx_o,gax_ref)):
        for j in range(wu.shape[1]//ch):
            sl=slice(j*ch,(j+1)*ch)
            w=wu[:,sl]
            act,gr=gelu_both(mm(nm,w))
            act_o[:,:,sl]=act.astype(bf).reshape(3,F,ch)
            gl=(ga_ref[:,:,sl].reshape(R,ch).astype(f32)*gr).astype(bf)
            gris_o[:,:,sl]=gl.reshape(3,F,ch)
            t=mm_nt(gl,w)
            if gm is None:
                gm_s[...]=t; gm=1
            else:
                gm_s[...]+=t
    gmid=gm_s[...]
    n1=resid_o[...].reshape(R,D)*r1
    u=gmid*gain1
    gres=cot_ref[...].reshape(R,D).astype(f32)+r1*(u-n1*jnp.mean(u*n1,axis=-1,keepdims=True))
    gsum1=jnp.sum(gmid*n1,axis=0,keepdims=True)
    r_s[...]=gres
    glow=gres.astype(bf)
    glow_o[...]=glow.reshape(3,F,D)
    gatt_s[:,0:H2]=mm_nt(glow,woo[...]).astype(bf)
    gatt_s[:,H2:D]=mm_nt(glow,wox[...]).astype(bf)
    def add(a,b): return b if a is None else a+b
    for n,(c,c2) in enumerate(pairs):
        prod_s[n*F:(n+1)*F,:]=(rows(gatt_s,c).astype(f32)*rows(v_s,c2).astype(f32)).astype(bf)
    gp_s[...]=mm(prod_s[...],e_ref[...])
    for c in range(3):
        own=[n for n,pr in enumerate(pairs) if pr[0]==c]
        ps=[rows(p_s,n) for n in own]
        gps=[rows(gp_s,n) for n in own]
        spread=functools.reduce(jnp.add,[p*gp for p,gp in zip(ps,gps)])
        for n,p,gp in zip(own,ps,gps): gp_s[n*F:(n+1)*F,:]=p*(gp-spread)*0.125
    prod_s[...]=mm(gp_s[...].astype(bf),et_ref[...]).astype(bf)
    for c in range(3):
        take=lambda which,left,right,at: functools.reduce(jnp.add,[rows(left,n).astype(f32)*rows(right,pr[1-which]).astype(f32) for n,pr in enumerate(pairs) if pr[which]==at]).astype(bf)
        for j,a in ((1,take(0,prod_s,k_s,c)),(2,take(1,prod_s,q_s,c)),(3,take(1,wide_s,gatt_s,c))):
            gpo_o[j,c]=a[:,0:H2]; gpx_o[j][c]=a[:,H2:D]
    gn=None
    for j in range(3):
        gn=add(gn,mm_nt(gpo_o[j+1].reshape(R,H2),pqo[j]))
        gn=gn+mm_nt(gpx_o[j+1][...].reshape(R,H2),pqx[j])
    gm_s[...]=gn
    tot=None; gsum0=None
    for c in range(3):
        gn=gm_s[c*F:(c+1)*F,:]
        n0=(g_ref[...].astype(f32)+emb_ref[c].astype(f32))*r0s[c]
        w=gn*gain0
        dx=r_s[c*F:(c+1)*F,:]+r0s[c]*(w-n0*jnp.mean(w*n0,axis=-1,keepdims=True))
        gsum0=add(gsum0,jnp.sum(gn*n0,axis=0,keepdims=True))
        dx_o[c]=dx.astype(bf)
        tot=add(tot,dx)
    gframe_o[...]=tot
    @pl.when(step==0)
    def _(): gg_o[...]=jnp.zeros_like(gg_o)
    gg_o[0:1,:]+=gsum0
    gg_o[1:2,:]+=gsum1

def local_skip(at_ref,*refs):
    @pl.when(at_ref[0]==1)
    def _():
        local_kernel(*refs)

def local_call(at,g,emb,cot,gao,gax,gains,pqo,pqx,woo,wox,wuo,wux,tile=128):
    N,D=g.shape; H2=D//2; FH=wuo.shape[1]; F=tile
    E=(jnp.arange(D)[:,None]//HEAD==jnp.arange(128)[None,:]).astype(bf)
    ET=E.T
    c3=lambda w: pl.BlockSpec((3,F,w),lambda i,s:(0,i,0))
    whole=lambda shp: pl.BlockSpec(shp,lambda i,s:(0,)*len(shp),pipeline_mode=pl.Buffered(1))
    sd=jax.ShapeDtypeStruct
    S=FH+3*D+4*H2
    out_shape=(sd((3,N,D),f32),sd((3,N,FH),bf),sd((3,N,FH),bf),sd((4,3,N,H2),bf),sd((3,N,FH),bf),sd((3,N,S),bf),sd((3,N,D),bf),sd((N,D),f32),sd((2,D),f32))
    gp=pl.BlockSpec((4,3,F,H2),lambda i,s:(0,0,i,0))
    return pl.pallas_call(local_skip, grid_spec=pltpu.PrefetchScalarGridSpec(num_scalar_prefetch=1,grid=(N//F,),
      in_specs=[pl.BlockSpec((F,D),lambda i,s:(i,0)),c3(D),c3(D),c3(FH),c3(FH),whole((2,D)),whole(E.shape),whole(ET.shape),
        whole(pqo.shape),whole(pqx.shape),whole(woo.shape),whole(wox.shape),whole(wuo.shape),whole(wux.shape)],
      out_specs=(c3(D),c3(FH),c3(FH),gp,c3(FH),c3(S),c3(D),pl.BlockSpec((F,D),lambda i,s:(i,0)),pl.BlockSpec((2,D),lambda i,s:(0,0))),
      scratch_shapes=[pltpu.VMEM((3*F,D),bf)]*3+[pltpu.VMEM((6*F,128),f32)]*2+[pltpu.VMEM((6*F,D),bf)]*2+[pltpu.VMEM((3*F,D),f32),pltpu.VMEM((3*F,D),f32),pltpu.VMEM((3*F,D),bf)]),
      out_shape=out_shape,
      compiler_params=pltpu.CompilerParams(vmem_limit_bytes=65400 * 1024),
      cost_estimate=lasting(57),
      name="local_layer",
    )(at,g,emb,cot,gao,gax,gains,E,ET,pqo,pqx,woo,wox,wuo,wux)

def attend_kernel(at_ref, xo_ref, xs_ref, xc_ref, xb_ref, gain_ref, proj_ref, qid_ref, kid_ref,
                  normed_ref, q_ref, k_ref, v_ref, near_ref, off_ref):
    step = pl.program_id(0)
    rows = xo_ref.shape[0]

    @pl.when((at_ref[0] == 0) & (step == 0))
    def _():
        for j, x_ref in enumerate((xo_ref, xs_ref, xc_ref, xb_ref)):
            part = slice(j * rows, (j + 1) * rows)
            x = x_ref[...].astype(f32)
            scale = lax.rsqrt(jnp.mean(x * x, axis=-1, keepdims=True) + eps)
            normed_ref[part, :] = (x * scale * gain_ref[0:1, :]).astype(bf)
        for j, ref in enumerate((q_ref, k_ref, v_ref)):
            ref[...] = mm(normed_ref[...], proj_ref[j]).astype(bf)

    @pl.when(at_ref[0] == 0)
    def _():
        bias = jnp.where(
            ((qid_ref[:, 1:2] == kid_ref[1:2, :]) & (kid_ref[0:1, :] <= qid_ref[:, 0:1]))
            | (kid_ref[0:1, :] == qid_ref[:, 0:1]),
            0.0,
            far,
        )
        lane = lax.broadcasted_iota(jnp.int32, (1, 2 * HEAD), 1) // HEAD
        here_rows = pl.ds(pl.multiple_of(step * rows, rows), rows)
        for pair in range(q_ref.shape[1] // (2 * HEAD)):
            cols = slice(pair * 2 * HEAD, (pair + 1) * 2 * HEAD)
            q, k, v = q_ref[here_rows, cols], k_ref[:, cols], v_ref[:, cols]
            total = None
            for side in range(2):
                here = lane == side
                scores = mm_nt(jnp.where(here, q * HEAD ** (-0.5), jnp.zeros_like(q)), k) + bias
                top = jnp.max(scores, axis=-1, keepdims=True)
                weights = jnp.exp(scores - top)
                mass = jnp.sum(weights, axis=-1, keepdims=True)
                probs = (weights * (1.0 / mass)).astype(bf)
                term = mm(probs, jnp.where(here, v, jnp.zeros_like(v)))
                total = term if total is None else total + term
            for odd, ref in ((0, near_ref), (1, off_ref)):

                @pl.when(step % 2 == odd)
                def _():
                    ref[0, :, cols] = total.astype(bf)


def attend_call(at, blocks, gains, proj, qid, kid):
    rows, width = blocks[0].shape
    cols = proj.shape[2] // 2
    total = 4 * rows
    whole = lambda shape: pl.BlockSpec(shape, lambda i, s: (0,) * len(shape))
    sd = jax.ShapeDtypeStruct
    half = pl.BlockSpec((1, rows, cols), lambda i, s: (i // 2, 0, 0))
    return pl.pallas_call(
        attend_kernel,
        grid_spec=pltpu.PrefetchScalarGridSpec(
            num_scalar_prefetch=1,
            grid=(4,),
            in_specs=[whole((rows, width))] * 4
            + [
                whole(gains.shape),
                pl.BlockSpec((3, width, cols), lambda i, s: (0, 0, s[2])),
                pl.BlockSpec((rows, 2), lambda i, s: (i, 0)),
                whole(kid.shape),
            ],
            out_specs=(whole((total, width)), *[whole((total, cols))] * 3, half, half),
        ),
        out_shape=(sd((total, width), bf), *[sd((total, cols), bf)] * 3, *[sd((2, rows, cols), bf)] * 2),
        compiler_params=pltpu.CompilerParams(vmem_limit_bytes=60 * 1024 * 1024),
        cost_estimate=lasting(18),
        name="frame_attention",
    )(at, *blocks, gains, proj, qid, kid)


def attend_back_kernel(at_ref, q_ref, k_ref, v_ref, g_ref, qid_ref, kid_ref, gq_ref, gk_ref, gv_ref, ks_ref, vs_ref):
    @pl.when(at_ref[0] == 0)
    def _():
        step = pl.program_id(0)

        @pl.when(step == 0)
        def _():
            ks_ref[...] = jnp.zeros_like(ks_ref)
            vs_ref[...] = jnp.zeros_like(vs_ref)

        bias = jnp.where(
            ((qid_ref[:, 1:2] == kid_ref[1:2, :]) & (kid_ref[0:1, :] <= qid_ref[:, 0:1]))
            | (kid_ref[0:1, :] == qid_ref[:, 0:1]),
            0.0,
            far,
        )
        lane = lax.broadcasted_iota(jnp.int32, (1, 2 * HEAD), 1) // HEAD
        for pair in range(q_ref.shape[1] // (2 * HEAD)):
            cols = slice(pair * 2 * HEAD, (pair + 1) * 2 * HEAD)
            q, k, v, g = q_ref[:, cols], k_ref[:, cols], v_ref[:, cols], g_ref[:, cols]
            gq = None
            for side in range(2):
                here = lane == side
                qh = jnp.where(here, q, jnp.zeros_like(q))
                gh = jnp.where(here, g, jnp.zeros_like(g))
                kh = jnp.where(here, k, jnp.zeros_like(k))
                scores = mm_nt(qh * HEAD ** (-0.5), k) + bias
                top = jnp.max(scores, axis=-1, keepdims=True)
                weights = jnp.exp(scores - top)
                mass = jnp.sum(weights, axis=-1, keepdims=True)
                probs = weights * (1.0 / mass)
                grad_probs = mm_nt(gh, v)
                spread = jnp.sum(probs * grad_probs, axis=-1, keepdims=True)
                gs = (probs * (grad_probs - spread) * HEAD ** (-0.5)).astype(bf)
                term = mm(gs, kh)
                gq = term if gq is None else gq + term
                ks_ref[:, cols] += across_rows(gs, qh)
                vs_ref[:, cols] += across_rows(probs.astype(bf), gh)
            gq_ref[:, cols] = gq.astype(bf)

        @pl.when(step == pl.num_programs(0) - 1)
        def _():
            gk_ref[...] = ks_ref[...].astype(bf)
            gv_ref[...] = vs_ref[...].astype(bf)


def attend_back_call(at, q, k, v, g, qid, kid, rows):
    total, width = q.shape
    part = pl.BlockSpec((rows, width), lambda i, s: (i, 0))
    whole = pl.BlockSpec((total, width), lambda i, s: (0, 0))
    shape = jax.ShapeDtypeStruct((total, width), bf)
    return pl.pallas_call(
        attend_back_kernel,
        grid_spec=pltpu.PrefetchScalarGridSpec(
            num_scalar_prefetch=1,
            grid=(total // rows,),
            in_specs=[part, whole, whole, part, pl.BlockSpec((rows, 2), lambda i, s: (i, 0)), pl.BlockSpec(kid.shape, lambda i, s: (0, 0))],
            out_specs=(part, whole, whole),
            scratch_shapes=[pltpu.VMEM((total, width), f32)] * 2,
        ),
        out_shape=(shape, shape, shape),
        compiler_params=pltpu.CompilerParams(vmem_limit_bytes=60 * 1024 * 1024),
        cost_estimate=lasting(0.01),
        name="frame_attention_back",
    )(at, q, k, v, g, qid, kid)


def front_kernel(at_ref, x_ref, near_ref, off_ref, core_ref, gain_ref, oo_ref, ox_ref, uo_ref, ux_ref, do_ref, dx_ref,
                 resid_ref, mid_ref, act_o, act_x, slope_o, slope_x, out_ref, total_ref):
    @pl.when(at_ref[0] == 0)
    def _():
        step = pl.program_id(0)
        turn = pl.num_programs(0) // 2

        @pl.when(step == 0)
        def _():
            cols = near_ref.shape[2]
            resid = x_ref[...].astype(f32)
            for flip, part, out in ((0, near_ref, oo_ref), (1, off_ref, oo_ref), (0, core_ref, ox_ref), (1, core_ref, ox_ref)):
                spot = pl.ds(pl.multiple_of((at_ref[2] ^ flip) * cols, cols), cols)
                resid = resid + mm(part[flip if part is core_ref else 0], out[spot, :])
            resid_ref[...] = resid
            scale = lax.rsqrt(jnp.mean(resid * resid, axis=-1, keepdims=True) + eps)
            mid_ref[...] = (resid * scale * gain_ref[1:2, :]).astype(bf)
            total_ref[...] = resid

        def part(up, down, act_ref, slope_ref):
            act, slope = gelu_both(mm(mid_ref[...], up[...]))
            act = act.astype(bf)
            act_ref[...] = act
            slope_ref[...] = slope.astype(bf)
            total_ref[...] += mm(act, down[...])

        @pl.when(step < turn)
        def _():
            part(uo_ref, do_ref, act_o, slope_o)

        @pl.when(step >= turn)
        def _():
            part(ux_ref, dx_ref, act_x, slope_x)

        @pl.when(step == pl.num_programs(0) - 1)
        def _():
            out_ref[...] = total_ref[...].astype(bf)


def halves_specs(turn, chunk, width, rows):
    first = lambda i, s: jnp.minimum(i, turn - 1) * (1 - s[0])
    later = lambda i, s: jnp.maximum(i - turn, 0) * (1 - s[0])
    ups = [pl.BlockSpec((width, chunk), lambda i, s, f=f: (0, f(i, s))) for f in (first, later)]
    downs = [pl.BlockSpec((chunk, width), lambda i, s, f=f: (f(i, s), 0)) for f in (first, later)]
    cols = [pl.BlockSpec((rows, chunk), lambda i, s, f=f: (0, f(i, s))) for f in (first, later)]
    return ups, downs, cols


def front_call(at, x, near, off, from_core, gains, out_own, out_oth, up_own, up_oth, down_own, down_oth, chunk=1024):
    rows, width = x.shape
    hidden = up_own.shape[1]
    turn = hidden // chunk
    ups, downs, cols = halves_specs(turn, chunk, width, rows)
    whole = lambda a: pl.BlockSpec(a.shape, lambda i, s: (0,) * a.ndim)
    sd = jax.ShapeDtypeStruct
    full = pl.BlockSpec((rows, width), lambda i, s: (0, 0))
    hid = sd((rows, hidden), bf)
    return pl.pallas_call(
        front_kernel,
        grid_spec=pltpu.PrefetchScalarGridSpec(
            num_scalar_prefetch=1,
            grid=(2 * turn,),
            in_specs=[full, whole(near), whole(off), whole(from_core), whole(gains), whole(out_own), whole(out_oth), *ups, *downs],
            out_specs=(full, full, cols[0], cols[1], cols[0], cols[1], full),
            scratch_shapes=[pltpu.VMEM((rows, width), f32)],
        ),
        out_shape=(sd((rows, width), f32), sd((rows, width), bf), hid, hid, hid, hid, sd((rows, width), bf)),
        compiler_params=pltpu.CompilerParams(vmem_limit_bytes=60 * 1024 * 1024),
        cost_estimate=lasting(15),
        name="global_forward",
    )(at, x, near, off, from_core, gains, out_own, out_oth, up_own, up_oth, down_own, down_oth)


def back_kernel(at_ref, g_ref, resid_ref, gain_ref, so_ref, sx_ref, uo_ref, ux_ref, do_ref, dx_ref,
                rise_o, rise_x, grad_ref, low_ref, gsum_ref, total_ref):
    @pl.when(at_ref[0] == 0)
    def _():
        step = pl.program_id(0)
        turn = pl.num_programs(0) // 2

        def part(up, down, slope_ref, rise_ref):
            rise = (mm_nt(g_ref[...], down[...]) * slope_ref[...].astype(f32)).astype(bf)
            rise_ref[...] = rise
            return mm_nt(rise, up[...])

        @pl.when(step == 0)
        def _():
            total_ref[...] = part(uo_ref, do_ref, so_ref, rise_o)

        @pl.when((step > 0) & (step < turn))
        def _():
            total_ref[...] += part(uo_ref, do_ref, so_ref, rise_o)

        @pl.when(step >= turn)
        def _():
            total_ref[...] += part(ux_ref, dx_ref, sx_ref, rise_x)

        @pl.when(step == pl.num_programs(0) - 1)
        def _():
            resid = resid_ref[...]
            scale = lax.rsqrt(jnp.mean(resid * resid, axis=-1, keepdims=True) + eps)
            normal = resid * scale
            total = total_ref[...]
            unit = total * gain_ref[1:2, :]
            grad = g_ref[...].astype(f32) + scale * (unit - normal * jnp.mean(unit * normal, axis=-1, keepdims=True))
            grad_ref[...] = grad
            low_ref[...] = grad.astype(bf)
            gsum_ref[...] = jnp.sum(total * normal, axis=0, keepdims=True)


def back_call(at, g, resid, gains, slope_own, slope_oth, up_own, up_oth, down_own, down_oth, chunk=1024):
    rows, width = g.shape
    hidden = up_own.shape[1]
    turn = hidden // chunk
    ups, downs, cols = halves_specs(turn, chunk, width, rows)
    sd = jax.ShapeDtypeStruct
    full = pl.BlockSpec((rows, width), lambda i, s: (0, 0))
    hid = sd((rows, hidden), bf)
    line = pl.BlockSpec((1, width), lambda i, s: (0, 0))
    return pl.pallas_call(
        back_kernel,
        grid_spec=pltpu.PrefetchScalarGridSpec(
            num_scalar_prefetch=1,
            grid=(2 * turn,),
            in_specs=[full, full, pl.BlockSpec(gains.shape, lambda i, s: (0, 0)), *cols, *ups, *downs],
            out_specs=(*cols, full, full, line),
            scratch_shapes=[pltpu.VMEM((rows, width), f32)],
        ),
        out_shape=(hid, hid, sd((rows, width), f32), sd((rows, width), bf), sd((1, width), f32)),
        compiler_params=pltpu.CompilerParams(vmem_limit_bytes=60 * 1024 * 1024),
        cost_estimate=lasting(13),
        name="global_backward",
    )(at, g, resid, gains, slope_own, slope_oth, up_own, up_oth, down_own, down_oth)


def split_sides(total, side, mine_ref, theirs_ref, at):
    half = total.shape[0] // 2
    top, bottom = total[:half].astype(bf), total[half:].astype(bf)
    mine_ref[at] = jnp.where(side == 0, top, bottom)
    theirs_ref[at] = jnp.where(side == 0, bottom, top)


def deal(total_ref, at_ref, mine_ref, theirs_ref, plane_first):
    piece = total_ref.shape[0] // 8
    for jz in range(4):
        for jy in range(2):
            place = (at_ref[1] ^ jz) * 2 + (at_ref[2] ^ jy)
            rows = pl.ds(pl.multiple_of(place * piece, piece), piece)
            low, high = jz % 2, jz // 2
            part = total_ref[rows, :].astype(bf)
            if plane_first:
                (theirs_ref if low else mine_ref)[high, jy] = part
            else:
                (theirs_ref if jy else mine_ref)[low * 2 + high] = part


def weight_kernel(at_ref, left, left_in, right, right_in, mine_ref, theirs_ref, total_ref, turned, turned_in, *, here, plane_first):
    @pl.when(at_ref[0] == here)
    def _():
        @pl.when(pl.program_id(0) == 0)
        def _():
            turned[...] = left[...].T
            turned_in[...] = left_in[...].T

        total_ref[...] = mm(turned[...], right[...]) + mm(turned_in[...], right_in[...])
        deal(total_ref, at_ref, mine_ref, theirs_ref, plane_first)


def weight_call(at, here, four, skip, plane_first, name, us, width, cols, chunk=512):
    piece = width // 8
    now = lambda i, s: jnp.where(s[0] == here, i, 0)
    whole = [
        pl.BlockSpec((a.shape[0], width), lambda i, s, c=c: (0, c), pipeline_mode=pl.Buffered(1))
        for a, c in zip(four[:2], skip)
    ]
    part = [
        pl.BlockSpec((a.shape[0], chunk), lambda i, s, c=c: (0, now(i, s) + c)) for a, c in zip(four[2:], skip[2:])
    ]
    if plane_first:
        shape = jax.ShapeDtypeStruct((2, 2, piece, cols), bf)
        out = pl.BlockSpec((2, 2, piece, chunk), lambda i, s: (0, 0, 0, now(i, s)))
    else:
        shape = jax.ShapeDtypeStruct((4, piece, cols), bf)
        out = pl.BlockSpec((4, piece, chunk), lambda i, s: (0, 0, now(i, s)))
    return pl.pallas_call(
        functools.partial(weight_kernel, here=here, plane_first=plane_first),
        grid_spec=pltpu.PrefetchScalarGridSpec(
            num_scalar_prefetch=1,
            grid=(cols // chunk,),
            in_specs=whole + part,
            out_specs=(out, out),
            scratch_shapes=[pltpu.VMEM((width, chunk), f32)] + [pltpu.VMEM((width, a.shape[0]), bf) for a in four[:2]],
        ),
        out_shape=(shape, shape),
        compiler_params=pltpu.CompilerParams(vmem_limit_bytes=60 * 1024 * 1024),
        cost_estimate=lasting(us),
        name=name,
    )(at, *four)


def rest_kernel(at_ref, *refs, here):
    pairs = (len(refs) - 3) // 4
    lows, normeds, rights = (refs[j * pairs : (j + 1) * pairs] for j in range(3))
    mine_ref, theirs_ref, total_ref = refs[3 * pairs : 3 * pairs + 3]
    turned = refs[3 * pairs + 3 :]
    step = pl.program_id(0)
    piece = total_ref.shape[0] // 8

    @pl.when(at_ref[0] == here)
    def _():
        for when, lefts in ((0, lows), (1, normeds)):

            @pl.when(step == when)
            def _():
                for left, turn in zip(lefts, turned):
                    turn[...] = left[...].T

        total = None
        for turn, right in zip(turned, rights):
            term = mm(turn[...], right[0] if len(right.shape) == 3 else right[...])
            total = term if total is None else total + term
        total_ref[...] = total
        for jz in range(4):
            for jy in range(2):
                place = (at_ref[1] ^ jz) * 2 + (at_ref[2] ^ jy)
                rows = pl.ds(pl.multiple_of(place * piece, piece), piece)
                for h in range(mine_ref.shape[2]):
                    cols = slice(h * mine_ref.shape[4], (h + 1) * mine_ref.shape[4])
                    (theirs_ref if jy else mine_ref)[jz % 2 * 2 + jz // 2, 0, h] = total_ref[rows, cols].astype(bf)


def rest_call(at, here, lows, normeds, rights, name, us, width):
    piece = width // 8
    count = 4
    narrow = width // 4
    size = rights[0][0].shape[2]
    whole = lambda pair: pl.BlockSpec((pair[0].shape[0], width), lambda i, s: (0, pair[1]), pipeline_mode=pl.Buffered(1))

    def part(pair):
        a, c = pair
        now = lambda i, s: jnp.where(s[0] == here, i, 0)
        if a.ndim == 3:
            return pl.BlockSpec((1,) + a.shape[1:], lambda i, s: (now(i, s), 0, 0))
        return pl.BlockSpec((a.shape[0], size), lambda i, s: (0, c + now(i, s)))

    halves = size // narrow
    shape = jax.ShapeDtypeStruct((4, count, halves, piece, narrow), bf)
    out = pl.BlockSpec((4, 1, halves, piece, narrow), lambda i, s: (0, jnp.where(s[0] == here, i, 0), 0, 0, 0))
    return pl.pallas_call(
        functools.partial(rest_kernel, here=here),
        grid_spec=pltpu.PrefetchScalarGridSpec(
            num_scalar_prefetch=1,
            grid=(count,),
            in_specs=[*map(whole, lows), *map(whole, normeds), *map(part, rights)],
            out_specs=(out, out),
            scratch_shapes=[pltpu.VMEM((width, size), f32)] + [pltpu.VMEM((width, a.shape[0]), bf) for a, _ in lows],
        ),
        out_shape=(shape, shape),
        compiler_params=pltpu.CompilerParams(vmem_limit_bytes=60 * 1024 * 1024),
        cost_estimate=lasting(us),
        name=name,
    )(at, *(a for a, _ in (*lows, *normeds, *rights)))


def fall_kernel(at_ref, resid_ref, ao_ref, ax_ref, do_ref, dx_ref, out_ref, total_ref):
    step = pl.program_id(0)
    turn = pl.num_programs(0) // 2
    books, planes, half = out_ref.shape[1], out_ref.shape[0], out_ref.shape[2]

    @pl.when(at_ref[0] == 1)
    def _():
        @pl.when(step == 0)
        def _():
            total_ref[...] = resid_ref[...]

        @pl.when(step < turn)
        def _():
            total_ref[...] += mm(ao_ref[...], do_ref[...])

        @pl.when(step >= turn)
        def _():
            total_ref[...] += mm(ax_ref[...], dx_ref[...])

        @pl.when(step == pl.num_programs(0) - 1)
        def _():
            for c in range(books):
                for z in range(planes):
                    first = (c * planes + z) * half
                    out_ref[z, c] = total_ref[first : first + half, :].astype(bf)


def fall_call(at, resid, act_own, act_oth, down_own, down_oth, planes, books, chunk=1024):
    rows, width = resid.shape
    turn = down_own.shape[0] // chunk
    first = lambda i, s: jnp.minimum(i, turn - 1) * s[0]
    later = lambda i, s: jnp.maximum(i - turn, 0) * s[0]
    col = lambda f: pl.BlockSpec((rows, chunk), lambda i, s: (0, f(i, s)))
    row = lambda f: pl.BlockSpec((chunk, width), lambda i, s: (f(i, s), 0))
    shape = (planes, books, rows // planes // books, width)
    return pl.pallas_call(
        fall_kernel,
        grid_spec=pltpu.PrefetchScalarGridSpec(
            num_scalar_prefetch=1,
            grid=(2 * turn,),
            in_specs=[pl.BlockSpec((rows, width), lambda i, s: (0, 0), pipeline_mode=pl.Buffered(1)), col(first), col(later), row(first), row(later)],
            out_specs=pl.BlockSpec(shape, lambda i, s: (0, 0, 0, 0)),
            scratch_shapes=[pltpu.VMEM((rows, width), f32)],
        ),
        out_shape=jax.ShapeDtypeStruct(shape, bf),
        compiler_params=pltpu.CompilerParams(vmem_limit_bytes=60 * 1024 * 1024),
        cost_estimate=lasting(0.01),
        name="local_output",
    )(at, resid, act_own, act_oth, down_own, down_oth)


def table_kernel(at_ref, code_ref, code_in_ref, own_ref, got_ref, low_ref, high_ref, total_ref):
    entries = total_ref.shape[0]
    slots = lax.broadcasted_iota(jnp.int32, (entries, code_ref.shape[2]), 0)
    piece = low_ref.shape[3]

    @pl.when(at_ref[0] == 1)
    def _():
        hot = (slots == code_ref[0]).astype(f32).astype(bf)
        hot_in = (slots == code_in_ref[0]).astype(f32).astype(bf)
        total_ref[...] = mm(hot, own_ref[0]) + mm(hot_in, got_ref[0])
        for jz in range(4):
            for jy in range(2):
                place = (at_ref[1] ^ jz) * 2 + (at_ref[2] ^ jy)
                spot = (jz % 2) * 2 + jz // 2
                for ref, base in ((low_ref, 0), (high_ref, entries // 2)):
                    rows = pl.ds(pl.multiple_of(base + place * piece, piece), piece)
                    ref[jy, spot, 0] = total_ref[rows, :].astype(bf)


def table_call(at, codes, codes_in, own, got, entries):
    books, rows = codes.shape
    width = own.shape[2]
    line = pl.BlockSpec((1, 1, rows), lambda c, s: (c, 0, 0))
    block = pl.BlockSpec((1, rows, width), lambda c, s: (c, 0, 0))
    shape = (2, 4, books, entries // 16, width)
    out = pl.BlockSpec((2, 4, 1, entries // 16, width), lambda c, s: (0, 0, c, 0, 0))
    return pl.pallas_call(
        table_kernel,
        grid_spec=pltpu.PrefetchScalarGridSpec(
            num_scalar_prefetch=1,
            grid=(books,),
            in_specs=[line, line, block, block],
            out_specs=(out, out),
            scratch_shapes=[pltpu.VMEM((entries, width), f32)],
        ),
        out_shape=(jax.ShapeDtypeStruct(shape, bf),) * 2,
        compiler_params=pltpu.CompilerParams(vmem_limit_bytes=60 * 1024 * 1024),
        cost_estimate=lasting(4),
        name="table_gradient",
    )(at, codes[:, None, :], codes_in[:, None, :], own, got)


def prepare_kernel(at_ref, code_ref, cot_ref, do_ref, dx_ref, table_ref, look_ref, po_ref, px_ref):
    step = pl.program_id(0)
    turn = pl.num_programs(0) // 2
    books, rows, chunk = po_ref.shape

    @pl.when(at_ref[0] == 1)
    def _():
        @pl.when(step < look_ref.shape[0])
        def _():
            slots = lax.broadcasted_iota(jnp.int32, (rows, table_ref.shape[1]), 1)
            hot = (slots == code_ref[jnp.minimum(step, look_ref.shape[0] - 1)]).astype(f32).astype(bf)
            look_ref[jnp.minimum(step, look_ref.shape[0] - 1)] = mm(hot, table_ref[0]).astype(bf)

        @pl.when(step < turn)
        def _():
            po_ref[...] = mm_nt(cot_ref[...], do_ref[...]).astype(bf).reshape(books, rows, chunk)

        @pl.when(step >= turn)
        def _():
            px_ref[...] = mm_nt(cot_ref[...], dx_ref[...]).astype(bf).reshape(books, rows, chunk)


def prepare_call(at, codes, cot, down_own, down_oth, table, chunk=512):
    books, rows = codes.shape
    width = cot.shape[1]
    hidden = down_own.shape[0]
    turn = hidden // chunk
    first = lambda i, s: jnp.minimum(i, turn - 1) * s[0]
    later = lambda i, s: jnp.maximum(i - turn, 0) * s[0]
    down = lambda f: pl.BlockSpec((chunk, width), lambda i, s: (f(i, s), 0))
    out = lambda f: pl.BlockSpec((books, rows, chunk), lambda i, s: (0, 0, f(i, s)))
    sd = jax.ShapeDtypeStruct
    return pl.pallas_call(
        prepare_kernel,
        grid_spec=pltpu.PrefetchScalarGridSpec(
            num_scalar_prefetch=1,
            grid=(2 * turn,),
            in_specs=[
                pl.BlockSpec((books, rows, 1), lambda i, s: (0, 0, 0)),
                pl.BlockSpec(cot.shape, lambda i, s: (0, 0)),
                down(first),
                down(later),
                pl.BlockSpec((1,) + table.shape[1:], lambda i, s: (jnp.minimum(i, books - 1) * s[0], 0, 0)),
            ],
            out_specs=(pl.BlockSpec((books, rows, width), lambda i, s: (0, 0, 0)), out(first), out(later)),
        ),
        out_shape=(sd((books, rows, width), bf), sd((books, rows, hidden), bf), sd((books, rows, hidden), bf)),
        compiler_params=pltpu.CompilerParams(vmem_limit_bytes=60 * 1024 * 1024),
        cost_estimate=lasting(5),
        name="local_prepare",
    )(at, codes[:, :, None], cot, down_own, down_oth, table)


def fence(*groups):
    return lax.optimization_barrier(groups)


def body(frames, codes, lengths, gains, w_qkv, w_out, w_up, w_down, table, cotangent):
    batches, share, width = frames.shape
    members = lax.axis_size("dp") // batches
    if (
        lax.axis_size("section") != 2
        or lax.axis_size("tensor") != 2
        or members != 2
        or lax.axis_size("dp") != 2 * batches
        or batches & (batches - 1)
        or share % 32
        or table.shape[1] != width
    ):
        return plain_body(frames, codes, lengths, gains, w_qkv, w_out, w_up, w_down, table, cotangent)
    place, core = lax.axis_index("dp"), lax.axis_index("tensor")
    plane, side = place // members, place % members
    on_first = lax.axis_index("section") == 0
    half = share // 2
    rows = batches * half
    count = 2 * batches
    at = jnp.stack([lax.axis_index("section"), plane, side]).astype(jnp.int32)

    everywhere, first, second = (0, 1), (0,), (1,)

    def linked(a, flip_place, flip_core, sections=everywhere):
        pairs = [
            ((z * count + i) * 2 + j, (z * count + (i ^ flip_place)) * 2 + (j ^ flip_core))
            for z in sections
            for i in range(count)
            for j in range(2)
        ]
        return lax.ppermute(a, ("section", "dp", "tensor"), pairs)

    def core_swap(a, sections=everywhere):
        return linked(a, 0, 1, sections)

    def side_swap(a, sections=everywhere):
        return linked(a, 1, 0, sections)

    def both_swap(a, sections=everywhere):
        return linked(a, 1, 1, sections)

    def to_local(a):
        return lax.ppermute(a, "section", [(0, 1)])

    def to_global(a):
        return lax.ppermute(a, "section", [(1, 0)])

    def planes_in(a, sections=everywhere):
        pieces = [lax.dynamic_slice_in_dim(a, plane ^ k, 1, 0) for k in range(batches)]
        return jnp.concatenate([pieces[0], *(linked(pieces[k], 2 * k, 0, sections) for k in range(1, batches))], 0)

    def planes_out(a, sections=everywhere):
        got = [a[:1], *(linked(a[k : k + 1], 2 * k, 0, sections) for k in range(1, batches))]
        out = jnp.zeros_like(a)
        for k in range(batches):
            out = lax.dynamic_update_slice_in_dim(out, got[k], plane ^ k, 0)
        return out

    def core_half(a, axis):
        return lax.dynamic_slice_in_dim(a, core * half, half, axis)

    def join_cores(a, axis):
        other = core_swap(a)
        return jnp.where(core == 0, jnp.concatenate([a, other], axis), jnp.concatenate([other, a], axis))

    def quarter(a, axis):
        size = a.shape[axis] // 2
        return lax.dynamic_slice_in_dim(a, side * size, size, axis)

    def by_side(mine, theirs, axis):
        return jnp.where(side == 0, jnp.concatenate([mine, theirs], axis), jnp.concatenate([theirs, mine], axis))

    x_own = planes_in(core_half(frames, 1), first).reshape(rows, width)
    x_side = side_swap(x_own, first)
    x_core, x_both = core_swap(x_own), core_swap(x_side)

    def positions(jt, js):
        base = ((jnp.arange(batches)[:, None] ^ plane) * 2 + (side ^ js)) * share + (core ^ jt) * half
        return (base + jnp.arange(half)[None, :]).reshape(-1)

    pos = jnp.concatenate([positions(0, 0), positions(0, 1), positions(1, 0), positions(1, 1)]).astype(jnp.int32)
    doc_ends = jnp.cumsum(lax.dynamic_index_in_dim(lengths, plane, 0, keepdims=False))
    doc = doc_index(pos, doc_ends)
    qid = jnp.stack([pos, doc], 1)
    kid = jnp.stack([pos, jnp.where(pos < doc_ends[-1], doc, -1)], 0)

    cot = planes_in(core_half(cotangent.transpose(0, 2, 1, 3), 2), second)
    codes_own = planes_in(core_half(codes.transpose(0, 2, 1), 2), second)
    (x_core, x_both, qid, kid, cot, codes_own), (w_qkv, w_out, w_up, w_down) = fence(
        (x_core, x_both, qid, kid, cot, codes_own), (w_qkv, w_out, w_up, w_down)
    )
    gains_here = gains[0]
    proj_own = w_qkv[0].transpose(1, 0, 2)
    out_own, up_own, down_own = w_out[0], w_up[0], w_down[0]
    out_oth, up_oth, down_oth = (core_swap(w) for w in (out_own, up_own, down_own))
    proj_oth = core_swap(proj_own)

    normed_all, q, k, v, near, off = attend_call(at, (x_own, x_side, x_core, x_both), gains_here, proj_own, qid, kid)
    proj_mine = quarter(proj_own, 2)
    off_got = side_swap(off, first)
    from_core = core_swap(jnp.concatenate([near[1:], off_got[1:]], 0))
    attended = jnp.stack([near[0], off[0], near[1], off[1]]).reshape(4 * rows, -1)
    x32 = x_own.astype(f32)
    resid, mid, act_own, act_oth, slope_own, slope_oth, global_low = front_call(
        at, x_own, near, off_got, from_core, gains_here, out_own, out_oth, up_own, up_oth, down_own, down_oth
    )
    mid_in, act_in = core_swap(mid), core_swap(act_oth)

    arrived = to_local(global_low)
    cot = cot.transpose(1, 0, 2, 3).reshape(CODEBOOKS, rows, width)
    codes_own = codes_own.transpose(1, 0, 2).reshape(CODEBOOKS, rows)
    slots = jnp.arange(table.shape[1], dtype=jnp.int32)
    cot_rows = cot.reshape(-1, width)
    cot_in, codes_oth = core_swap(cot_rows), core_swap(codes_own)

    looked_up, pull_own, pull_oth = prepare_call(at, codes_own, cot_rows, down_own, down_oth, table)
    (
        l_resid, l_act, l_rise, l_pack, l_act_oth, l_send, l_grad, l_frame, l_gains,
    ) = local_call(
        at, arrived, looked_up, cot, pull_own, pull_oth, gains_here, proj_own, proj_oth, out_own, out_oth, up_own, up_oth
    )
    global_moved = planes_out(global_low.reshape(batches, half, width), first)
    (l_frame, l_grad, l_act_oth, global_moved), (l_send,) = fence((l_frame, l_grad, l_act_oth, global_moved), (l_send,))
    grad_low = to_global(l_frame.astype(bf))

    flat = lambda a: a.reshape(-1, a.shape[-1])
    hidden = up_own.shape[1]

    def swap(a, bit, sections=everywhere):
        return linked(a, 1 << bit, 0, sections)

    def meet(mine, got):
        return (mine.astype(f32) + got.astype(f32)).astype(bf)

    def cols_of(a, which):
        return lax.dynamic_slice_in_dim(a, which * (width // 2), width // 2, 2)

    l_grad_in, l_act_in = core_swap(cols_of(l_grad, 1 - core)), core_swap(flat(l_act_oth), second)
    table_low, table_high = table_call(at, codes_own, codes_oth, cols_of(l_grad, core), l_grad_in, table.shape[1])
    l_down_mine, l_down_theirs = weight_call(
        at, 1, (cot_rows, cot_in, flat(l_act), l_act_in), (0, 0, 0, 0), True, "local_down_gradient", 4, width, hidden
    )
    (table_low, table_high, grad_low, l_down_theirs), (l_send,) = fence(
        (table_low, table_high, grad_low, l_down_theirs), (l_send,)
    )
    l_got = core_swap(flat(l_send), second)

    grad_in_low = core_swap(grad_low)
    rise_own, rise_oth, grad_resid, low_own, gain_mid = back_call(
        at, grad_low, resid, gains_here, slope_own, slope_oth, up_own, up_oth, down_own, down_oth
    )
    rise_in = core_swap(rise_oth)
    local_low = fall_call(at, flat(l_resid), flat(l_act), flat(l_act_oth), down_own, down_oth, batches, CODEBOOKS)
    (low_own, grad_in_low, local_low), (l_got,) = fence((low_own, grad_in_low, local_low), (l_got,))
    local_moved = planes_out(local_low, second)
    low_side = side_swap(low_own, first)
    down_mine, down_theirs = weight_call(
        at, 0, (grad_low, grad_in_low, act_own, act_in), (0, 0, 0, 0), True, "down_gradient", 8, width, hidden
    )
    l_up_mine, l_up_theirs = weight_call(
        at, 1, (flat(l_send), l_got, flat(l_rise), l_got),
        (hidden // width, hidden // width, 0, 0), False, "local_up_gradient", 4, width, hidden,
    )
    down_theirs = jnp.where(on_first, down_theirs, l_down_theirs)
    (down_theirs, l_up_theirs, local_moved), (rise_in, table_low) = fence(
        (down_theirs, l_up_theirs, local_moved), (rise_in, table_low)
    )
    table_moved = to_global(table_low)
    down_got = swap(down_theirs, 1)
    up_mine, up_theirs = weight_call(
        at, 0, (mid, mid_in, rise_own, rise_in), (0, 0, 0, 0), False, "up_gradient", 8, width, hidden
    )
    up_theirs = jnp.where(on_first, up_theirs, l_up_theirs)
    (up_theirs, low_side), (l_pack, l_act) = fence((up_theirs, low_side), (l_pack, l_act))
    up_got = swap(up_theirs, 0)
    low_at = hidden // width + 1
    l_rest_mine, l_rest_theirs = rest_call(
        at, 1, ((flat(l_send), low_at), (l_got, low_at)), ((flat(l_send), low_at + 1), (l_got, low_at + 1)),
        ((l_pack.reshape(4, CODEBOOKS * rows, -1), 0), (l_got, (hidden + 3 * width) // l_pack.shape[-1])),
        "local_rest_gradient", 0.01, width,
    )
    (l_rest_theirs, low_side), = fence((l_rest_theirs, low_side))
    low_all = jnp.concatenate([low_own, low_side, core_swap(low_own), core_swap(low_side)], 0)
    grad_att = against_rows(low_all, quarter(out_own, 0)).astype(bf)
    grad_packs = attend_back_call(at, q, k, v, grad_att, qid, kid, rows)
    rest_mine, rest_theirs = rest_call(
        at, 0, ((low_all, 0),), ((normed_all, 0),), ((jnp.stack([attended, *grad_packs]), 0),), "rest_gradient", 0.01, width
    )
    flip = side == 0
    empty = jnp.zeros_like(rest_mine)

    def spread_out(a):
        return jnp.concatenate([jnp.where(flip, a, empty), jnp.where(flip, empty, a)], 2)

    rest_theirs = jnp.where(on_first, spread_out(rest_theirs), l_rest_theirs)
    (rest_theirs, down_got, up_got), (grad_packs, rest_mine, local_moved) = fence(
        (rest_theirs, down_got, up_got), (grad_packs, rest_mine, local_moved)
    )
    rest_got = swap(rest_theirs, 0)
    rest_mine = jnp.where(on_first, spread_out(rest_mine), l_rest_mine)
    up_now = meet(jnp.where(on_first, up_mine, l_up_mine), up_got)
    up_got = swap(up_now[2:], 1)
    down_now = meet(jnp.where(on_first, down_mine, l_down_mine), down_got)
    down_got = swap(down_now[1], 2)
    part_normed = sum(against_rows(g, proj_mine[j]) for j, g in enumerate(grad_packs))
    pair = part_normed[: 2 * rows] + core_swap(part_normed[2 * rows :].astype(bf)).astype(f32)
    pair_side = side_swap(pair[rows:].astype(bf), first)
    local_sent = to_global(local_moved)
    (rest_got, rest_mine, up_got, down_got, pair_side, table_moved), = fence(
        (rest_got, rest_mine, up_got, down_got, pair_side, table_moved)
    )
    rest_now = meet(rest_mine, rest_got)
    (rest_now,), (up_got, down_got, pair_side) = fence((rest_now,), (up_got, down_got, pair_side))
    rest_got = swap(rest_now[2:], 1)
    down_now = meet(down_now[0], down_got)
    down_got = swap(down_now[1], 0)
    up_now = meet(up_now[:2], up_got)
    up_got = swap(up_now[1], 2)
    grad_normed = pair[:rows] + pair_side.astype(f32)
    back_in, gain_in = rms_back(x32, gains_here[0], grad_normed)
    grad_frames = grad_resid + back_in
    gain_sum = jnp.where(on_first, jnp.concatenate([gain_in[None], gain_mid]), l_gains)
    gain_sum = (gain_sum + core_swap(gain_sum)).reshape(2, batches, 2, -1)
    piece = width // count
    gain_rows = jnp.concatenate(
        [
            lax.dynamic_slice(gain_sum, (0, plane ^ (2 * j + i), side ^ y, 0), (2, 1, 1, piece)).reshape(1, -1)
            for y in range(2)
            for i in range(2)
            for j in range(2)
        ]
    ).reshape(2, batches, 2 * piece)
    gain_rows = jnp.pad(gain_rows.astype(bf)[:, :, None, :], ((0, 0), (0, 0), (0, 15), (0, width // 2 - 2 * piece)))
    table_now = jnp.where(on_first, table_moved, table_high).reshape(2, batches, -1, width // 2)
    table_now = jnp.concatenate([table_now, gain_rows], 2)
    table_got = swap(table_now[1], 0)
    inner = jnp.where(on_first, grad_frames, l_frame).astype(bf).reshape(2, 2, half, width)
    inner_got = swap(inner[1], 2)
    (rest_got, up_got, down_got, table_got, local_sent, inner_got), (global_moved,) = fence(
        (rest_got, up_got, down_got, table_got, local_sent, inner_got), (global_moved,)
    )
    rest_now = meet(rest_now[:2], rest_got)
    rest_got = swap(rest_now[1], 2)
    table_now = meet(table_now[0], table_got)
    table_got = swap(table_now[2:], 1)
    near_got = swap(jnp.stack([inner[0, 1], inner_got[1]]), 1)
    global_sent = to_local(global_moved)
    local_out = join_cores(jnp.where(on_first, local_sent, local_moved), 2).transpose(0, 2, 1, 3)
    (near_got, rest_got, global_sent, local_out), = fence((near_got, rest_got, global_sent, local_out))
    blocks = (inner[0, 0], near_got[0], inner_got[0], near_got[1])
    inner = jnp.zeros((batches, half, width), bf)
    for k, block in enumerate(blocks):
        inner = lax.dynamic_update_slice_in_dim(inner, block[None], plane ^ k, 0)
    global_out = join_cores(jnp.where(on_first, global_moved, global_sent), 1)
    down_share = down_now[0].astype(f32) + down_got.astype(f32)
    up_share = up_now[0].astype(f32) + up_got.astype(f32)
    table_now = meet(table_now[:2], table_got)
    table_got = swap(table_now[1], 2)
    input_grads = join_cores(inner, 1).astype(f32)[None]
    mix = out_own.shape[0]
    (local_out, global_out, up_share, down_share), (rest_got, table_got) = fence(
        (local_out, global_out, up_share, down_share.T), (rest_got, table_got)
    )
    rest_share = rest_now[0].astype(f32) + rest_got.astype(f32)
    table_now = table_now[0].astype(f32) + table_got.astype(f32)
    gain_share = table_now[-16, : 2 * piece].reshape(2, piece)
    grad_table = join_cores(table_now[:-16].reshape(CODEBOOKS, -1, width // 2).astype(bf), 2).astype(f32)

    mix = out_own.shape[0]
    proj_share = rest_share[1:].transpose(2, 0, 1, 3).reshape(piece, 3, mix)
    return (
        global_out,
        local_out,
        input_grads,
        proj_share[None],
        rest_share[0].transpose(0, 2, 1).reshape(mix, piece)[None],
        up_share[None],
        down_share[None],
        gain_share[None],
        grad_table,
    )


def solution(mesh):
    in_specs = (
        P(None, "dp", None),
        P(None, "dp", None),
        P(),
        P("section", None, None),
        P("section", None, None, "tensor"),
        P("section", "tensor", None),
        P("section", None, "tensor"),
        P("section", "tensor", None),
        P(),
        P(None, "dp", None, None),
    )
    out_specs = (
        P(None, "dp", None),
        P(None, "dp", None, None),
        P("section", None, "dp", None),
        P("section", "dp", None, "tensor"),
        P("section", "tensor", "dp"),
        P("section", "dp", "tensor"),
        P("section", "tensor", "dp"),
        P("section", None, "dp"),
        P(None, ("section", "dp"), None),
    )
    return jax.shard_map(body, mesh=mesh, in_specs=in_specs, out_specs=out_specs, check_vma=False)
```

```python
import functools

import jax
import jax.numpy as jnp
from jax import lax
from jax.experimental import pallas as pl
from jax.experimental.pallas import tpu as pltpu
from jax.sharding import PartitionSpec as P

HEAD = 64
CODEBOOKS = 3


eps = 1e-05
far = -1e30


def from_behind(block, axis, distance):
    devices = range(lax.axis_size(axis))
    route = [(i - distance, i) for i in devices if i - distance in devices]
    return lax.ppermute(block, axis, route)


def rms_scale(values):
    return lax.rsqrt(jnp.mean(values * values, axis=-1, keepdims=True) + eps)


def rms_back(values, gain_row, grad_normed):
    factor = rms_scale(values)
    normal = values * factor
    grad_unit = grad_normed * gain_row
    grad_values = factor * (
        grad_unit - normal * jnp.mean(grad_unit * normal, axis=-1, keepdims=True)
    )
    return (grad_values, jnp.sum(grad_normed * normal, axis=0))


def head_total(partial_sum):
    return lax.psum(partial_sum, "tensor")


def matmul(left, right):
    return jnp.dot(left, right, preferred_element_type=jnp.float32)


def across_rows(left, right):
    return lax.dot_general(
        left, right, (((0,), (0,)), ((), ())), preferred_element_type=jnp.float32
    )


def against_rows(left, right):
    return lax.dot_general(
        left, right, (((1,), (1,)), ((), ())), preferred_element_type=jnp.float32
    )


def smooth_gate(values):
    return jax.nn.gelu(values, approximate=True)


def doc_index(positions, doc_ends):
    return jnp.sum((positions[:, None] >= doc_ends[None, :]).astype(jnp.int32), axis=1)


def allowed_mask(query_pos, key_pos, doc_ends):
    same_doc = doc_index(query_pos, doc_ends)[:, None] == doc_index(key_pos, doc_ends)[None, :]
    earlier = key_pos[None, :] <= query_pos[:, None]
    live = (key_pos < doc_ends[-1])[None, :]
    return same_doc & earlier & live | (key_pos[None, :] == query_pos[:, None])


def masked_softmax(scores, mask, factor):
    logits = jnp.where(mask, scores * factor, far)
    top = jnp.max(logits, axis=-1, keepdims=True)
    weights = jnp.exp(logits - top)
    mass = jnp.sum(weights, axis=-1, keepdims=True)
    return (weights / mass, (top + jnp.log(mass))[..., 0])


def frame_forward(packed, query_pos, doc_ends, head_count):
    row_count = packed.shape[0]
    width = packed.shape[1] // 3
    factor = HEAD ** (-0.5)
    parts = packed.reshape(row_count, 3, width)
    all_keys, all_values = (
        lax.all_gather(parts[:, 1], "dp", axis=0, tiled=True),
        lax.all_gather(parts[:, 2], "dp", axis=0, tiled=True),
    )
    key_count = all_keys.shape[0]
    key_pos = jnp.arange(key_count, dtype=jnp.int32)
    mask = allowed_mask(query_pos, key_pos, doc_ends)
    queries = parts[:, 0].reshape(row_count, head_count, -1)
    scores = jnp.einsum(
        "qhe,khe->hqk",
        queries,
        all_keys.reshape(key_count, head_count, -1),
        preferred_element_type=jnp.float32,
    )
    probs, log_mass = masked_softmax(scores, mask[None], factor)
    attended = jnp.einsum(
        "hqk,khe->qhe",
        probs.astype(jnp.bfloat16),
        all_values.reshape(key_count, head_count, -1),
        preferred_element_type=jnp.float32,
    )
    return (attended.reshape(row_count, width), log_mass)


def frame_backward(packed, grad_att, log_mass, query_pos, doc_ends, head_count):
    row_count = packed.shape[0]
    width = packed.shape[1] // 3
    factor = HEAD ** (-0.5)
    parts = packed.reshape(row_count, 3, width)
    all_keys, all_values = (
        lax.all_gather(parts[:, 1], "dp", axis=0, tiled=True),
        lax.all_gather(parts[:, 2], "dp", axis=0, tiled=True),
    )
    key_count = all_keys.shape[0]
    key_pos = jnp.arange(key_count, dtype=jnp.int32)
    queries = parts[:, 0].reshape(row_count, head_count, -1)
    grad_heads = grad_att.reshape(row_count, head_count, -1)
    keys_heads = all_keys.reshape(key_count, head_count, -1)
    scores = jnp.einsum("qhe,khe->hqk", queries, keys_heads, preferred_element_type=jnp.float32)
    mask = allowed_mask(query_pos, key_pos, doc_ends)
    probs = jnp.exp(jnp.where(mask[None], scores * factor, far) - log_mass[:, :, None])
    grad_probs = jnp.einsum(
        "qhe,khe->hqk",
        grad_heads,
        all_values.reshape(key_count, head_count, -1),
        preferred_element_type=jnp.float32,
    )
    spread = jnp.sum(probs * grad_probs, axis=-1)
    grad_scores = (probs * (grad_probs - spread[:, :, None]) * factor).astype(jnp.bfloat16)
    grad_queries = jnp.einsum(
        "hqk,khe->qhe", grad_scores, keys_heads, preferred_element_type=jnp.float32
    ).reshape(row_count, width)
    keys_term = jnp.einsum(
        "hqk,qhe->khe", grad_scores, queries, preferred_element_type=jnp.float32
    ).reshape(key_count, width)
    values_term = jnp.einsum(
        "hqk,qhe->khe", probs.astype(jnp.bfloat16), grad_heads, preferred_element_type=jnp.float32
    ).reshape(key_count, width)
    grad_keys, grad_values = (
        lax.psum_scatter(keys_term, "dp", scatter_dimension=0, tiled=True),
        lax.psum_scatter(values_term, "dp", scatter_dimension=0, tiled=True),
    )
    return jnp.stack([grad_queries, grad_keys, grad_values], axis=1).reshape(row_count, 3 * width)


def codebook_forward(packed, head_count):
    row_count = packed.shape[0]
    width = packed.shape[1] // 3
    factor = HEAD ** (-0.5)
    parts = packed.reshape(row_count // CODEBOOKS, CODEBOOKS, 3, head_count, -1)
    scores = jnp.einsum(
        "nche,ndhe->nhcd", parts[:, :, 0], parts[:, :, 1], preferred_element_type=jnp.float32
    )
    order = jnp.arange(CODEBOOKS, dtype=jnp.int32)
    mask = order[None, :] <= order[:, None]
    probs, log_mass = masked_softmax(scores, mask, factor)
    attended = jnp.einsum(
        "nhcd,ndhe->nche",
        probs.astype(jnp.bfloat16),
        parts[:, :, 2],
        preferred_element_type=jnp.float32,
    )
    return (attended.reshape(row_count, width), probs)


def codebook_backward(packed, grad_att, probs, head_count):
    row_count = packed.shape[0]
    width = packed.shape[1] // 3
    factor = HEAD ** (-0.5)
    parts = packed.reshape(row_count // CODEBOOKS, CODEBOOKS, 3, head_count, -1)
    grad_heads = grad_att.reshape(row_count // CODEBOOKS, CODEBOOKS, head_count, -1)
    grad_probs = jnp.einsum(
        "nche,ndhe->nhcd", grad_heads, parts[:, :, 2], preferred_element_type=jnp.float32
    )
    spread = jnp.sum(probs * grad_probs, axis=-1, keepdims=True)
    grad_scores = (probs * (grad_probs - spread) * factor).astype(jnp.bfloat16)
    grad_queries = jnp.einsum(
        "nhcd,ndhe->nche", grad_scores, parts[:, :, 1], preferred_element_type=jnp.float32
    )
    grad_keys = jnp.einsum(
        "nhcd,nche->ndhe", grad_scores, parts[:, :, 0], preferred_element_type=jnp.float32
    )
    grad_values = jnp.einsum(
        "nhcd,nche->ndhe",
        probs.astype(jnp.bfloat16),
        grad_heads,
        preferred_element_type=jnp.float32,
    )
    return jnp.stack([grad_queries, grad_keys, grad_values], axis=2).reshape(row_count, 3 * width)


def layer_forward(inputs, gain_pair, layer_weights, attend):
    w_proj, w_mix, w_rise, w_fall = layer_weights
    normed = (inputs * rms_scale(inputs) * gain_pair[0]).astype(jnp.bfloat16)
    packed = matmul(normed, w_proj.reshape(w_proj.shape[0], -1)).astype(jnp.bfloat16)
    attended, saved = attend(packed)
    attended_low = attended.astype(jnp.bfloat16)
    resid = inputs + head_total(matmul(attended_low, w_mix))
    normed_mid = (resid * rms_scale(resid) * gain_pair[1]).astype(jnp.bfloat16)
    rise = matmul(normed_mid, w_rise)
    active = smooth_gate(rise).astype(jnp.bfloat16)
    result = resid + head_total(matmul(active, w_fall))
    return (result, (normed, packed, attended_low, saved, resid, normed_mid, rise, active))


def layer_backward(inputs, gain_pair, layer_weights, kept, grad_result, attend_back):
    w_proj, w_mix, w_rise, w_fall = layer_weights
    normed, packed, attended_low, saved, resid, normed_mid, rise, active = kept
    grad_fall_low = grad_result.astype(jnp.bfloat16)
    grad_fall_w = across_rows(active, grad_fall_low)
    grad_active = against_rows(grad_fall_low, w_fall)
    grad_rise = jax.vjp(smooth_gate, rise)[1](grad_active)[0].astype(jnp.bfloat16)
    grad_rise_w = across_rows(normed_mid, grad_rise)
    grad_mid = head_total(against_rows(grad_rise, w_rise))
    back_mid, gain_mid = rms_back(resid, gain_pair[1], grad_mid)
    grad_resid = grad_result + back_mid
    resid_low = grad_resid.astype(jnp.bfloat16)
    grad_mix_w = across_rows(attended_low, resid_low)
    grad_att = against_rows(resid_low, w_mix).astype(jnp.bfloat16)
    grad_packed = attend_back(packed, grad_att, saved).astype(jnp.bfloat16)
    flat_proj = w_proj.reshape(w_proj.shape[0], -1)
    grad_proj_w = across_rows(normed, grad_packed).reshape(w_proj.shape)
    grad_normed = head_total(against_rows(grad_packed, flat_proj))
    back_in, gain_in = rms_back(inputs, gain_pair[0], grad_normed)
    return (
        grad_resid + back_in,
        (grad_proj_w, grad_mix_w, grad_rise_w, grad_fall_w, jnp.stack([gain_in, gain_mid])),
    )


def plain_body(frames, codes, lengths, gains, w_qkv, w_out, w_up, w_down, table, cotangent):
    on_first = lax.axis_index("section") == 0
    head_count = w_qkv.shape[3] // HEAD
    layer_weights = (w_qkv[0], w_out[0], w_up[0], w_down[0])
    gains_here = gains[0]
    frame_count = frames.shape[1]
    query_pos = lax.axis_index("dp") * frame_count + jnp.arange(frame_count, dtype=jnp.int32)
    zero_grads = (
        jnp.zeros(w_qkv.shape[1:], jnp.float32),
        jnp.zeros(w_out.shape[1:], jnp.float32),
        jnp.zeros(w_up.shape[1:], jnp.float32),
        jnp.zeros(w_down.shape[1:], jnp.float32),
        jnp.zeros(gains.shape[1:], jnp.float32),
    )

    def global_forward_rows(frame_rows, slot_lengths):
        doc_ends = jnp.cumsum(slot_lengths)
        return (
            doc_ends,
            layer_forward(
                frame_rows.astype(jnp.float32),
                gains_here,
                layer_weights,
                lambda packed: frame_forward(packed, query_pos, doc_ends, head_count),
            ),
        )

    def global_step(carry, inputs):
        doc_ends, (result, kept) = global_forward_rows(inputs[0], inputs[1])
        return (carry, result.astype(jnp.bfloat16))

    global_low = lax.scan(global_step, jnp.zeros((), jnp.int32), (frames, lengths))[1]
    arrived = from_behind(global_low, "section", 1)
    books = jnp.arange(CODEBOOKS, dtype=jnp.int32)
    looked_up = table[books[None, None, :], codes]
    local_in = arrived.astype(jnp.float32)[:, :, None, :] + looked_up.astype(jnp.float32)
    local_rows = local_in.reshape(-1, local_in.shape[-1])
    local_result, local_kept = layer_forward(
        local_rows, gains_here, layer_weights, lambda packed: codebook_forward(packed, head_count)
    )
    grad_rows, local_grads = layer_backward(
        local_rows,
        gains_here,
        layer_weights,
        local_kept,
        cotangent.astype(jnp.float32).reshape(local_rows.shape),
        lambda packed, grad_att, saved: codebook_backward(packed, grad_att, saved, head_count),
    )
    grad_frame = jnp.sum(grad_rows.reshape(local_in.shape), axis=2)
    table_slots = (books[None, None, :] * table.shape[1] + codes).reshape(-1)
    table_term = jax.ops.segment_sum(
        grad_rows, table_slots, num_segments=table.shape[0] * table.shape[1]
    ).reshape(table.shape)
    local_low = local_result.astype(jnp.bfloat16).reshape(cotangent.shape)
    table_part = jnp.where(on_first, jnp.zeros(table.shape, jnp.float32), table_term)
    grad_frame = jnp.where(on_first, jnp.zeros(frames.shape, jnp.float32), grad_frame)
    grad_table = lax.psum_scatter(table_part, ("section", "dp"), scatter_dimension=1, tiled=True)
    grad_back, local_copy = from_behind((grad_frame.astype(jnp.bfloat16), local_low), "section", -1)

    def global_back(totals, inputs):
        frame_rows, slot_lengths, grad_low = inputs
        doc_ends, (result, kept) = global_forward_rows(frame_rows, slot_lengths)
        grad_in, grads = layer_backward(
            frame_rows.astype(jnp.float32),
            gains_here,
            layer_weights,
            kept,
            grad_low.astype(jnp.float32),
            lambda packed, grad_att, saved: frame_backward(
                packed, grad_att, saved, query_pos, doc_ends, head_count
            ),
        )
        return (jax.tree.map(jnp.add, totals, grads), grad_in)

    global_grads, grad_frames = lax.scan(global_back, zero_grads, (frames, lengths, grad_back))

    def pick(global_part, local_part):
        return jnp.where(on_first, global_part, local_part)

    proj_sum, mix_sum, rise_sum, fall_sum, gain_sum = jax.tree.map(pick, global_grads, local_grads)
    proj_share, mix_share, rise_share, fall_share, gain_share = (
        lax.psum_scatter(proj_sum, "dp", scatter_dimension=0, tiled=True),
        lax.psum_scatter(mix_sum, "dp", scatter_dimension=1, tiled=True),
        lax.psum_scatter(rise_sum, "dp", scatter_dimension=0, tiled=True),
        lax.psum_scatter(fall_sum, "dp", scatter_dimension=1, tiled=True),
        lax.psum_scatter(gain_sum, "dp", scatter_dimension=1, tiled=True),
    )
    global_out = jnp.where(on_first, global_low, arrived)
    local_out = jnp.where(on_first, local_copy, local_low)
    input_grads = jnp.where(on_first, grad_frames, grad_frame)[None]
    return (
        global_out,
        local_out,
        input_grads,
        proj_share[None],
        mix_share[None],
        rise_share[None],
        fall_share[None],
        gain_share[None],
        grad_table,
    )


def lasting(us):
    return pl.CostEstimate(flops=int(us * 1.1e9), bytes_accessed=int(us * 1e6), transcendentals=0)

f32=jnp.float32; bf=jnp.bfloat16

def mm(a,b): return jnp.dot(a,b,preferred_element_type=f32)
def mm_nt(a,b): return lax.dot_general(a,b,(((1,),(1,)),((),())),preferred_element_type=f32)

def gelu_both(v):
    c0 = 0.7978845608028654
    c1 = c0 * 0.044715
    sq = v * v
    half = 0.5 + 0.5 * jnp.tanh(v * (c0 + c1 * sq))
    act = v * half
    return act, half + act * (1.0 - half) * (2.0 * c0 + 6.0 * c1 * sq)


def local_kernel(g_ref, emb_ref, cot_ref, gao_ref, gax_ref, gains_ref, e_ref, et_ref,
                 pqo, pqx, woo, wox, wuo, wux,
                 resid_o, acto_o, griso_o, gpo_o, actx_o, send_o, dx_o, gframe_o, gg_o,
                 q_s, k_s, v_s, p_s, gp_s, prod_s, wide_s, r_s, gm_s, gatt_s):
    F=g_ref.shape[0]; R=3*F; D=g_ref.shape[1]; H2=D//2
    W=acto_o.shape[2]
    grisx_o=send_o.at[:,:,0:W]
    mid_o,glow_o,normed_o=(send_o.at[:,:,W+j*D:W+(j+1)*D] for j in range(3))
    gpx_o=[send_o.at[:,:,W+3*D+j*H2:W+3*D+(j+1)*H2] for j in range(4)]
    step=pl.program_id(0)
    gain0=gains_ref[0:1,:]; gain1=gains_ref[1:2,:]
    g=g_ref[...].astype(f32)
    scr=(q_s,k_s,v_s)
    r0s=[]
    for c in range(3):
        x=g+emb_ref[c].astype(f32)
        r0=lax.rsqrt(jnp.mean(x*x,axis=-1,keepdims=True)+eps)
        r0s.append(r0)
        normed_o[c]=(x*r0*gain0).astype(bf)
    normed=normed_o[...].reshape(R,D)
    for j in range(3):
        scr[j][:,0:H2]=mm(normed,pqo[j]).astype(bf)
        scr[j][:,H2:D]=mm(normed,pqx[j]).astype(bf)
    pairs=[(c,c2) for c in range(3) for c2 in range(c+1)]
    rows=lambda ref,c: ref[c*F:(c+1)*F,:]
    for n,(c,c2) in enumerate(pairs):
        prod_s[n*F:(n+1)*F,:]=(rows(q_s,c).astype(f32)*rows(k_s,c2).astype(f32)).astype(bf)
    p_s[...]=mm(prod_s[...],e_ref[...])*0.125
    for c in range(3):
        own=[n for n,pr in enumerate(pairs) if pr[0]==c]
        ss=[rows(p_s,n) for n in own]
        top=functools.reduce(jnp.maximum,ss)
        ws=[jnp.exp(s-top) for s in ss]
        inv=1.0/functools.reduce(jnp.add,ws)
        for n,w in zip(own,ws): p_s[n*F:(n+1)*F,:]=w*inv
    wide_s[...]=mm(p_s[...].astype(bf),et_ref[...]).astype(bf)
    for c in range(3):
        acc=functools.reduce(jnp.add,[rows(wide_s,n).astype(f32)*rows(v_s,pr[1]).astype(f32) for n,pr in enumerate(pairs) if pr[0]==c])
        att=acc.astype(bf)
        gpo_o[0,c]=att[:,0:H2]; gpx_o[0][c]=att[:,H2:D]
    xs=(g_ref[...].astype(f32)[None]+emb_ref[...].astype(f32)).reshape(R,D)
    resid=xs+mm(gpo_o[0].reshape(R,H2),woo[...])+mm(gpx_o[0][...].reshape(R,H2),wox[...])
    r1=lax.rsqrt(jnp.mean(resid*resid,axis=-1,keepdims=True)+eps)
    resid_o[...]=resid.reshape(3,F,D)
    nm=(resid*r1*gain1).astype(bf)
    mid_o[...]=nm.reshape(3,F,D)
    ch=512
    gm=None
    for (wu,act_o,gris_o,ga_ref) in ((wuo,acto_o,griso_o,gao_ref),(wux,actx_o,grisx_o,gax_ref)):
        for j in range(wu.shape[1]//ch):
            sl=slice(j*ch,(j+1)*ch)
            w=wu[:,sl]
            act,gr=gelu_both(mm(nm,w))
            act_o[:,:,sl]=act.astype(bf).reshape(3,F,ch)
            gl=(ga_ref[:,:,sl].reshape(R,ch).astype(f32)*gr).astype(bf)
            gris_o[:,:,sl]=gl.reshape(3,F,ch)
            t=mm_nt(gl,w)
            if gm is None:
                gm_s[...]=t; gm=1
            else:
                gm_s[...]+=t
    gmid=gm_s[...]
    n1=resid_o[...].reshape(R,D)*r1
    u=gmid*gain1
    gres=cot_ref[...].reshape(R,D).astype(f32)+r1*(u-n1*jnp.mean(u*n1,axis=-1,keepdims=True))
    gsum1=jnp.sum(gmid*n1,axis=0,keepdims=True)
    r_s[...]=gres
    glow=gres.astype(bf)
    glow_o[...]=glow.reshape(3,F,D)
    gatt_s[:,0:H2]=mm_nt(glow,woo[...]).astype(bf)
    gatt_s[:,H2:D]=mm_nt(glow,wox[...]).astype(bf)
    def add(a,b): return b if a is None else a+b
    for n,(c,c2) in enumerate(pairs):
        prod_s[n*F:(n+1)*F,:]=(rows(gatt_s,c).astype(f32)*rows(v_s,c2).astype(f32)).astype(bf)
    gp_s[...]=mm(prod_s[...],e_ref[...])
    for c in range(3):
        own=[n for n,pr in enumerate(pairs) if pr[0]==c]
        ps=[rows(p_s,n) for n in own]
        gps=[rows(gp_s,n) for n in own]
        spread=functools.reduce(jnp.add,[p*gp for p,gp in zip(ps,gps)])
        for n,p,gp in zip(own,ps,gps): gp_s[n*F:(n+1)*F,:]=p*(gp-spread)*0.125
    prod_s[...]=mm(gp_s[...].astype(bf),et_ref[...]).astype(bf)
    for c in range(3):
        take=lambda which,left,right,at: functools.reduce(jnp.add,[rows(left,n).astype(f32)*rows(right,pr[1-which]).astype(f32) for n,pr in enumerate(pairs) if pr[which]==at]).astype(bf)
        for j,a in ((1,take(0,prod_s,k_s,c)),(2,take(1,prod_s,q_s,c)),(3,take(1,wide_s,gatt_s,c))):
            gpo_o[j,c]=a[:,0:H2]; gpx_o[j][c]=a[:,H2:D]
    gn=None
    for j in range(3):
        gn=add(gn,mm_nt(gpo_o[j+1].reshape(R,H2),pqo[j]))
        gn=gn+mm_nt(gpx_o[j+1][...].reshape(R,H2),pqx[j])
    gm_s[...]=gn
    tot=None; gsum0=None
    for c in range(3):
        gn=gm_s[c*F:(c+1)*F,:]
        n0=(g_ref[...].astype(f32)+emb_ref[c].astype(f32))*r0s[c]
        w=gn*gain0
        dx=r_s[c*F:(c+1)*F,:]+r0s[c]*(w-n0*jnp.mean(w*n0,axis=-1,keepdims=True))
        gsum0=add(gsum0,jnp.sum(gn*n0,axis=0,keepdims=True))
        dx_o[c]=dx.astype(bf)
        tot=add(tot,dx)
    gframe_o[...]=tot
    @pl.when(step==0)
    def _(): gg_o[...]=jnp.zeros_like(gg_o)
    gg_o[0:1,:]+=gsum0
    gg_o[1:2,:]+=gsum1

def local_skip(at_ref,*refs):
    @pl.when(at_ref[0]==1)
    def _():
        local_kernel(*refs)

def local_call(at,g,emb,cot,gao,gax,gains,pqo,pqx,woo,wox,wuo,wux,tile=128):
    N,D=g.shape; H2=D//2; FH=wuo.shape[1]; F=tile
    E=(jnp.arange(D)[:,None]//HEAD==jnp.arange(128)[None,:]).astype(bf)
    ET=E.T
    c3=lambda w: pl.BlockSpec((3,F,w),lambda i,s:(0,i,0))
    whole=lambda shp: pl.BlockSpec(shp,lambda i,s:(0,)*len(shp),pipeline_mode=pl.Buffered(1))
    sd=jax.ShapeDtypeStruct
    S=FH+3*D+4*H2
    out_shape=(sd((3,N,D),f32),sd((3,N,FH),bf),sd((3,N,FH),bf),sd((4,3,N,H2),bf),sd((3,N,FH),bf),sd((3,N,S),bf),sd((3,N,D),bf),sd((N,D),f32),sd((2,D),f32))
    gp=pl.BlockSpec((4,3,F,H2),lambda i,s:(0,0,i,0))
    return pl.pallas_call(local_skip, grid_spec=pltpu.PrefetchScalarGridSpec(num_scalar_prefetch=1,grid=(N//F,),
      in_specs=[pl.BlockSpec((F,D),lambda i,s:(i,0)),c3(D),c3(D),c3(FH),c3(FH),whole((2,D)),whole(E.shape),whole(ET.shape),
        whole(pqo.shape),whole(pqx.shape),whole(woo.shape),whole(wox.shape),whole(wuo.shape),whole(wux.shape)],
      out_specs=(c3(D),c3(FH),c3(FH),gp,c3(FH),c3(S),c3(D),pl.BlockSpec((F,D),lambda i,s:(i,0)),pl.BlockSpec((2,D),lambda i,s:(0,0))),
      scratch_shapes=[pltpu.VMEM((3*F,D),bf)]*3+[pltpu.VMEM((6*F,128),f32)]*2+[pltpu.VMEM((6*F,D),bf)]*2+[pltpu.VMEM((3*F,D),f32),pltpu.VMEM((3*F,D),f32),pltpu.VMEM((3*F,D),bf)]),
      out_shape=out_shape,
      compiler_params=pltpu.CompilerParams(vmem_limit_bytes=65400 * 1024),
      cost_estimate=lasting(57),
      name="local_layer",
    )(at,g,emb,cot,gao,gax,gains,E,ET,pqo,pqx,woo,wox,wuo,wux)

def attend_kernel(at_ref, xo_ref, xs_ref, xc_ref, xb_ref, gain_ref, proj_ref, qid_ref, kid_ref,
                  normed_ref, q_ref, k_ref, v_ref, near_ref, off_ref):
    step = pl.program_id(0)
    rows = xo_ref.shape[0]

    @pl.when((at_ref[0] == 0) & (step == 0))
    def _():
        for j, x_ref in enumerate((xo_ref, xs_ref, xc_ref, xb_ref)):
            part = slice(j * rows, (j + 1) * rows)
            x = x_ref[...].astype(f32)
            scale = lax.rsqrt(jnp.mean(x * x, axis=-1, keepdims=True) + eps)
            normed_ref[part, :] = (x * scale * gain_ref[0:1, :]).astype(bf)
        for j, ref in enumerate((q_ref, k_ref, v_ref)):
            ref[...] = mm(normed_ref[...], proj_ref[j]).astype(bf)

    @pl.when(at_ref[0] == 0)
    def _():
        bias = jnp.where(
            ((qid_ref[:, 1:2] == kid_ref[1:2, :]) & (kid_ref[0:1, :] <= qid_ref[:, 0:1]))
            | (kid_ref[0:1, :] == qid_ref[:, 0:1]),
            0.0,
            far,
        )
        lane = lax.broadcasted_iota(jnp.int32, (1, 2 * HEAD), 1) // HEAD
        here_rows = pl.ds(pl.multiple_of(step * rows, rows), rows)
        for pair in range(q_ref.shape[1] // (2 * HEAD)):
            cols = slice(pair * 2 * HEAD, (pair + 1) * 2 * HEAD)
            q, k, v = q_ref[here_rows, cols], k_ref[:, cols], v_ref[:, cols]
            total = None
            for side in range(2):
                here = lane == side
                scores = mm_nt(jnp.where(here, q * HEAD ** (-0.5), jnp.zeros_like(q)), k) + bias
                top = jnp.max(scores, axis=-1, keepdims=True)
                weights = jnp.exp(scores - top)
                mass = jnp.sum(weights, axis=-1, keepdims=True)
                probs = (weights * (1.0 / mass)).astype(bf)
                term = mm(probs, jnp.where(here, v, jnp.zeros_like(v)))
                total = term if total is None else total + term
            for odd, ref in ((0, near_ref), (1, off_ref)):

                @pl.when(step % 2 == odd)
                def _():
                    ref[0, :, cols] = total.astype(bf)


def attend_call(at, blocks, gains, proj, qid, kid):
    rows, width = blocks[0].shape
    cols = proj.shape[2] // 2
    total = 4 * rows
    whole = lambda shape: pl.BlockSpec(shape, lambda i, s: (0,) * len(shape))
    sd = jax.ShapeDtypeStruct
    half = pl.BlockSpec((1, rows, cols), lambda i, s: (i // 2, 0, 0))
    return pl.pallas_call(
        attend_kernel,
        grid_spec=pltpu.PrefetchScalarGridSpec(
            num_scalar_prefetch=1,
            grid=(4,),
            in_specs=[whole((rows, width))] * 4
            + [
                whole(gains.shape),
                pl.BlockSpec((3, width, cols), lambda i, s: (0, 0, s[2])),
                pl.BlockSpec((rows, 2), lambda i, s: (i, 0)),
                whole(kid.shape),
            ],
            out_specs=(whole((total, width)), *[whole((total, cols))] * 3, half, half),
        ),
        out_shape=(sd((total, width), bf), *[sd((total, cols), bf)] * 3, *[sd((2, rows, cols), bf)] * 2),
        compiler_params=pltpu.CompilerParams(vmem_limit_bytes=60 * 1024 * 1024),
        cost_estimate=lasting(18),
        name="frame_attention",
    )(at, *blocks, gains, proj, qid, kid)


def attend_back_kernel(at_ref, q_ref, k_ref, v_ref, g_ref, qid_ref, kid_ref, gq_ref, gk_ref, gv_ref, ks_ref, vs_ref):
    @pl.when(at_ref[0] == 0)
    def _():
        step = pl.program_id(0)

        @pl.when(step == 0)
        def _():
            ks_ref[...] = jnp.zeros_like(ks_ref)
            vs_ref[...] = jnp.zeros_like(vs_ref)

        bias = jnp.where(
            ((qid_ref[:, 1:2] == kid_ref[1:2, :]) & (kid_ref[0:1, :] <= qid_ref[:, 0:1]))
            | (kid_ref[0:1, :] == qid_ref[:, 0:1]),
            0.0,
            far,
        )
        lane = lax.broadcasted_iota(jnp.int32, (1, 2 * HEAD), 1) // HEAD
        for pair in range(q_ref.shape[1] // (2 * HEAD)):
            cols = slice(pair * 2 * HEAD, (pair + 1) * 2 * HEAD)
            q, k, v, g = q_ref[:, cols], k_ref[:, cols], v_ref[:, cols], g_ref[:, cols]
            gq = None
            for side in range(2):
                here = lane == side
                qh = jnp.where(here, q, jnp.zeros_like(q))
                gh = jnp.where(here, g, jnp.zeros_like(g))
                kh = jnp.where(here, k, jnp.zeros_like(k))
                scores = mm_nt(qh * HEAD ** (-0.5), k) + bias
                top = jnp.max(scores, axis=-1, keepdims=True)
                weights = jnp.exp(scores - top)
                mass = jnp.sum(weights, axis=-1, keepdims=True)
                probs = weights * (1.0 / mass)
                grad_probs = mm_nt(gh, v)
                spread = jnp.sum(probs * grad_probs, axis=-1, keepdims=True)
                gs = (probs * (grad_probs - spread) * HEAD ** (-0.5)).astype(bf)
                term = mm(gs, kh)
                gq = term if gq is None else gq + term
                ks_ref[:, cols] += across_rows(gs, qh)
                vs_ref[:, cols] += across_rows(probs.astype(bf), gh)
            gq_ref[:, cols] = gq.astype(bf)

        @pl.when(step == pl.num_programs(0) - 1)
        def _():
            gk_ref[...] = ks_ref[...].astype(bf)
            gv_ref[...] = vs_ref[...].astype(bf)


def attend_back_call(at, q, k, v, g, qid, kid, rows):
    total, width = q.shape
    part = pl.BlockSpec((rows, width), lambda i, s: (i, 0))
    whole = pl.BlockSpec((total, width), lambda i, s: (0, 0))
    shape = jax.ShapeDtypeStruct((total, width), bf)
    return pl.pallas_call(
        attend_back_kernel,
        grid_spec=pltpu.PrefetchScalarGridSpec(
            num_scalar_prefetch=1,
            grid=(total // rows,),
            in_specs=[part, whole, whole, part, pl.BlockSpec((rows, 2), lambda i, s: (i, 0)), pl.BlockSpec(kid.shape, lambda i, s: (0, 0))],
            out_specs=(part, whole, whole),
            scratch_shapes=[pltpu.VMEM((total, width), f32)] * 2,
        ),
        out_shape=(shape, shape, shape),
        compiler_params=pltpu.CompilerParams(vmem_limit_bytes=60 * 1024 * 1024),
        cost_estimate=lasting(0.01),
        name="frame_attention_back",
    )(at, q, k, v, g, qid, kid)


def front_kernel(at_ref, x_ref, near_ref, off_ref, core_ref, gain_ref, oo_ref, ox_ref, uo_ref, ux_ref, do_ref, dx_ref,
                 resid_ref, mid_ref, act_o, act_x, slope_o, slope_x, out_ref, total_ref):
    @pl.when(at_ref[0] == 0)
    def _():
        step = pl.program_id(0)
        turn = pl.num_programs(0) // 2

        @pl.when(step == 0)
        def _():
            cols = near_ref.shape[2]
            resid = x_ref[...].astype(f32)
            for flip, part, out in ((0, near_ref, oo_ref), (1, off_ref, oo_ref), (0, core_ref, ox_ref), (1, core_ref, ox_ref)):
                spot = pl.ds(pl.multiple_of((at_ref[2] ^ flip) * cols, cols), cols)
                resid = resid + mm(part[flip if part is core_ref else 0], out[spot, :])
            resid_ref[...] = resid
            scale = lax.rsqrt(jnp.mean(resid * resid, axis=-1, keepdims=True) + eps)
            mid_ref[...] = (resid * scale * gain_ref[1:2, :]).astype(bf)
            total_ref[...] = resid

        def part(up, down, act_ref, slope_ref):
            act, slope = gelu_both(mm(mid_ref[...], up[...]))
            act = act.astype(bf)
            act_ref[...] = act
            slope_ref[...] = slope.astype(bf)
            total_ref[...] += mm(act, down[...])

        @pl.when(step < turn)
        def _():
            part(uo_ref, do_ref, act_o, slope_o)

        @pl.when(step >= turn)
        def _():
            part(ux_ref, dx_ref, act_x, slope_x)

        @pl.when(step == pl.num_programs(0) - 1)
        def _():
            out_ref[...] = total_ref[...].astype(bf)


def halves_specs(turn, chunk, width, rows):
    first = lambda i, s: jnp.minimum(i, turn - 1) * (1 - s[0])
    later = lambda i, s: jnp.maximum(i - turn, 0) * (1 - s[0])
    ups = [pl.BlockSpec((width, chunk), lambda i, s, f=f: (0, f(i, s))) for f in (first, later)]
    downs = [pl.BlockSpec((chunk, width), lambda i, s, f=f: (f(i, s), 0)) for f in (first, later)]
    cols = [pl.BlockSpec((rows, chunk), lambda i, s, f=f: (0, f(i, s))) for f in (first, later)]
    return ups, downs, cols


def front_call(at, x, near, off, from_core, gains, out_own, out_oth, up_own, up_oth, down_own, down_oth, chunk=1024):
    rows, width = x.shape
    hidden = up_own.shape[1]
    turn = hidden // chunk
    ups, downs, cols = halves_specs(turn, chunk, width, rows)
    whole = lambda a: pl.BlockSpec(a.shape, lambda i, s: (0,) * a.ndim)
    sd = jax.ShapeDtypeStruct
    full = pl.BlockSpec((rows, width), lambda i, s: (0, 0))
    hid = sd((rows, hidden), bf)
    return pl.pallas_call(
        front_kernel,
        grid_spec=pltpu.PrefetchScalarGridSpec(
            num_scalar_prefetch=1,
            grid=(2 * turn,),
            in_specs=[full, whole(near), whole(off), whole(from_core), whole(gains), whole(out_own), whole(out_oth), *ups, *downs],
            out_specs=(full, full, cols[0], cols[1], cols[0], cols[1], full),
            scratch_shapes=[pltpu.VMEM((rows, width), f32)],
        ),
        out_shape=(sd((rows, width), f32), sd((rows, width), bf), hid, hid, hid, hid, sd((rows, width), bf)),
        compiler_params=pltpu.CompilerParams(vmem_limit_bytes=60 * 1024 * 1024),
        cost_estimate=lasting(15),
        name="global_forward",
    )(at, x, near, off, from_core, gains, out_own, out_oth, up_own, up_oth, down_own, down_oth)


def back_kernel(at_ref, g_ref, resid_ref, gain_ref, so_ref, sx_ref, uo_ref, ux_ref, do_ref, dx_ref,
                rise_o, rise_x, grad_ref, low_ref, gsum_ref, total_ref):
    @pl.when(at_ref[0] == 0)
    def _():
        step = pl.program_id(0)
        turn = pl.num_programs(0) // 2

        def part(up, down, slope_ref, rise_ref):
            rise = (mm_nt(g_ref[...], down[...]) * slope_ref[...].astype(f32)).astype(bf)
            rise_ref[...] = rise
            return mm_nt(rise, up[...])

        @pl.when(step == 0)
        def _():
            total_ref[...] = part(uo_ref, do_ref, so_ref, rise_o)

        @pl.when((step > 0) & (step < turn))
        def _():
            total_ref[...] += part(uo_ref, do_ref, so_ref, rise_o)

        @pl.when(step >= turn)
        def _():
            total_ref[...] += part(ux_ref, dx_ref, sx_ref, rise_x)

        @pl.when(step == pl.num_programs(0) - 1)
        def _():
            resid = resid_ref[...]
            scale = lax.rsqrt(jnp.mean(resid * resid, axis=-1, keepdims=True) + eps)
            normal = resid * scale
            total = total_ref[...]
            unit = total * gain_ref[1:2, :]
            grad = g_ref[...].astype(f32) + scale * (unit - normal * jnp.mean(unit * normal, axis=-1, keepdims=True))
            grad_ref[...] = grad
            low_ref[...] = grad.astype(bf)
            gsum_ref[...] = jnp.sum(total * normal, axis=0, keepdims=True)


def back_call(at, g, resid, gains, slope_own, slope_oth, up_own, up_oth, down_own, down_oth, chunk=1024):
    rows, width = g.shape
    hidden = up_own.shape[1]
    turn = hidden // chunk
    ups, downs, cols = halves_specs(turn, chunk, width, rows)
    sd = jax.ShapeDtypeStruct
    full = pl.BlockSpec((rows, width), lambda i, s: (0, 0))
    hid = sd((rows, hidden), bf)
    line = pl.BlockSpec((1, width), lambda i, s: (0, 0))
    return pl.pallas_call(
        back_kernel,
        grid_spec=pltpu.PrefetchScalarGridSpec(
            num_scalar_prefetch=1,
            grid=(2 * turn,),
            in_specs=[full, full, pl.BlockSpec(gains.shape, lambda i, s: (0, 0)), *cols, *ups, *downs],
            out_specs=(*cols, full, full, line),
            scratch_shapes=[pltpu.VMEM((rows, width), f32)],
        ),
        out_shape=(hid, hid, sd((rows, width), f32), sd((rows, width), bf), sd((1, width), f32)),
        compiler_params=pltpu.CompilerParams(vmem_limit_bytes=60 * 1024 * 1024),
        cost_estimate=lasting(13),
        name="global_backward",
    )(at, g, resid, gains, slope_own, slope_oth, up_own, up_oth, down_own, down_oth)


def split_sides(total, side, mine_ref, theirs_ref, at):
    half = total.shape[0] // 2
    top, bottom = total[:half].astype(bf), total[half:].astype(bf)
    mine_ref[at] = jnp.where(side == 0, top, bottom)
    theirs_ref[at] = jnp.where(side == 0, bottom, top)


def deal(total_ref, at_ref, mine_ref, theirs_ref, plane_first):
    piece = total_ref.shape[0] // 8
    for jz in range(4):
        for jy in range(2):
            place = (at_ref[1] ^ jz) * 2 + (at_ref[2] ^ jy)
            rows = pl.ds(pl.multiple_of(place * piece, piece), piece)
            low, high = jz % 2, jz // 2
            part = total_ref[rows, :].astype(bf)
            if plane_first:
                (theirs_ref if low else mine_ref)[high, jy] = part
            else:
                (theirs_ref if jy else mine_ref)[low * 2 + high] = part


def weight_kernel(at_ref, left, left_in, right, right_in, mine_ref, theirs_ref, total_ref, turned, turned_in, *, here, plane_first):
    @pl.when(at_ref[0] == here)
    def _():
        @pl.when(pl.program_id(0) == 0)
        def _():
            turned[...] = left[...].T
            turned_in[...] = left_in[...].T

        total_ref[...] = mm(turned[...], right[...]) + mm(turned_in[...], right_in[...])
        deal(total_ref, at_ref, mine_ref, theirs_ref, plane_first)


def weight_call(at, here, four, skip, plane_first, name, us, width, cols, chunk=512):
    piece = width // 8
    now = lambda i, s: jnp.where(s[0] == here, i, 0)
    whole = [
        pl.BlockSpec((a.shape[0], width), lambda i, s, c=c: (0, c), pipeline_mode=pl.Buffered(1))
        for a, c in zip(four[:2], skip)
    ]
    part = [
        pl.BlockSpec((a.shape[0], chunk), lambda i, s, c=c: (0, now(i, s) + c)) for a, c in zip(four[2:], skip[2:])
    ]
    if plane_first:
        shape = jax.ShapeDtypeStruct((2, 2, piece, cols), bf)
        out = pl.BlockSpec((2, 2, piece, chunk), lambda i, s: (0, 0, 0, now(i, s)))
    else:
        shape = jax.ShapeDtypeStruct((4, piece, cols), bf)
        out = pl.BlockSpec((4, piece, chunk), lambda i, s: (0, 0, now(i, s)))
    return pl.pallas_call(
        functools.partial(weight_kernel, here=here, plane_first=plane_first),
        grid_spec=pltpu.PrefetchScalarGridSpec(
            num_scalar_prefetch=1,
            grid=(cols // chunk,),
            in_specs=whole + part,
            out_specs=(out, out),
            scratch_shapes=[pltpu.VMEM((width, chunk), f32)] + [pltpu.VMEM((width, a.shape[0]), bf) for a in four[:2]],
        ),
        out_shape=(shape, shape),
        compiler_params=pltpu.CompilerParams(vmem_limit_bytes=60 * 1024 * 1024),
        cost_estimate=lasting(us),
        name=name,
    )(at, *four)


def rest_kernel(at_ref, *refs, here):
    pairs = (len(refs) - 3) // 4
    lows, normeds, rights = (refs[j * pairs : (j + 1) * pairs] for j in range(3))
    mine_ref, theirs_ref, total_ref = refs[3 * pairs : 3 * pairs + 3]
    turned = refs[3 * pairs + 3 :]
    step = pl.program_id(0)
    piece = total_ref.shape[0] // 8

    @pl.when(at_ref[0] == here)
    def _():
        for when, lefts in ((0, lows), (1, normeds)):

            @pl.when(step == when)
            def _():
                for left, turn in zip(lefts, turned):
                    turn[...] = left[...].T

        total = None
        for turn, right in zip(turned, rights):
            term = mm(turn[...], right[0] if len(right.shape) == 3 else right[...])
            total = term if total is None else total + term
        total_ref[...] = total
        for jz in range(4):
            for jy in range(2):
                place = (at_ref[1] ^ jz) * 2 + (at_ref[2] ^ jy)
                rows = pl.ds(pl.multiple_of(place * piece, piece), piece)
                for h in range(mine_ref.shape[2]):
                    cols = slice(h * mine_ref.shape[4], (h + 1) * mine_ref.shape[4])
                    (theirs_ref if jy else mine_ref)[jz % 2 * 2 + jz // 2, 0, h] = total_ref[rows, cols].astype(bf)


def rest_call(at, here, lows, normeds, rights, name, us, width):
    piece = width // 8
    count = 4
    narrow = width // 4
    size = rights[0][0].shape[2]
    whole = lambda pair: pl.BlockSpec((pair[0].shape[0], width), lambda i, s: (0, pair[1]), pipeline_mode=pl.Buffered(1))

    def part(pair):
        a, c = pair
        now = lambda i, s: jnp.where(s[0] == here, i, 0)
        if a.ndim == 3:
            return pl.BlockSpec((1,) + a.shape[1:], lambda i, s: (now(i, s), 0, 0))
        return pl.BlockSpec((a.shape[0], size), lambda i, s: (0, c + now(i, s)))

    halves = size // narrow
    shape = jax.ShapeDtypeStruct((4, count, halves, piece, narrow), bf)
    out = pl.BlockSpec((4, 1, halves, piece, narrow), lambda i, s: (0, jnp.where(s[0] == here, i, 0), 0, 0, 0))
    return pl.pallas_call(
        functools.partial(rest_kernel, here=here),
        grid_spec=pltpu.PrefetchScalarGridSpec(
            num_scalar_prefetch=1,
            grid=(count,),
            in_specs=[*map(whole, lows), *map(whole, normeds), *map(part, rights)],
            out_specs=(out, out),
            scratch_shapes=[pltpu.VMEM((width, size), f32)] + [pltpu.VMEM((width, a.shape[0]), bf) for a, _ in lows],
        ),
        out_shape=(shape, shape),
        compiler_params=pltpu.CompilerParams(vmem_limit_bytes=60 * 1024 * 1024),
        cost_estimate=lasting(us),
        name=name,
    )(at, *(a for a, _ in (*lows, *normeds, *rights)))


def fall_kernel(at_ref, resid_ref, ao_ref, ax_ref, do_ref, dx_ref, out_ref, total_ref):
    step = pl.program_id(0)
    turn = pl.num_programs(0) // 2
    books, planes, half = out_ref.shape[1], out_ref.shape[0], out_ref.shape[2]

    @pl.when(at_ref[0] == 1)
    def _():
        @pl.when(step == 0)
        def _():
            total_ref[...] = resid_ref[...]

        @pl.when(step < turn)
        def _():
            total_ref[...] += mm(ao_ref[...], do_ref[...])

        @pl.when(step >= turn)
        def _():
            total_ref[...] += mm(ax_ref[...], dx_ref[...])

        @pl.when(step == pl.num_programs(0) - 1)
        def _():
            for c in range(books):
                for z in range(planes):
                    first = (c * planes + z) * half
                    out_ref[z, c] = total_ref[first : first + half, :].astype(bf)


def fall_call(at, resid, act_own, act_oth, down_own, down_oth, planes, books, chunk=1024):
    rows, width = resid.shape
    turn = down_own.shape[0] // chunk
    first = lambda i, s: jnp.minimum(i, turn - 1) * s[0]
    later = lambda i, s: jnp.maximum(i - turn, 0) * s[0]
    col = lambda f: pl.BlockSpec((rows, chunk), lambda i, s: (0, f(i, s)))
    row = lambda f: pl.BlockSpec((chunk, width), lambda i, s: (f(i, s), 0))
    shape = (planes, books, rows // planes // books, width)
    return pl.pallas_call(
        fall_kernel,
        grid_spec=pltpu.PrefetchScalarGridSpec(
            num_scalar_prefetch=1,
            grid=(2 * turn,),
            in_specs=[pl.BlockSpec((rows, width), lambda i, s: (0, 0), pipeline_mode=pl.Buffered(1)), col(first), col(later), row(first), row(later)],
            out_specs=pl.BlockSpec(shape, lambda i, s: (0, 0, 0, 0)),
            scratch_shapes=[pltpu.VMEM((rows, width), f32)],
        ),
        out_shape=jax.ShapeDtypeStruct(shape, bf),
        compiler_params=pltpu.CompilerParams(vmem_limit_bytes=60 * 1024 * 1024),
        cost_estimate=lasting(0.01),
        name="local_output",
    )(at, resid, act_own, act_oth, down_own, down_oth)


def table_kernel(at_ref, code_ref, code_in_ref, own_ref, got_ref, low_ref, high_ref, total_ref):
    entries = total_ref.shape[0]
    slots = lax.broadcasted_iota(jnp.int32, (entries, code_ref.shape[2]), 0)
    piece = low_ref.shape[3]

    @pl.when(at_ref[0] == 1)
    def _():
        hot = (slots == code_ref[0]).astype(f32).astype(bf)
        hot_in = (slots == code_in_ref[0]).astype(f32).astype(bf)
        total_ref[...] = mm(hot, own_ref[0]) + mm(hot_in, got_ref[0])
        for jz in range(4):
            for jy in range(2):
                place = (at_ref[1] ^ jz) * 2 + (at_ref[2] ^ jy)
                spot = (jz % 2) * 2 + jz // 2
                for ref, base in ((low_ref, 0), (high_ref, entries // 2)):
                    rows = pl.ds(pl.multiple_of(base + place * piece, piece), piece)
                    ref[jy, spot, 0] = total_ref[rows, :].astype(bf)


def table_call(at, codes, codes_in, own, got, entries):
    books, rows = codes.shape
    width = own.shape[2]
    line = pl.BlockSpec((1, 1, rows), lambda c, s: (c, 0, 0))
    block = pl.BlockSpec((1, rows, width), lambda c, s: (c, 0, 0))
    shape = (2, 4, books, entries // 16, width)
    out = pl.BlockSpec((2, 4, 1, entries // 16, width), lambda c, s: (0, 0, c, 0, 0))
    return pl.pallas_call(
        table_kernel,
        grid_spec=pltpu.PrefetchScalarGridSpec(
            num_scalar_prefetch=1,
            grid=(books,),
            in_specs=[line, line, block, block],
            out_specs=(out, out),
            scratch_shapes=[pltpu.VMEM((entries, width), f32)],
        ),
        out_shape=(jax.ShapeDtypeStruct(shape, bf),) * 2,
        compiler_params=pltpu.CompilerParams(vmem_limit_bytes=60 * 1024 * 1024),
        cost_estimate=lasting(4),
        name="table_gradient",
    )(at, codes[:, None, :], codes_in[:, None, :], own, got)


def prepare_kernel(at_ref, code_ref, cot_ref, do_ref, dx_ref, table_ref, look_ref, po_ref, px_ref):
    step = pl.program_id(0)
    turn = pl.num_programs(0) // 2
    books, rows, chunk = po_ref.shape

    @pl.when(at_ref[0] == 1)
    def _():
        @pl.when(step < look_ref.shape[0])
        def _():
            slots = lax.broadcasted_iota(jnp.int32, (rows, table_ref.shape[1]), 1)
            hot = (slots == code_ref[jnp.minimum(step, look_ref.shape[0] - 1)]).astype(f32).astype(bf)
            look_ref[jnp.minimum(step, look_ref.shape[0] - 1)] = mm(hot, table_ref[0]).astype(bf)

        @pl.when(step < turn)
        def _():
            po_ref[...] = mm_nt(cot_ref[...], do_ref[...]).astype(bf).reshape(books, rows, chunk)

        @pl.when(step >= turn)
        def _():
            px_ref[...] = mm_nt(cot_ref[...], dx_ref[...]).astype(bf).reshape(books, rows, chunk)


def prepare_call(at, codes, cot, down_own, down_oth, table, chunk=512):
    books, rows = codes.shape
    width = cot.shape[1]
    hidden = down_own.shape[0]
    turn = hidden // chunk
    first = lambda i, s: jnp.minimum(i, turn - 1) * s[0]
    later = lambda i, s: jnp.maximum(i - turn, 0) * s[0]
    down = lambda f: pl.BlockSpec((chunk, width), lambda i, s: (f(i, s), 0))
    out = lambda f: pl.BlockSpec((books, rows, chunk), lambda i, s: (0, 0, f(i, s)))
    sd = jax.ShapeDtypeStruct
    return pl.pallas_call(
        prepare_kernel,
        grid_spec=pltpu.PrefetchScalarGridSpec(
            num_scalar_prefetch=1,
            grid=(2 * turn,),
            in_specs=[
                pl.BlockSpec((books, rows, 1), lambda i, s: (0, 0, 0)),
                pl.BlockSpec(cot.shape, lambda i, s: (0, 0)),
                down(first),
                down(later),
                pl.BlockSpec((1,) + table.shape[1:], lambda i, s: (jnp.minimum(i, books - 1) * s[0], 0, 0)),
            ],
            out_specs=(pl.BlockSpec((books, rows, width), lambda i, s: (0, 0, 0)), out(first), out(later)),
        ),
        out_shape=(sd((books, rows, width), bf), sd((books, rows, hidden), bf), sd((books, rows, hidden), bf)),
        compiler_params=pltpu.CompilerParams(vmem_limit_bytes=60 * 1024 * 1024),
        cost_estimate=lasting(5),
        name="local_prepare",
    )(at, codes[:, :, None], cot, down_own, down_oth, table)


def fence(*groups):
    return lax.optimization_barrier(groups)


def body(frames, codes, lengths, gains, w_qkv, w_out, w_up, w_down, table, cotangent):
    batches, share, width = frames.shape
    members = lax.axis_size("dp") // batches
    if (
        lax.axis_size("section") != 2
        or lax.axis_size("tensor") != 2
        or members != 2
        or lax.axis_size("dp") != 2 * batches
        or batches & (batches - 1)
        or share % 32
        or table.shape[1] != width
    ):
        return plain_body(frames, codes, lengths, gains, w_qkv, w_out, w_up, w_down, table, cotangent)
    place, core = lax.axis_index("dp"), lax.axis_index("tensor")
    plane, side = place // members, place % members
    on_first = lax.axis_index("section") == 0
    half = share // 2
    rows = batches * half
    count = 2 * batches
    at = jnp.stack([lax.axis_index("section"), plane, side]).astype(jnp.int32)

    everywhere, first, second = (0, 1), (0,), (1,)

    def linked(a, flip_place, flip_core, sections=everywhere):
        pairs = [
            ((z * count + i) * 2 + j, (z * count + (i ^ flip_place)) * 2 + (j ^ flip_core))
            for z in sections
            for i in range(count)
            for j in range(2)
        ]
        return lax.ppermute(a, ("section", "dp", "tensor"), pairs)

    def core_swap(a, sections=everywhere):
        return linked(a, 0, 1, sections)

    def side_swap(a, sections=everywhere):
        return linked(a, 1, 0, sections)

    def both_swap(a, sections=everywhere):
        return linked(a, 1, 1, sections)

    def to_local(a):
        return lax.ppermute(a, "section", [(0, 1)])

    def to_global(a):
        return lax.ppermute(a, "section", [(1, 0)])

    def planes_in(a, sections=everywhere):
        pieces = [lax.dynamic_slice_in_dim(a, plane ^ k, 1, 0) for k in range(batches)]
        return jnp.concatenate([pieces[0], *(linked(pieces[k], 2 * k, 0, sections) for k in range(1, batches))], 0)

    def planes_out(a, sections=everywhere):
        got = [a[:1], *(linked(a[k : k + 1], 2 * k, 0, sections) for k in range(1, batches))]
        out = jnp.zeros_like(a)
        for k in range(batches):
            out = lax.dynamic_update_slice_in_dim(out, got[k], plane ^ k, 0)
        return out

    def core_half(a, axis):
        return lax.dynamic_slice_in_dim(a, core * half, half, axis)

    def join_cores(a, axis):
        other = core_swap(a)
        return jnp.where(core == 0, jnp.concatenate([a, other], axis), jnp.concatenate([other, a], axis))

    def quarter(a, axis):
        size = a.shape[axis] // 2
        return lax.dynamic_slice_in_dim(a, side * size, size, axis)

    def by_side(mine, theirs, axis):
        return jnp.where(side == 0, jnp.concatenate([mine, theirs], axis), jnp.concatenate([theirs, mine], axis))

    x_own = planes_in(core_half(frames, 1), first).reshape(rows, width)
    x_side = side_swap(x_own, first)
    x_core, x_both = core_swap(x_own), core_swap(x_side)

    def positions(jt, js):
        base = ((jnp.arange(batches)[:, None] ^ plane) * 2 + (side ^ js)) * share + (core ^ jt) * half
        return (base + jnp.arange(half)[None, :]).reshape(-1)

    pos = jnp.concatenate([positions(0, 0), positions(0, 1), positions(1, 0), positions(1, 1)]).astype(jnp.int32)
    doc_ends = jnp.cumsum(lax.dynamic_index_in_dim(lengths, plane, 0, keepdims=False))
    doc = doc_index(pos, doc_ends)
    qid = jnp.stack([pos, doc], 1)
    kid = jnp.stack([pos, jnp.where(pos < doc_ends[-1], doc, -1)], 0)

    cot = planes_in(core_half(cotangent.transpose(0, 2, 1, 3), 2), second)
    codes_own = planes_in(core_half(codes.transpose(0, 2, 1), 2), second)
    (x_core, x_both, qid, kid, cot, codes_own), (w_qkv, w_out, w_up, w_down) = fence(
        (x_core, x_both, qid, kid, cot, codes_own), (w_qkv, w_out, w_up, w_down)
    )
    gains_here = gains[0]
    proj_own = w_qkv[0].transpose(1, 0, 2)
    out_own, up_own, down_own = w_out[0], w_up[0], w_down[0]
    out_oth, up_oth, down_oth = (core_swap(w) for w in (out_own, up_own, down_own))
    proj_oth = core_swap(proj_own)

    normed_all, q, k, v, near, off = attend_call(at, (x_own, x_side, x_core, x_both), gains_here, proj_own, qid, kid)
    proj_mine = quarter(proj_own, 2)
    off_got = side_swap(off, first)
    from_core = core_swap(jnp.concatenate([near[1:], off_got[1:]], 0))
    attended = jnp.stack([near[0], off[0], near[1], off[1]]).reshape(4 * rows, -1)
    x32 = x_own.astype(f32)
    resid, mid, act_own, act_oth, slope_own, slope_oth, global_low = front_call(
        at, x_own, near, off_got, from_core, gains_here, out_own, out_oth, up_own, up_oth, down_own, down_oth
    )
    mid_in, act_in = core_swap(mid), core_swap(act_oth)

    arrived = to_local(global_low)
    cot = cot.transpose(1, 0, 2, 3).reshape(CODEBOOKS, rows, width)
    codes_own = codes_own.transpose(1, 0, 2).reshape(CODEBOOKS, rows)
    slots = jnp.arange(table.shape[1], dtype=jnp.int32)
    cot_rows = cot.reshape(-1, width)
    cot_in, codes_oth = core_swap(cot_rows), core_swap(codes_own)

    looked_up, pull_own, pull_oth = prepare_call(at, codes_own, cot_rows, down_own, down_oth, table)
    (pull_own, codes_oth, cot_in), = fence((pull_own, codes_oth, cot_in))
    (
        l_resid, l_act, l_rise, l_pack, l_act_oth, l_send, l_grad, l_frame, l_gains,
    ) = local_call(
        at, arrived, looked_up, cot, pull_own, pull_oth, gains_here, proj_own, proj_oth, out_own, out_oth, up_own, up_oth
    )
    global_moved = planes_out(global_low.reshape(batches, half, width), first)
    global_sent = to_local(global_moved)
    (l_frame, l_grad, l_act_oth, global_moved, global_sent), (l_send,) = fence(
        (l_frame, l_grad, l_act_oth, global_moved, global_sent), (l_send,)
    )
    grad_low = to_global(l_frame.astype(bf))

    flat = lambda a: a.reshape(-1, a.shape[-1])
    hidden = up_own.shape[1]

    def swap(a, bit, sections=everywhere):
        return linked(a, 1 << bit, 0, sections)

    def meet(mine, got):
        return (mine.astype(f32) + got.astype(f32)).astype(bf)

    def cols_of(a, which):
        return lax.dynamic_slice_in_dim(a, which * (width // 2), width // 2, 2)

    l_grad_in, l_act_in = core_swap(cols_of(l_grad, 1 - core)), core_swap(flat(l_act_oth), second)
    table_low, table_high = table_call(at, codes_own, codes_oth, cols_of(l_grad, core), l_grad_in, table.shape[1])
    l_down_mine, l_down_theirs = weight_call(
        at, 1, (cot_rows, cot_in, flat(l_act), l_act_in), (0, 0, 0, 0), True, "local_down_gradient", 4, width, hidden
    )
    (table_low, table_high, grad_low, l_down_theirs), (l_send,) = fence(
        (table_low, table_high, grad_low, l_down_theirs), (l_send,)
    )
    l_got = core_swap(flat(l_send), second)

    grad_in_low = core_swap(grad_low)
    rise_own, rise_oth, grad_resid, low_own, gain_mid = back_call(
        at, grad_low, resid, gains_here, slope_own, slope_oth, up_own, up_oth, down_own, down_oth
    )
    rise_in = core_swap(rise_oth)
    local_low = fall_call(at, flat(l_resid), flat(l_act), flat(l_act_oth), down_own, down_oth, batches, CODEBOOKS)
    (low_own, grad_in_low, local_low), (l_got,) = fence((low_own, grad_in_low, local_low), (l_got,))
    local_moved = planes_out(local_low, second)
    low_side = side_swap(low_own, first)
    down_mine, down_theirs = weight_call(
        at, 0, (grad_low, grad_in_low, act_own, act_in), (0, 0, 0, 0), True, "down_gradient", 8, width, hidden
    )
    l_up_mine, l_up_theirs = weight_call(
        at, 1, (flat(l_send), l_got, flat(l_rise), l_got),
        (hidden // width, hidden // width, 0, 0), False, "local_up_gradient", 4, width, hidden,
    )
    down_theirs = jnp.where(on_first, down_theirs, l_down_theirs)
    (down_theirs, l_up_theirs, local_moved), (rise_in, table_low) = fence(
        (down_theirs, l_up_theirs, local_moved), (rise_in, table_low)
    )
    table_moved = to_global(table_low)
    down_got = swap(down_theirs, 1)
    up_mine, up_theirs = weight_call(
        at, 0, (mid, mid_in, rise_own, rise_in), (0, 0, 0, 0), False, "up_gradient", 8, width, hidden
    )
    up_theirs = jnp.where(on_first, up_theirs, l_up_theirs)
    (up_theirs, low_side), (l_pack, l_act) = fence((up_theirs, low_side), (l_pack, l_act))
    up_got = swap(up_theirs, 0)
    low_at = hidden // width + 1
    l_rest_mine, l_rest_theirs = rest_call(
        at, 1, ((flat(l_send), low_at), (l_got, low_at)), ((flat(l_send), low_at + 1), (l_got, low_at + 1)),
        ((l_pack.reshape(4, CODEBOOKS * rows, -1), 0), (l_got, (hidden + 3 * width) // l_pack.shape[-1])),
        "local_rest_gradient", 0.01, width,
    )
    (l_rest_theirs, low_side), = fence((l_rest_theirs, low_side))
    low_all = jnp.concatenate([low_own, low_side, core_swap(low_own), core_swap(low_side)], 0)
    grad_att = against_rows(low_all, quarter(out_own, 0)).astype(bf)
    grad_packs = attend_back_call(at, q, k, v, grad_att, qid, kid, rows)
    rest_mine, rest_theirs = rest_call(
        at, 0, ((low_all, 0),), ((normed_all, 0),), ((jnp.stack([attended, *grad_packs]), 0),), "rest_gradient", 0.01, width
    )
    flip = side == 0
    empty = jnp.zeros_like(rest_mine)

    def spread_out(a):
        return jnp.concatenate([jnp.where(flip, a, empty), jnp.where(flip, empty, a)], 2)

    rest_theirs = jnp.where(on_first, spread_out(rest_theirs), l_rest_theirs)
    (rest_theirs, down_got, up_got), (grad_packs, rest_mine, local_moved) = fence(
        (rest_theirs, down_got, up_got), (grad_packs, rest_mine, local_moved)
    )
    rest_got = swap(rest_theirs, 0)
    rest_mine = jnp.where(on_first, spread_out(rest_mine), l_rest_mine)
    up_now = meet(jnp.where(on_first, up_mine, l_up_mine), up_got)
    up_got = swap(up_now[2:], 1)
    down_now = meet(jnp.where(on_first, down_mine, l_down_mine), down_got)
    down_got = swap(down_now[1], 2)
    part_normed = sum(against_rows(g, proj_mine[j]) for j, g in enumerate(grad_packs))
    pair = part_normed[: 2 * rows] + core_swap(part_normed[2 * rows :].astype(bf)).astype(f32)
    pair_side = side_swap(pair[rows:].astype(bf), first)
    local_sent = to_global(local_moved)
    (rest_got, rest_mine, up_got, down_got, pair_side, table_moved), = fence(
        (rest_got, rest_mine, up_got, down_got, pair_side, table_moved)
    )
    rest_now = meet(rest_mine, rest_got)
    (rest_now,), (up_got, down_got, pair_side) = fence((rest_now,), (up_got, down_got, pair_side))
    rest_got = swap(rest_now[2:], 1)
    down_now = meet(down_now[0], down_got)
    down_got = swap(down_now[1], 0)
    up_now = meet(up_now[:2], up_got)
    up_got = swap(up_now[1], 2)
    grad_normed = pair[:rows] + pair_side.astype(f32)
    back_in, gain_in = rms_back(x32, gains_here[0], grad_normed)
    grad_frames = grad_resid + back_in
    gain_sum = jnp.where(on_first, jnp.concatenate([gain_in[None], gain_mid]), l_gains)
    gain_sum = (gain_sum + core_swap(gain_sum)).reshape(2, batches, 2, -1)
    piece = width // count
    gain_rows = jnp.concatenate(
        [
            lax.dynamic_slice(gain_sum, (0, plane ^ (2 * j + i), side ^ y, 0), (2, 1, 1, piece)).reshape(1, -1)
            for y in range(2)
            for i in range(2)
            for j in range(2)
        ]
    ).reshape(2, batches, 2 * piece)
    gain_rows = jnp.pad(gain_rows.astype(bf)[:, :, None, :], ((0, 0), (0, 0), (0, 15), (0, width // 2 - 2 * piece)))
    table_now = jnp.where(on_first, table_moved, table_high).reshape(2, batches, -1, width // 2)
    table_now = jnp.concatenate([table_now, gain_rows], 2)
    table_got = swap(table_now[1], 0)
    inner = jnp.where(on_first, grad_frames, l_frame).astype(bf).reshape(2, 2, half, width)
    inner_got = swap(inner[1], 2)
    (rest_got, up_got, down_got, table_got, local_sent, inner_got), = fence(
        (rest_got, up_got, down_got, table_got, local_sent, inner_got)
    )
    rest_now = meet(rest_now[:2], rest_got)
    table_now = meet(table_now[0], table_got)
    (table_now, rest_now), (inner_got, local_sent) = fence((table_now, rest_now), (inner_got, local_sent))
    table_got = swap(table_now[2:], 1)
    rest_got = swap(rest_now[1], 2)
    near_got = swap(jnp.stack([inner[0, 1], inner_got[1]]), 1)
    local_out = join_cores(jnp.where(on_first, local_sent, local_moved), 2).transpose(0, 2, 1, 3)
    (near_got, rest_got, table_got, local_out), = fence((near_got, rest_got, table_got, local_out))
    blocks = (inner[0, 0], near_got[0], inner_got[0], near_got[1])
    inner = jnp.zeros((batches, half, width), bf)
    for k, block in enumerate(blocks):
        inner = lax.dynamic_update_slice_in_dim(inner, block[None], plane ^ k, 0)
    global_out = join_cores(jnp.where(on_first, global_moved, global_sent), 1)
    down_share = down_now[0].astype(f32) + down_got.astype(f32)
    up_share = up_now[0].astype(f32) + up_got.astype(f32)
    table_now = meet(table_now[:2], table_got)
    table_got = swap(table_now[1], 2)
    input_grads = join_cores(inner, 1).astype(f32)[None]
    mix = out_own.shape[0]
    rest_share = rest_now[0].astype(f32) + rest_got.astype(f32)
    proj_share = rest_share[1:].transpose(2, 0, 1, 3).reshape(piece, 3, mix)
    out_share = rest_share[0].transpose(0, 2, 1).reshape(mix, piece)
    (local_out, global_out, up_share, down_share, input_grads, proj_share, out_share), (table_got,) = fence(
        (local_out, global_out, up_share, down_share.T, input_grads, proj_share, out_share), (table_got,)
    )
    table_now = table_now[0].astype(f32) + table_got.astype(f32)
    gain_share = table_now[-16, : 2 * piece].reshape(2, piece)
    grad_table = join_cores(table_now[:-16].reshape(CODEBOOKS, -1, width // 2).astype(bf), 2).astype(f32)

    return (
        global_out,
        local_out,
        input_grads,
        proj_share[None],
        out_share[None],
        up_share[None],
        down_share[None],
        gain_share[None],
        grad_table,
    )


def solution(mesh):
    in_specs = (
        P(None, "dp", None),
        P(None, "dp", None),
        P(),
        P("section", None, None),
        P("section", None, None, "tensor"),
        P("section", "tensor", None),
        P("section", None, "tensor"),
        P("section", "tensor", None),
        P(),
        P(None, "dp", None, None),
    )
    out_specs = (
        P(None, "dp", None),
        P(None, "dp", None, None),
        P("section", None, "dp", None),
        P("section", "dp", None, "tensor"),
        P("section", "tensor", "dp"),
        P("section", "dp", "tensor"),
        P("section", "tensor", "dp"),
        P("section", None, "dp"),
        P(None, ("section", "dp"), None),
    )
    return jax.shard_map(body, mesh=mesh, in_specs=in_specs, out_specs=out_specs, check_vma=False)
```

```python
import functools

import jax
import jax.numpy as jnp
from jax import lax
from jax.experimental import pallas as pl
from jax.experimental.pallas import tpu as pltpu
from jax.sharding import PartitionSpec as P

HEAD = 64
CODEBOOKS = 3


eps = 1e-05
far = -1e30


def from_behind(block, axis, distance):
    devices = range(lax.axis_size(axis))
    route = [(i - distance, i) for i in devices if i - distance in devices]
    return lax.ppermute(block, axis, route)


def rms_scale(values):
    return lax.rsqrt(jnp.mean(values * values, axis=-1, keepdims=True) + eps)


def rms_back(values, gain_row, grad_normed):
    factor = rms_scale(values)
    normal = values * factor
    grad_unit = grad_normed * gain_row
    grad_values = factor * (
        grad_unit - normal * jnp.mean(grad_unit * normal, axis=-1, keepdims=True)
    )
    return (grad_values, jnp.sum(grad_normed * normal, axis=0))


def head_total(partial_sum):
    return lax.psum(partial_sum, "tensor")


def matmul(left, right):
    return jnp.dot(left, right, preferred_element_type=jnp.float32)


def across_rows(left, right):
    return lax.dot_general(
        left, right, (((0,), (0,)), ((), ())), preferred_element_type=jnp.float32
    )


def against_rows(left, right):
    return lax.dot_general(
        left, right, (((1,), (1,)), ((), ())), preferred_element_type=jnp.float32
    )


def smooth_gate(values):
    return jax.nn.gelu(values, approximate=True)


def doc_index(positions, doc_ends):
    return jnp.sum((positions[:, None] >= doc_ends[None, :]).astype(jnp.int32), axis=1)


def allowed_mask(query_pos, key_pos, doc_ends):
    same_doc = doc_index(query_pos, doc_ends)[:, None] == doc_index(key_pos, doc_ends)[None, :]
    earlier = key_pos[None, :] <= query_pos[:, None]
    live = (key_pos < doc_ends[-1])[None, :]
    return same_doc & earlier & live | (key_pos[None, :] == query_pos[:, None])


def masked_softmax(scores, mask, factor):
    logits = jnp.where(mask, scores * factor, far)
    top = jnp.max(logits, axis=-1, keepdims=True)
    weights = jnp.exp(logits - top)
    mass = jnp.sum(weights, axis=-1, keepdims=True)
    return (weights / mass, (top + jnp.log(mass))[..., 0])


def frame_forward(packed, query_pos, doc_ends, head_count):
    row_count = packed.shape[0]
    width = packed.shape[1] // 3
    factor = HEAD ** (-0.5)
    parts = packed.reshape(row_count, 3, width)
    all_keys, all_values = (
        lax.all_gather(parts[:, 1], "dp", axis=0, tiled=True),
        lax.all_gather(parts[:, 2], "dp", axis=0, tiled=True),
    )
    key_count = all_keys.shape[0]
    key_pos = jnp.arange(key_count, dtype=jnp.int32)
    mask = allowed_mask(query_pos, key_pos, doc_ends)
    queries = parts[:, 0].reshape(row_count, head_count, -1)
    scores = jnp.einsum(
        "qhe,khe->hqk",
        queries,
        all_keys.reshape(key_count, head_count, -1),
        preferred_element_type=jnp.float32,
    )
    probs, log_mass = masked_softmax(scores, mask[None], factor)
    attended = jnp.einsum(
        "hqk,khe->qhe",
        probs.astype(jnp.bfloat16),
        all_values.reshape(key_count, head_count, -1),
        preferred_element_type=jnp.float32,
    )
    return (attended.reshape(row_count, width), log_mass)


def frame_backward(packed, grad_att, log_mass, query_pos, doc_ends, head_count):
    row_count = packed.shape[0]
    width = packed.shape[1] // 3
    factor = HEAD ** (-0.5)
    parts = packed.reshape(row_count, 3, width)
    all_keys, all_values = (
        lax.all_gather(parts[:, 1], "dp", axis=0, tiled=True),
        lax.all_gather(parts[:, 2], "dp", axis=0, tiled=True),
    )
    key_count = all_keys.shape[0]
    key_pos = jnp.arange(key_count, dtype=jnp.int32)
    queries = parts[:, 0].reshape(row_count, head_count, -1)
    grad_heads = grad_att.reshape(row_count, head_count, -1)
    keys_heads = all_keys.reshape(key_count, head_count, -1)
    scores = jnp.einsum("qhe,khe->hqk", queries, keys_heads, preferred_element_type=jnp.float32)
    mask = allowed_mask(query_pos, key_pos, doc_ends)
    probs = jnp.exp(jnp.where(mask[None], scores * factor, far) - log_mass[:, :, None])
    grad_probs = jnp.einsum(
        "qhe,khe->hqk",
        grad_heads,
        all_values.reshape(key_count, head_count, -1),
        preferred_element_type=jnp.float32,
    )
    spread = jnp.sum(probs * grad_probs, axis=-1)
    grad_scores = (probs * (grad_probs - spread[:, :, None]) * factor).astype(jnp.bfloat16)
    grad_queries = jnp.einsum(
        "hqk,khe->qhe", grad_scores, keys_heads, preferred_element_type=jnp.float32
    ).reshape(row_count, width)
    keys_term = jnp.einsum(
        "hqk,qhe->khe", grad_scores, queries, preferred_element_type=jnp.float32
    ).reshape(key_count, width)
    values_term = jnp.einsum(
        "hqk,qhe->khe", probs.astype(jnp.bfloat16), grad_heads, preferred_element_type=jnp.float32
    ).reshape(key_count, width)
    grad_keys, grad_values = (
        lax.psum_scatter(keys_term, "dp", scatter_dimension=0, tiled=True),
        lax.psum_scatter(values_term, "dp", scatter_dimension=0, tiled=True),
    )
    return jnp.stack([grad_queries, grad_keys, grad_values], axis=1).reshape(row_count, 3 * width)


def codebook_forward(packed, head_count):
    row_count = packed.shape[0]
    width = packed.shape[1] // 3
    factor = HEAD ** (-0.5)
    parts = packed.reshape(row_count // CODEBOOKS, CODEBOOKS, 3, head_count, -1)
    scores = jnp.einsum(
        "nche,ndhe->nhcd", parts[:, :, 0], parts[:, :, 1], preferred_element_type=jnp.float32
    )
    order = jnp.arange(CODEBOOKS, dtype=jnp.int32)
    mask = order[None, :] <= order[:, None]
    probs, log_mass = masked_softmax(scores, mask, factor)
    attended = jnp.einsum(
        "nhcd,ndhe->nche",
        probs.astype(jnp.bfloat16),
        parts[:, :, 2],
        preferred_element_type=jnp.float32,
    )
    return (attended.reshape(row_count, width), probs)


def codebook_backward(packed, grad_att, probs, head_count):
    row_count = packed.shape[0]
    width = packed.shape[1] // 3
    factor = HEAD ** (-0.5)
    parts = packed.reshape(row_count // CODEBOOKS, CODEBOOKS, 3, head_count, -1)
    grad_heads = grad_att.reshape(row_count // CODEBOOKS, CODEBOOKS, head_count, -1)
    grad_probs = jnp.einsum(
        "nche,ndhe->nhcd", grad_heads, parts[:, :, 2], preferred_element_type=jnp.float32
    )
    spread = jnp.sum(probs * grad_probs, axis=-1, keepdims=True)
    grad_scores = (probs * (grad_probs - spread) * factor).astype(jnp.bfloat16)
    grad_queries = jnp.einsum(
        "nhcd,ndhe->nche", grad_scores, parts[:, :, 1], preferred_element_type=jnp.float32
    )
    grad_keys = jnp.einsum(
        "nhcd,nche->ndhe", grad_scores, parts[:, :, 0], preferred_element_type=jnp.float32
    )
    grad_values = jnp.einsum(
        "nhcd,nche->ndhe",
        probs.astype(jnp.bfloat16),
        grad_heads,
        preferred_element_type=jnp.float32,
    )
    return jnp.stack([grad_queries, grad_keys, grad_values], axis=2).reshape(row_count, 3 * width)


def layer_forward(inputs, gain_pair, layer_weights, attend):
    w_proj, w_mix, w_rise, w_fall = layer_weights
    normed = (inputs * rms_scale(inputs) * gain_pair[0]).astype(jnp.bfloat16)
    packed = matmul(normed, w_proj.reshape(w_proj.shape[0], -1)).astype(jnp.bfloat16)
    attended, saved = attend(packed)
    attended_low = attended.astype(jnp.bfloat16)
    resid = inputs + head_total(matmul(attended_low, w_mix))
    normed_mid = (resid * rms_scale(resid) * gain_pair[1]).astype(jnp.bfloat16)
    rise = matmul(normed_mid, w_rise)
    active = smooth_gate(rise).astype(jnp.bfloat16)
    result = resid + head_total(matmul(active, w_fall))
    return (result, (normed, packed, attended_low, saved, resid, normed_mid, rise, active))


def layer_backward(inputs, gain_pair, layer_weights, kept, grad_result, attend_back):
    w_proj, w_mix, w_rise, w_fall = layer_weights
    normed, packed, attended_low, saved, resid, normed_mid, rise, active = kept
    grad_fall_low = grad_result.astype(jnp.bfloat16)
    grad_fall_w = across_rows(active, grad_fall_low)
    grad_active = against_rows(grad_fall_low, w_fall)
    grad_rise = jax.vjp(smooth_gate, rise)[1](grad_active)[0].astype(jnp.bfloat16)
    grad_rise_w = across_rows(normed_mid, grad_rise)
    grad_mid = head_total(against_rows(grad_rise, w_rise))
    back_mid, gain_mid = rms_back(resid, gain_pair[1], grad_mid)
    grad_resid = grad_result + back_mid
    resid_low = grad_resid.astype(jnp.bfloat16)
    grad_mix_w = across_rows(attended_low, resid_low)
    grad_att = against_rows(resid_low, w_mix).astype(jnp.bfloat16)
    grad_packed = attend_back(packed, grad_att, saved).astype(jnp.bfloat16)
    flat_proj = w_proj.reshape(w_proj.shape[0], -1)
    grad_proj_w = across_rows(normed, grad_packed).reshape(w_proj.shape)
    grad_normed = head_total(against_rows(grad_packed, flat_proj))
    back_in, gain_in = rms_back(inputs, gain_pair[0], grad_normed)
    return (
        grad_resid + back_in,
        (grad_proj_w, grad_mix_w, grad_rise_w, grad_fall_w, jnp.stack([gain_in, gain_mid])),
    )


def plain_body(frames, codes, lengths, gains, w_qkv, w_out, w_up, w_down, table, cotangent):
    on_first = lax.axis_index("section") == 0
    head_count = w_qkv.shape[3] // HEAD
    layer_weights = (w_qkv[0], w_out[0], w_up[0], w_down[0])
    gains_here = gains[0]
    frame_count = frames.shape[1]
    query_pos = lax.axis_index("dp") * frame_count + jnp.arange(frame_count, dtype=jnp.int32)
    zero_grads = (
        jnp.zeros(w_qkv.shape[1:], jnp.float32),
        jnp.zeros(w_out.shape[1:], jnp.float32),
        jnp.zeros(w_up.shape[1:], jnp.float32),
        jnp.zeros(w_down.shape[1:], jnp.float32),
        jnp.zeros(gains.shape[1:], jnp.float32),
    )

    def global_forward_rows(frame_rows, slot_lengths):
        doc_ends = jnp.cumsum(slot_lengths)
        return (
            doc_ends,
            layer_forward(
                frame_rows.astype(jnp.float32),
                gains_here,
                layer_weights,
                lambda packed: frame_forward(packed, query_pos, doc_ends, head_count),
            ),
        )

    def global_step(carry, inputs):
        doc_ends, (result, kept) = global_forward_rows(inputs[0], inputs[1])
        return (carry, result.astype(jnp.bfloat16))

    global_low = lax.scan(global_step, jnp.zeros((), jnp.int32), (frames, lengths))[1]
    arrived = from_behind(global_low, "section", 1)
    books = jnp.arange(CODEBOOKS, dtype=jnp.int32)
    looked_up = table[books[None, None, :], codes]
    local_in = arrived.astype(jnp.float32)[:, :, None, :] + looked_up.astype(jnp.float32)
    local_rows = local_in.reshape(-1, local_in.shape[-1])
    local_result, local_kept = layer_forward(
        local_rows, gains_here, layer_weights, lambda packed: codebook_forward(packed, head_count)
    )
    grad_rows, local_grads = layer_backward(
        local_rows,
        gains_here,
        layer_weights,
        local_kept,
        cotangent.astype(jnp.float32).reshape(local_rows.shape),
        lambda packed, grad_att, saved: codebook_backward(packed, grad_att, saved, head_count),
    )
    grad_frame = jnp.sum(grad_rows.reshape(local_in.shape), axis=2)
    table_slots = (books[None, None, :] * table.shape[1] + codes).reshape(-1)
    table_term = jax.ops.segment_sum(
        grad_rows, table_slots, num_segments=table.shape[0] * table.shape[1]
    ).reshape(table.shape)
    local_low = local_result.astype(jnp.bfloat16).reshape(cotangent.shape)
    table_part = jnp.where(on_first, jnp.zeros(table.shape, jnp.float32), table_term)
    grad_frame = jnp.where(on_first, jnp.zeros(frames.shape, jnp.float32), grad_frame)
    grad_table = lax.psum_scatter(table_part, ("section", "dp"), scatter_dimension=1, tiled=True)
    grad_back, local_copy = from_behind((grad_frame.astype(jnp.bfloat16), local_low), "section", -1)

    def global_back(totals, inputs):
        frame_rows, slot_lengths, grad_low = inputs
        doc_ends, (result, kept) = global_forward_rows(frame_rows, slot_lengths)
        grad_in, grads = layer_backward(
            frame_rows.astype(jnp.float32),
            gains_here,
            layer_weights,
            kept,
            grad_low.astype(jnp.float32),
            lambda packed, grad_att, saved: frame_backward(
                packed, grad_att, saved, query_pos, doc_ends, head_count
            ),
        )
        return (jax.tree.map(jnp.add, totals, grads), grad_in)

    global_grads, grad_frames = lax.scan(global_back, zero_grads, (frames, lengths, grad_back))

    def pick(global_part, local_part):
        return jnp.where(on_first, global_part, local_part)

    proj_sum, mix_sum, rise_sum, fall_sum, gain_sum = jax.tree.map(pick, global_grads, local_grads)
    proj_share, mix_share, rise_share, fall_share, gain_share = (
        lax.psum_scatter(proj_sum, "dp", scatter_dimension=0, tiled=True),
        lax.psum_scatter(mix_sum, "dp", scatter_dimension=1, tiled=True),
        lax.psum_scatter(rise_sum, "dp", scatter_dimension=0, tiled=True),
        lax.psum_scatter(fall_sum, "dp", scatter_dimension=1, tiled=True),
        lax.psum_scatter(gain_sum, "dp", scatter_dimension=1, tiled=True),
    )
    global_out = jnp.where(on_first, global_low, arrived)
    local_out = jnp.where(on_first, local_copy, local_low)
    input_grads = jnp.where(on_first, grad_frames, grad_frame)[None]
    return (
        global_out,
        local_out,
        input_grads,
        proj_share[None],
        mix_share[None],
        rise_share[None],
        fall_share[None],
        gain_share[None],
        grad_table,
    )


def lasting(us):
    return pl.CostEstimate(flops=int(us * 1.1e9), bytes_accessed=int(us * 1e6), transcendentals=0)

f32=jnp.float32; bf=jnp.bfloat16

def mm(a,b): return jnp.dot(a,b,preferred_element_type=f32)
def mm_nt(a,b): return lax.dot_general(a,b,(((1,),(1,)),((),())),preferred_element_type=f32)

def gelu_both(v):
    c0 = 0.7978845608028654
    c1 = c0 * 0.044715
    sq = v * v
    half = 0.5 + 0.5 * jnp.tanh(v * (c0 + c1 * sq))
    act = v * half
    return act, half + act * (1.0 - half) * (2.0 * c0 + 6.0 * c1 * sq)


def local_kernel(g_ref, emb_ref, cot_ref, gao_ref, gax_ref, gains_ref, e_ref, et_ref,
                 pqo, pqx, woo, wox, wuo, wux,
                 resid_o, acto_o, griso_o, gpo_o, actx_o, send_o, dx_o, gframe_o, gg_o,
                 q_s, k_s, v_s, p_s, gp_s, prod_s, wide_s, r_s, gm_s, gatt_s):
    F=g_ref.shape[0]; R=3*F; D=g_ref.shape[1]; H2=D//2
    W=acto_o.shape[2]
    grisx_o=send_o.at[:,:,0:W]
    mid_o,glow_o,normed_o=(send_o.at[:,:,W+j*D:W+(j+1)*D] for j in range(3))
    gpx_o=[send_o.at[:,:,W+3*D+j*H2:W+3*D+(j+1)*H2] for j in range(4)]
    step=pl.program_id(0)
    gain0=gains_ref[0:1,:]; gain1=gains_ref[1:2,:]
    g=g_ref[...].astype(f32)
    scr=(q_s,k_s,v_s)
    r0s=[]
    for c in range(3):
        x=g+emb_ref[c].astype(f32)
        r0=lax.rsqrt(jnp.mean(x*x,axis=-1,keepdims=True)+eps)
        r0s.append(r0)
        normed_o[c]=(x*r0*gain0).astype(bf)
    normed=normed_o[...].reshape(R,D)
    for j in range(3):
        scr[j][:,0:H2]=mm(normed,pqo[j]).astype(bf)
        scr[j][:,H2:D]=mm(normed,pqx[j]).astype(bf)
    pairs=[(c,c2) for c in range(3) for c2 in range(c+1)]
    rows=lambda ref,c: ref[c*F:(c+1)*F,:]
    for n,(c,c2) in enumerate(pairs):
        prod_s[n*F:(n+1)*F,:]=(rows(q_s,c).astype(f32)*rows(k_s,c2).astype(f32)).astype(bf)
    p_s[...]=mm(prod_s[...],e_ref[...])*0.125
    for c in range(3):
        own=[n for n,pr in enumerate(pairs) if pr[0]==c]
        ss=[rows(p_s,n) for n in own]
        top=functools.reduce(jnp.maximum,ss)
        ws=[jnp.exp(s-top) for s in ss]
        inv=1.0/functools.reduce(jnp.add,ws)
        for n,w in zip(own,ws): p_s[n*F:(n+1)*F,:]=w*inv
    wide_s[...]=mm(p_s[...].astype(bf),et_ref[...]).astype(bf)
    for c in range(3):
        acc=functools.reduce(jnp.add,[rows(wide_s,n).astype(f32)*rows(v_s,pr[1]).astype(f32) for n,pr in enumerate(pairs) if pr[0]==c])
        att=acc.astype(bf)
        gpo_o[0,c]=att[:,0:H2]; gpx_o[0][c]=att[:,H2:D]
    xs=(g_ref[...].astype(f32)[None]+emb_ref[...].astype(f32)).reshape(R,D)
    resid=xs+mm(gpo_o[0].reshape(R,H2),woo[...])+mm(gpx_o[0][...].reshape(R,H2),wox[...])
    r1=lax.rsqrt(jnp.mean(resid*resid,axis=-1,keepdims=True)+eps)
    resid_o[...]=resid.reshape(3,F,D)
    nm=(resid*r1*gain1).astype(bf)
    mid_o[...]=nm.reshape(3,F,D)
    ch=512
    gm=None
    for (wu,act_o,gris_o,ga_ref) in ((wuo,acto_o,griso_o,gao_ref),(wux,actx_o,grisx_o,gax_ref)):
        for j in range(wu.shape[1]//ch):
            sl=slice(j*ch,(j+1)*ch)
            w=wu[:,sl]
            act,gr=gelu_both(mm(nm,w))
            act_o[:,:,sl]=act.astype(bf).reshape(3,F,ch)
            gl=(ga_ref[:,:,sl].reshape(R,ch).astype(f32)*gr).astype(bf)
            gris_o[:,:,sl]=gl.reshape(3,F,ch)
            t=mm_nt(gl,w)
            if gm is None:
                gm_s[...]=t; gm=1
            else:
                gm_s[...]+=t
    gmid=gm_s[...]
    n1=resid_o[...].reshape(R,D)*r1
    u=gmid*gain1
    gres=cot_ref[...].reshape(R,D).astype(f32)+r1*(u-n1*jnp.mean(u*n1,axis=-1,keepdims=True))
    gsum1=jnp.sum(gmid*n1,axis=0,keepdims=True)
    r_s[...]=gres
    glow=gres.astype(bf)
    glow_o[...]=glow.reshape(3,F,D)
    gatt_s[:,0:H2]=mm_nt(glow,woo[...]).astype(bf)
    gatt_s[:,H2:D]=mm_nt(glow,wox[...]).astype(bf)
    def add(a,b): return b if a is None else a+b
    for n,(c,c2) in enumerate(pairs):
        prod_s[n*F:(n+1)*F,:]=(rows(gatt_s,c).astype(f32)*rows(v_s,c2).astype(f32)).astype(bf)
    gp_s[...]=mm(prod_s[...],e_ref[...])
    for c in range(3):
        own=[n for n,pr in enumerate(pairs) if pr[0]==c]
        ps=[rows(p_s,n) for n in own]
        gps=[rows(gp_s,n) for n in own]
        spread=functools.reduce(jnp.add,[p*gp for p,gp in zip(ps,gps)])
        for n,p,gp in zip(own,ps,gps): gp_s[n*F:(n+1)*F,:]=p*(gp-spread)*0.125
    prod_s[...]=mm(gp_s[...].astype(bf),et_ref[...]).astype(bf)
    for c in range(3):
        take=lambda which,left,right,at: functools.reduce(jnp.add,[rows(left,n).astype(f32)*rows(right,pr[1-which]).astype(f32) for n,pr in enumerate(pairs) if pr[which]==at]).astype(bf)
        for j,a in ((1,take(0,prod_s,k_s,c)),(2,take(1,prod_s,q_s,c)),(3,take(1,wide_s,gatt_s,c))):
            gpo_o[j,c]=a[:,0:H2]; gpx_o[j][c]=a[:,H2:D]
    gn=None
    for j in range(3):
        gn=add(gn,mm_nt(gpo_o[j+1].reshape(R,H2),pqo[j]))
        gn=gn+mm_nt(gpx_o[j+1][...].reshape(R,H2),pqx[j])
    gm_s[...]=gn
    tot=None; gsum0=None
    for c in range(3):
        gn=gm_s[c*F:(c+1)*F,:]
        n0=(g_ref[...].astype(f32)+emb_ref[c].astype(f32))*r0s[c]
        w=gn*gain0
        dx=r_s[c*F:(c+1)*F,:]+r0s[c]*(w-n0*jnp.mean(w*n0,axis=-1,keepdims=True))
        gsum0=add(gsum0,jnp.sum(gn*n0,axis=0,keepdims=True))
        dx_o[c]=dx.astype(bf)
        tot=add(tot,dx)
    gframe_o[...]=tot
    @pl.when(step==0)
    def _(): gg_o[...]=jnp.zeros_like(gg_o)
    gg_o[0:1,:]+=gsum0
    gg_o[1:2,:]+=gsum1

def local_skip(at_ref,*refs):
    @pl.when(at_ref[0]==1)
    def _():
        local_kernel(*refs)

def local_call(at,g,emb,cot,gao,gax,gains,pqo,pqx,woo,wox,wuo,wux,tile=128):
    N,D=g.shape; H2=D//2; FH=wuo.shape[1]; F=tile
    E=(jnp.arange(D)[:,None]//HEAD==jnp.arange(128)[None,:]).astype(bf)
    ET=E.T
    c3=lambda w: pl.BlockSpec((3,F,w),lambda i,s:(0,i,0))
    whole=lambda shp: pl.BlockSpec(shp,lambda i,s:(0,)*len(shp),pipeline_mode=pl.Buffered(1))
    sd=jax.ShapeDtypeStruct
    S=FH+3*D+4*H2
    out_shape=(sd((3,N,D),f32),sd((3,N,FH),bf),sd((3,N,FH),bf),sd((4,3,N,H2),bf),sd((3,N,FH),bf),sd((3,N,S),bf),sd((3,N,D),bf),sd((N,D),f32),sd((2,D),f32))
    gp=pl.BlockSpec((4,3,F,H2),lambda i,s:(0,0,i,0))
    return pl.pallas_call(local_skip, grid_spec=pltpu.PrefetchScalarGridSpec(num_scalar_prefetch=1,grid=(N//F,),
      in_specs=[pl.BlockSpec((F,D),lambda i,s:(i,0)),c3(D),c3(D),c3(FH),c3(FH),whole((2,D)),whole(E.shape),whole(ET.shape),
        whole(pqo.shape),whole(pqx.shape),whole(woo.shape),whole(wox.shape),whole(wuo.shape),whole(wux.shape)],
      out_specs=(c3(D),c3(FH),c3(FH),gp,c3(FH),c3(S),c3(D),pl.BlockSpec((F,D),lambda i,s:(i,0)),pl.BlockSpec((2,D),lambda i,s:(0,0))),
      scratch_shapes=[pltpu.VMEM((3*F,D),bf)]*3+[pltpu.VMEM((6*F,128),f32)]*2+[pltpu.VMEM((6*F,D),bf)]*2+[pltpu.VMEM((3*F,D),f32),pltpu.VMEM((3*F,D),f32),pltpu.VMEM((3*F,D),bf)]),
      out_shape=out_shape,
      compiler_params=pltpu.CompilerParams(vmem_limit_bytes=65400 * 1024),
      cost_estimate=lasting(57),
      name="local_layer",
    )(at,g,emb,cot,gao,gax,gains,E,ET,pqo,pqx,woo,wox,wuo,wux)

def attend_kernel(at_ref, xo_ref, xs_ref, xc_ref, xb_ref, gain_ref, proj_ref, qid_ref, kid_ref,
                  normed_ref, q_ref, k_ref, v_ref, near_ref, off_ref):
    step = pl.program_id(0)
    rows = xo_ref.shape[0]

    @pl.when((at_ref[0] == 0) & (step == 0))
    def _():
        for j, x_ref in enumerate((xo_ref, xs_ref, xc_ref, xb_ref)):
            part = slice(j * rows, (j + 1) * rows)
            x = x_ref[...].astype(f32)
            scale = lax.rsqrt(jnp.mean(x * x, axis=-1, keepdims=True) + eps)
            normed_ref[part, :] = (x * scale * gain_ref[0:1, :]).astype(bf)
        for j, ref in enumerate((q_ref, k_ref, v_ref)):
            ref[...] = mm(normed_ref[...], proj_ref[j]).astype(bf)

    @pl.when(at_ref[0] == 0)
    def _():
        bias = jnp.where(
            ((qid_ref[:, 1:2] == kid_ref[1:2, :]) & (kid_ref[0:1, :] <= qid_ref[:, 0:1]))
            | (kid_ref[0:1, :] == qid_ref[:, 0:1]),
            0.0,
            far,
        )
        lane = lax.broadcasted_iota(jnp.int32, (1, 2 * HEAD), 1) // HEAD
        here_rows = pl.ds(pl.multiple_of(step * rows, rows), rows)
        for pair in range(q_ref.shape[1] // (2 * HEAD)):
            cols = slice(pair * 2 * HEAD, (pair + 1) * 2 * HEAD)
            q, k, v = q_ref[here_rows, cols], k_ref[:, cols], v_ref[:, cols]
            total = None
            for side in range(2):
                here = lane == side
                scores = mm_nt(jnp.where(here, q * HEAD ** (-0.5), jnp.zeros_like(q)), k) + bias
                top = jnp.max(scores, axis=-1, keepdims=True)
                weights = jnp.exp(scores - top)
                mass = jnp.sum(weights, axis=-1, keepdims=True)
                probs = (weights * (1.0 / mass)).astype(bf)
                term = mm(probs, jnp.where(here, v, jnp.zeros_like(v)))
                total = term if total is None else total + term
            for odd, ref in ((0, near_ref), (1, off_ref)):

                @pl.when(step % 2 == odd)
                def _():
                    ref[0, :, cols] = total.astype(bf)


def attend_call(at, blocks, gains, proj, qid, kid):
    rows, width = blocks[0].shape
    cols = proj.shape[2] // 2
    total = 4 * rows
    whole = lambda shape: pl.BlockSpec(shape, lambda i, s: (0,) * len(shape))
    sd = jax.ShapeDtypeStruct
    half = pl.BlockSpec((1, rows, cols), lambda i, s: (i // 2, 0, 0))
    return pl.pallas_call(
        attend_kernel,
        grid_spec=pltpu.PrefetchScalarGridSpec(
            num_scalar_prefetch=1,
            grid=(4,),
            in_specs=[whole((rows, width))] * 4
            + [
                whole(gains.shape),
                pl.BlockSpec((3, width, cols), lambda i, s: (0, 0, s[2])),
                pl.BlockSpec((rows, 2), lambda i, s: (i, 0)),
                whole(kid.shape),
            ],
            out_specs=(whole((total, width)), *[whole((total, cols))] * 3, half, half),
        ),
        out_shape=(sd((total, width), bf), *[sd((total, cols), bf)] * 3, *[sd((2, rows, cols), bf)] * 2),
        compiler_params=pltpu.CompilerParams(vmem_limit_bytes=60 * 1024 * 1024),
        cost_estimate=lasting(18),
        name="frame_attention",
    )(at, *blocks, gains, proj, qid, kid)


def attend_back_kernel(at_ref, q_ref, k_ref, v_ref, g_ref, qid_ref, kid_ref, gq_ref, gk_ref, gv_ref, ks_ref, vs_ref):
    @pl.when(at_ref[0] == 0)
    def _():
        step = pl.program_id(0)

        @pl.when(step == 0)
        def _():
            ks_ref[...] = jnp.zeros_like(ks_ref)
            vs_ref[...] = jnp.zeros_like(vs_ref)

        bias = jnp.where(
            ((qid_ref[:, 1:2] == kid_ref[1:2, :]) & (kid_ref[0:1, :] <= qid_ref[:, 0:1]))
            | (kid_ref[0:1, :] == qid_ref[:, 0:1]),
            0.0,
            far,
        )
        lane = lax.broadcasted_iota(jnp.int32, (1, 2 * HEAD), 1) // HEAD
        for pair in range(q_ref.shape[1] // (2 * HEAD)):
            cols = slice(pair * 2 * HEAD, (pair + 1) * 2 * HEAD)
            q, k, v, g = q_ref[:, cols], k_ref[:, cols], v_ref[:, cols], g_ref[:, cols]
            gq = None
            for side in range(2):
                here = lane == side
                qh = jnp.where(here, q, jnp.zeros_like(q))
                gh = jnp.where(here, g, jnp.zeros_like(g))
                kh = jnp.where(here, k, jnp.zeros_like(k))
                scores = mm_nt(qh * HEAD ** (-0.5), k) + bias
                top = jnp.max(scores, axis=-1, keepdims=True)
                weights = jnp.exp(scores - top)
                mass = jnp.sum(weights, axis=-1, keepdims=True)
                probs = weights * (1.0 / mass)
                grad_probs = mm_nt(gh, v)
                spread = jnp.sum(probs * grad_probs, axis=-1, keepdims=True)
                gs = (probs * (grad_probs - spread) * HEAD ** (-0.5)).astype(bf)
                term = mm(gs, kh)
                gq = term if gq is None else gq + term
                ks_ref[:, cols] += across_rows(gs, qh)
                vs_ref[:, cols] += across_rows(probs.astype(bf), gh)
            gq_ref[:, cols] = gq.astype(bf)

        @pl.when(step == pl.num_programs(0) - 1)
        def _():
            gk_ref[...] = ks_ref[...].astype(bf)
            gv_ref[...] = vs_ref[...].astype(bf)


def attend_back_call(at, q, k, v, g, qid, kid, rows):
    total, width = q.shape
    part = pl.BlockSpec((rows, width), lambda i, s: (i, 0))
    whole = pl.BlockSpec((total, width), lambda i, s: (0, 0))
    shape = jax.ShapeDtypeStruct((total, width), bf)
    return pl.pallas_call(
        attend_back_kernel,
        grid_spec=pltpu.PrefetchScalarGridSpec(
            num_scalar_prefetch=1,
            grid=(total // rows,),
            in_specs=[part, whole, whole, part, pl.BlockSpec((rows, 2), lambda i, s: (i, 0)), pl.BlockSpec(kid.shape, lambda i, s: (0, 0))],
            out_specs=(part, whole, whole),
            scratch_shapes=[pltpu.VMEM((total, width), f32)] * 2,
        ),
        out_shape=(shape, shape, shape),
        compiler_params=pltpu.CompilerParams(vmem_limit_bytes=60 * 1024 * 1024),
        cost_estimate=lasting(0.01),
        name="frame_attention_back",
    )(at, q, k, v, g, qid, kid)


def front_kernel(at_ref, x_ref, near_ref, off_ref, core_ref, gain_ref, oo_ref, ox_ref, uo_ref, ux_ref, do_ref, dx_ref,
                 resid_ref, mid_ref, act_o, act_x, slope_o, slope_x, out_ref, total_ref):
    @pl.when(at_ref[0] == 0)
    def _():
        step = pl.program_id(0)
        turn = pl.num_programs(0) // 2

        @pl.when(step == 0)
        def _():
            cols = near_ref.shape[2]
            resid = x_ref[...].astype(f32)
            for flip, part, out in ((0, near_ref, oo_ref), (1, off_ref, oo_ref), (0, core_ref, ox_ref), (1, core_ref, ox_ref)):
                spot = pl.ds(pl.multiple_of((at_ref[2] ^ flip) * cols, cols), cols)
                resid = resid + mm(part[flip if part is core_ref else 0], out[spot, :])
            resid_ref[...] = resid
            scale = lax.rsqrt(jnp.mean(resid * resid, axis=-1, keepdims=True) + eps)
            mid_ref[...] = (resid * scale * gain_ref[1:2, :]).astype(bf)
            total_ref[...] = resid

        def part(up, down, act_ref, slope_ref):
            act, slope = gelu_both(mm(mid_ref[...], up[...]))
            act = act.astype(bf)
            act_ref[...] = act
            slope_ref[...] = slope.astype(bf)
            total_ref[...] += mm(act, down[...])

        @pl.when(step < turn)
        def _():
            part(uo_ref, do_ref, act_o, slope_o)

        @pl.when(step >= turn)
        def _():
            part(ux_ref, dx_ref, act_x, slope_x)

        @pl.when(step == pl.num_programs(0) - 1)
        def _():
            out_ref[...] = total_ref[...].astype(bf)


def halves_specs(turn, chunk, width, rows):
    first = lambda i, s: jnp.minimum(i, turn - 1) * (1 - s[0])
    later = lambda i, s: jnp.maximum(i - turn, 0) * (1 - s[0])
    ups = [pl.BlockSpec((width, chunk), lambda i, s, f=f: (0, f(i, s))) for f in (first, later)]
    downs = [pl.BlockSpec((chunk, width), lambda i, s, f=f: (f(i, s), 0)) for f in (first, later)]
    cols = [pl.BlockSpec((rows, chunk), lambda i, s, f=f: (0, f(i, s))) for f in (first, later)]
    return ups, downs, cols


def front_call(at, x, near, off, from_core, gains, out_own, out_oth, up_own, up_oth, down_own, down_oth, chunk=1024):
    rows, width = x.shape
    hidden = up_own.shape[1]
    turn = hidden // chunk
    ups, downs, cols = halves_specs(turn, chunk, width, rows)
    whole = lambda a: pl.BlockSpec(a.shape, lambda i, s: (0,) * a.ndim)
    sd = jax.ShapeDtypeStruct
    full = pl.BlockSpec((rows, width), lambda i, s: (0, 0))
    hid = sd((rows, hidden), bf)
    return pl.pallas_call(
        front_kernel,
        grid_spec=pltpu.PrefetchScalarGridSpec(
            num_scalar_prefetch=1,
            grid=(2 * turn,),
            in_specs=[full, whole(near), whole(off), whole(from_core), whole(gains), whole(out_own), whole(out_oth), *ups, *downs],
            out_specs=(full, full, cols[0], cols[1], cols[0], cols[1], full),
            scratch_shapes=[pltpu.VMEM((rows, width), f32)],
        ),
        out_shape=(sd((rows, width), f32), sd((rows, width), bf), hid, hid, hid, hid, sd((rows, width), bf)),
        compiler_params=pltpu.CompilerParams(vmem_limit_bytes=60 * 1024 * 1024),
        cost_estimate=lasting(15),
        name="global_forward",
    )(at, x, near, off, from_core, gains, out_own, out_oth, up_own, up_oth, down_own, down_oth)


def back_kernel(at_ref, g_ref, resid_ref, gain_ref, so_ref, sx_ref, uo_ref, ux_ref, do_ref, dx_ref,
                rise_o, rise_x, grad_ref, low_ref, gsum_ref, total_ref):
    @pl.when(at_ref[0] == 0)
    def _():
        step = pl.program_id(0)
        turn = pl.num_programs(0) // 2

        def part(up, down, slope_ref, rise_ref):
            rise = (mm_nt(g_ref[...], down[...]) * slope_ref[...].astype(f32)).astype(bf)
            rise_ref[...] = rise
            return mm_nt(rise, up[...])

        @pl.when(step == 0)
        def _():
            total_ref[...] = part(uo_ref, do_ref, so_ref, rise_o)

        @pl.when((step > 0) & (step < turn))
        def _():
            total_ref[...] += part(uo_ref, do_ref, so_ref, rise_o)

        @pl.when(step >= turn)
        def _():
            total_ref[...] += part(ux_ref, dx_ref, sx_ref, rise_x)

        @pl.when(step == pl.num_programs(0) - 1)
        def _():
            resid = resid_ref[...]
            scale = lax.rsqrt(jnp.mean(resid * resid, axis=-1, keepdims=True) + eps)
            normal = resid * scale
            total = total_ref[...]
            unit = total * gain_ref[1:2, :]
            grad = g_ref[...].astype(f32) + scale * (unit - normal * jnp.mean(unit * normal, axis=-1, keepdims=True))
            grad_ref[...] = grad
            low_ref[...] = grad.astype(bf)
            gsum_ref[...] = jnp.sum(total * normal, axis=0, keepdims=True)


def back_call(at, g, resid, gains, slope_own, slope_oth, up_own, up_oth, down_own, down_oth, chunk=1024):
    rows, width = g.shape
    hidden = up_own.shape[1]
    turn = hidden // chunk
    ups, downs, cols = halves_specs(turn, chunk, width, rows)
    sd = jax.ShapeDtypeStruct
    full = pl.BlockSpec((rows, width), lambda i, s: (0, 0))
    hid = sd((rows, hidden), bf)
    line = pl.BlockSpec((1, width), lambda i, s: (0, 0))
    return pl.pallas_call(
        back_kernel,
        grid_spec=pltpu.PrefetchScalarGridSpec(
            num_scalar_prefetch=1,
            grid=(2 * turn,),
            in_specs=[full, full, pl.BlockSpec(gains.shape, lambda i, s: (0, 0)), *cols, *ups, *downs],
            out_specs=(*cols, full, full, line),
            scratch_shapes=[pltpu.VMEM((rows, width), f32)],
        ),
        out_shape=(hid, hid, sd((rows, width), f32), sd((rows, width), bf), sd((1, width), f32)),
        compiler_params=pltpu.CompilerParams(vmem_limit_bytes=60 * 1024 * 1024),
        cost_estimate=lasting(13),
        name="global_backward",
    )(at, g, resid, gains, slope_own, slope_oth, up_own, up_oth, down_own, down_oth)


def split_sides(total, side, mine_ref, theirs_ref, at):
    half = total.shape[0] // 2
    top, bottom = total[:half].astype(bf), total[half:].astype(bf)
    mine_ref[at] = jnp.where(side == 0, top, bottom)
    theirs_ref[at] = jnp.where(side == 0, bottom, top)


def deal(total_ref, at_ref, mine_ref, theirs_ref, plane_first):
    piece = total_ref.shape[0] // 8
    for jz in range(4):
        for jy in range(2):
            place = (at_ref[1] ^ jz) * 2 + (at_ref[2] ^ jy)
            rows = pl.ds(pl.multiple_of(place * piece, piece), piece)
            low, high = jz % 2, jz // 2
            part = total_ref[rows, :].astype(bf)
            if plane_first:
                (theirs_ref if low else mine_ref)[high, jy] = part
            else:
                (theirs_ref if jy else mine_ref)[low * 2 + high] = part


def weight_kernel(at_ref, left, left_in, right, right_in, *refs, here, plane_first):
    other, (mine_ref, theirs_ref, total_ref, turned, turned_in) = refs[:-5], refs[-5:]

    if other:

        @pl.when(at_ref[0] != here)
        def _():
            theirs_ref[...] = other[0][...]

    @pl.when(at_ref[0] == here)
    def _():
        @pl.when(pl.program_id(0) == 0)
        def _():
            turned[...] = left[...].T
            turned_in[...] = left_in[...].T

        total_ref[...] = mm(turned[...], right[...]) + mm(turned_in[...], right_in[...])
        deal(total_ref, at_ref, mine_ref, theirs_ref, plane_first)


def weight_call(at, here, four, skip, plane_first, name, us, width, cols, other=None, chunk=512):
    piece = width // 8
    now = lambda i, s: jnp.where(s[0] == here, i, 0)
    whole = [
        pl.BlockSpec((a.shape[0], width), lambda i, s, c=c: (0, c), pipeline_mode=pl.Buffered(1))
        for a, c in zip(four[:2], skip)
    ]
    part = [
        pl.BlockSpec((a.shape[0], chunk), lambda i, s, c=c: (0, now(i, s) + c)) for a, c in zip(four[2:], skip[2:])
    ]
    if plane_first:
        shape = jax.ShapeDtypeStruct((2, 2, piece, cols), bf)
    else:
        shape = jax.ShapeDtypeStruct((4, piece, cols), bf)
    block = lambda at_col: pl.BlockSpec(
        shape.shape[:-1] + (chunk,), lambda i, s: (0,) * (len(shape.shape) - 1) + (at_col(i, s),)
    )
    passed = () if other is None else (other,)
    theirs = block(now) if other is None else block(lambda i, s: i)
    return pl.pallas_call(
        functools.partial(weight_kernel, here=here, plane_first=plane_first),
        grid_spec=pltpu.PrefetchScalarGridSpec(
            num_scalar_prefetch=1,
            grid=(cols // chunk,),
            in_specs=whole + part + [block(lambda i, s: jnp.where(s[0] == here, 0, i)) for _ in passed],
            out_specs=(block(now), theirs),
            scratch_shapes=[pltpu.VMEM((width, chunk), f32)] + [pltpu.VMEM((width, a.shape[0]), bf) for a in four[:2]],
        ),
        out_shape=(shape, shape),
        compiler_params=pltpu.CompilerParams(vmem_limit_bytes=60 * 1024 * 1024),
        cost_estimate=lasting(us),
        name=name,
    )(at, *four, *passed)


def rest_kernel(at_ref, *refs, here):
    pairs = (len(refs) - 3) // 4
    lows, normeds, rights = (refs[j * pairs : (j + 1) * pairs] for j in range(3))
    mine_ref, theirs_ref, total_ref = refs[3 * pairs : 3 * pairs + 3]
    turned = refs[3 * pairs + 3 :]
    step = pl.program_id(0)
    piece = total_ref.shape[0] // 8

    @pl.when(at_ref[0] == here)
    def _():
        for when, lefts in ((0, lows), (1, normeds)):

            @pl.when(step == when)
            def _():
                for left, turn in zip(lefts, turned):
                    turn[...] = left[...].T

        total = None
        for turn, right in zip(turned, rights):
            term = mm(turn[...], right[0] if len(right.shape) == 3 else right[...])
            total = term if total is None else total + term
        total_ref[...] = total
        for jz in range(4):
            for jy in range(2):
                place = (at_ref[1] ^ jz) * 2 + (at_ref[2] ^ jy)
                rows = pl.ds(pl.multiple_of(place * piece, piece), piece)
                for h in range(mine_ref.shape[2]):
                    cols = slice(h * mine_ref.shape[4], (h + 1) * mine_ref.shape[4])
                    (theirs_ref if jy else mine_ref)[jz % 2 * 2 + jz // 2, 0, h] = total_ref[rows, cols].astype(bf)


def rest_call(at, here, lows, normeds, rights, name, us, width):
    piece = width // 8
    count = 4
    narrow = width // 4
    size = rights[0][0].shape[2]
    whole = lambda pair: pl.BlockSpec((pair[0].shape[0], width), lambda i, s: (0, pair[1]), pipeline_mode=pl.Buffered(1))

    def part(pair):
        a, c = pair
        now = lambda i, s: jnp.where(s[0] == here, i, 0)
        if a.ndim == 3:
            return pl.BlockSpec((1,) + a.shape[1:], lambda i, s: (now(i, s), 0, 0))
        return pl.BlockSpec((a.shape[0], size), lambda i, s: (0, c + now(i, s)))

    halves = size // narrow
    shape = jax.ShapeDtypeStruct((4, count, halves, piece, narrow), bf)
    out = pl.BlockSpec((4, 1, halves, piece, narrow), lambda i, s: (0, jnp.where(s[0] == here, i, 0), 0, 0, 0))
    return pl.pallas_call(
        functools.partial(rest_kernel, here=here),
        grid_spec=pltpu.PrefetchScalarGridSpec(
            num_scalar_prefetch=1,
            grid=(count,),
            in_specs=[*map(whole, lows), *map(whole, normeds), *map(part, rights)],
            out_specs=(out, out),
            scratch_shapes=[pltpu.VMEM((width, size), f32)] + [pltpu.VMEM((width, a.shape[0]), bf) for a, _ in lows],
        ),
        out_shape=(shape, shape),
        compiler_params=pltpu.CompilerParams(vmem_limit_bytes=60 * 1024 * 1024),
        cost_estimate=lasting(us),
        name=name,
    )(at, *(a for a, _ in (*lows, *normeds, *rights)))


def fall_kernel(at_ref, resid_ref, ao_ref, ax_ref, do_ref, dx_ref, out_ref, total_ref):
    step = pl.program_id(0)
    turn = pl.num_programs(0) // 2
    books, planes, half = out_ref.shape[1], out_ref.shape[0], out_ref.shape[2]

    @pl.when(at_ref[0] == 1)
    def _():
        @pl.when(step == 0)
        def _():
            total_ref[...] = resid_ref[...]

        @pl.when(step < turn)
        def _():
            total_ref[...] += mm(ao_ref[...], do_ref[...])

        @pl.when(step >= turn)
        def _():
            total_ref[...] += mm(ax_ref[...], dx_ref[...])

        @pl.when(step == pl.num_programs(0) - 1)
        def _():
            for c in range(books):
                for z in range(planes):
                    first = (c * planes + z) * half
                    out_ref[z, c] = total_ref[first : first + half, :].astype(bf)


def fall_call(at, resid, act_own, act_oth, down_own, down_oth, planes, books, chunk=1024):
    rows, width = resid.shape
    turn = down_own.shape[0] // chunk
    first = lambda i, s: jnp.minimum(i, turn - 1) * s[0]
    later = lambda i, s: jnp.maximum(i - turn, 0) * s[0]
    col = lambda f: pl.BlockSpec((rows, chunk), lambda i, s: (0, f(i, s)))
    row = lambda f: pl.BlockSpec((chunk, width), lambda i, s: (f(i, s), 0))
    shape = (planes, books, rows // planes // books, width)
    return pl.pallas_call(
        fall_kernel,
        grid_spec=pltpu.PrefetchScalarGridSpec(
            num_scalar_prefetch=1,
            grid=(2 * turn,),
            in_specs=[pl.BlockSpec((rows, width), lambda i, s: (0, 0), pipeline_mode=pl.Buffered(1)), col(first), col(later), row(first), row(later)],
            out_specs=pl.BlockSpec(shape, lambda i, s: (0, 0, 0, 0)),
            scratch_shapes=[pltpu.VMEM((rows, width), f32)],
        ),
        out_shape=jax.ShapeDtypeStruct(shape, bf),
        compiler_params=pltpu.CompilerParams(vmem_limit_bytes=60 * 1024 * 1024),
        cost_estimate=lasting(0.01),
        name="local_output",
    )(at, resid, act_own, act_oth, down_own, down_oth)


def table_kernel(at_ref, code_ref, code_in_ref, own_ref, got_ref, low_ref, high_ref, total_ref):
    entries = total_ref.shape[0]
    slots = lax.broadcasted_iota(jnp.int32, (entries, code_ref.shape[2]), 0)
    piece = low_ref.shape[3]

    @pl.when(at_ref[0] == 1)
    def _():
        hot = (slots == code_ref[0]).astype(f32).astype(bf)
        hot_in = (slots == code_in_ref[0]).astype(f32).astype(bf)
        total_ref[...] = mm(hot, own_ref[0]) + mm(hot_in, got_ref[0])
        for jz in range(4):
            for jy in range(2):
                place = (at_ref[1] ^ jz) * 2 + (at_ref[2] ^ jy)
                spot = (jz % 2) * 2 + jz // 2
                for ref, base in ((low_ref, 0), (high_ref, entries // 2)):
                    rows = pl.ds(pl.multiple_of(base + place * piece, piece), piece)
                    ref[jy, spot, 0] = total_ref[rows, :].astype(bf)


def table_call(at, codes, codes_in, own, got, entries):
    books, rows = codes.shape
    width = own.shape[2]
    line = pl.BlockSpec((1, 1, rows), lambda c, s: (c, 0, 0))
    block = pl.BlockSpec((1, rows, width), lambda c, s: (c, 0, 0))
    shape = (2, 4, books, entries // 16, width)
    out = pl.BlockSpec((2, 4, 1, entries // 16, width), lambda c, s: (0, 0, c, 0, 0))
    return pl.pallas_call(
        table_kernel,
        grid_spec=pltpu.PrefetchScalarGridSpec(
            num_scalar_prefetch=1,
            grid=(books,),
            in_specs=[line, line, block, block],
            out_specs=(out, out),
            scratch_shapes=[pltpu.VMEM((entries, width), f32)],
        ),
        out_shape=(jax.ShapeDtypeStruct(shape, bf),) * 2,
        compiler_params=pltpu.CompilerParams(vmem_limit_bytes=60 * 1024 * 1024),
        cost_estimate=lasting(4),
        name="table_gradient",
    )(at, codes[:, None, :], codes_in[:, None, :], own, got)


def prepare_kernel(at_ref, code_ref, cot_ref, do_ref, dx_ref, table_ref, look_ref, po_ref, px_ref):
    step = pl.program_id(0)
    turn = pl.num_programs(0) // 2
    books, rows, chunk = po_ref.shape

    @pl.when(at_ref[0] == 1)
    def _():
        @pl.when(step < look_ref.shape[0])
        def _():
            slots = lax.broadcasted_iota(jnp.int32, (rows, table_ref.shape[1]), 1)
            hot = (slots == code_ref[jnp.minimum(step, look_ref.shape[0] - 1)]).astype(f32).astype(bf)
            look_ref[jnp.minimum(step, look_ref.shape[0] - 1)] = mm(hot, table_ref[0]).astype(bf)

        @pl.when(step < turn)
        def _():
            po_ref[...] = mm_nt(cot_ref[...], do_ref[...]).astype(bf).reshape(books, rows, chunk)

        @pl.when(step >= turn)
        def _():
            px_ref[...] = mm_nt(cot_ref[...], dx_ref[...]).astype(bf).reshape(books, rows, chunk)


def prepare_call(at, codes, cot, down_own, down_oth, table, chunk=512):
    books, rows = codes.shape
    width = cot.shape[1]
    hidden = down_own.shape[0]
    turn = hidden // chunk
    first = lambda i, s: jnp.minimum(i, turn - 1) * s[0]
    later = lambda i, s: jnp.maximum(i - turn, 0) * s[0]
    down = lambda f: pl.BlockSpec((chunk, width), lambda i, s: (f(i, s), 0))
    out = lambda f: pl.BlockSpec((books, rows, chunk), lambda i, s: (0, 0, f(i, s)))
    sd = jax.ShapeDtypeStruct
    return pl.pallas_call(
        prepare_kernel,
        grid_spec=pltpu.PrefetchScalarGridSpec(
            num_scalar_prefetch=1,
            grid=(2 * turn,),
            in_specs=[
                pl.BlockSpec((books, rows, 1), lambda i, s: (0, 0, 0)),
                pl.BlockSpec(cot.shape, lambda i, s: (0, 0)),
                down(first),
                down(later),
                pl.BlockSpec((1,) + table.shape[1:], lambda i, s: (jnp.minimum(i, books - 1) * s[0], 0, 0)),
            ],
            out_specs=(pl.BlockSpec((books, rows, width), lambda i, s: (0, 0, 0)), out(first), out(later)),
        ),
        out_shape=(sd((books, rows, width), bf), sd((books, rows, hidden), bf), sd((books, rows, hidden), bf)),
        compiler_params=pltpu.CompilerParams(vmem_limit_bytes=60 * 1024 * 1024),
        cost_estimate=lasting(5),
        name="local_prepare",
    )(at, codes[:, :, None], cot, down_own, down_oth, table)


def fence(*groups):
    return lax.optimization_barrier(groups)


def body(frames, codes, lengths, gains, w_qkv, w_out, w_up, w_down, table, cotangent):
    batches, share, width = frames.shape
    members = lax.axis_size("dp") // batches
    if (
        lax.axis_size("section") != 2
        or lax.axis_size("tensor") != 2
        or members != 2
        or lax.axis_size("dp") != 2 * batches
        or batches & (batches - 1)
        or share % 32
        or table.shape[1] != width
    ):
        return plain_body(frames, codes, lengths, gains, w_qkv, w_out, w_up, w_down, table, cotangent)
    place, core = lax.axis_index("dp"), lax.axis_index("tensor")
    plane, side = place // members, place % members
    on_first = lax.axis_index("section") == 0
    half = share // 2
    rows = batches * half
    count = 2 * batches
    at = jnp.stack([lax.axis_index("section"), plane, side]).astype(jnp.int32)

    everywhere, first, second = (0, 1), (0,), (1,)

    def linked(a, flip_place, flip_core, sections=everywhere):
        pairs = [
            ((z * count + i) * 2 + j, (z * count + (i ^ flip_place)) * 2 + (j ^ flip_core))
            for z in sections
            for i in range(count)
            for j in range(2)
        ]
        return lax.ppermute(a, ("section", "dp", "tensor"), pairs)

    def core_swap(a, sections=everywhere):
        return linked(a, 0, 1, sections)

    def side_swap(a, sections=everywhere):
        return linked(a, 1, 0, sections)

    def both_swap(a, sections=everywhere):
        return linked(a, 1, 1, sections)

    def to_local(a):
        return lax.ppermute(a, "section", [(0, 1)])

    def to_global(a):
        return lax.ppermute(a, "section", [(1, 0)])

    def planes_in(a, sections=everywhere):
        pieces = [lax.dynamic_slice_in_dim(a, plane ^ k, 1, 0) for k in range(batches)]
        return jnp.concatenate([pieces[0], *(linked(pieces[k], 2 * k, 0, sections) for k in range(1, batches))], 0)

    def planes_out(a, sections=everywhere):
        got = [a[:1], *(linked(a[k : k + 1], 2 * k, 0, sections) for k in range(1, batches))]
        out = jnp.zeros_like(a)
        for k in range(batches):
            out = lax.dynamic_update_slice_in_dim(out, got[k], plane ^ k, 0)
        return out

    def core_half(a, axis):
        return lax.dynamic_slice_in_dim(a, core * half, half, axis)

    def join_cores(a, axis):
        other = core_swap(a)
        return jnp.where(core == 0, jnp.concatenate([a, other], axis), jnp.concatenate([other, a], axis))

    def quarter(a, axis):
        size = a.shape[axis] // 2
        return lax.dynamic_slice_in_dim(a, side * size, size, axis)

    def by_side(mine, theirs, axis):
        return jnp.where(side == 0, jnp.concatenate([mine, theirs], axis), jnp.concatenate([theirs, mine], axis))

    x_own = planes_in(core_half(frames, 1), first).reshape(rows, width)
    x_side = side_swap(x_own, first)
    x_core, x_both = core_swap(x_own), core_swap(x_side)

    def positions(jt, js):
        base = ((jnp.arange(batches)[:, None] ^ plane) * 2 + (side ^ js)) * share + (core ^ jt) * half
        return (base + jnp.arange(half)[None, :]).reshape(-1)

    pos = jnp.concatenate([positions(0, 0), positions(0, 1), positions(1, 0), positions(1, 1)]).astype(jnp.int32)
    doc_ends = jnp.cumsum(lax.dynamic_index_in_dim(lengths, plane, 0, keepdims=False))
    doc = doc_index(pos, doc_ends)
    qid = jnp.stack([pos, doc], 1)
    kid = jnp.stack([pos, jnp.where(pos < doc_ends[-1], doc, -1)], 0)

    cot = planes_in(core_half(cotangent.transpose(0, 2, 1, 3), 2), second)
    codes_own = planes_in(core_half(codes.transpose(0, 2, 1), 2), second)
    (x_core, x_both, qid, kid, cot, codes_own), (w_qkv, w_out, w_up, w_down) = fence(
        (x_core, x_both, qid, kid, cot, codes_own), (w_qkv, w_out, w_up, w_down)
    )
    gains_here = gains[0]
    proj_own = w_qkv[0].transpose(1, 0, 2)
    out_own, up_own, down_own = w_out[0], w_up[0], w_down[0]
    out_oth, up_oth, down_oth = (core_swap(w) for w in (out_own, up_own, down_own))
    proj_oth = core_swap(proj_own)

    normed_all, q, k, v, near, off = attend_call(at, (x_own, x_side, x_core, x_both), gains_here, proj_own, qid, kid)
    proj_mine = quarter(proj_own, 2)
    off_got = side_swap(off, first)
    from_core = core_swap(jnp.concatenate([near[1:], off_got[1:]], 0))
    attended = jnp.stack([near[0], off[0], near[1], off[1]]).reshape(4 * rows, -1)
    x32 = x_own.astype(f32)
    resid, mid, act_own, act_oth, slope_own, slope_oth, global_low = front_call(
        at, x_own, near, off_got, from_core, gains_here, out_own, out_oth, up_own, up_oth, down_own, down_oth
    )
    mid_in, act_in = core_swap(mid), core_swap(act_oth)

    arrived = to_local(global_low)
    cot = cot.transpose(1, 0, 2, 3).reshape(CODEBOOKS, rows, width)
    codes_own = codes_own.transpose(1, 0, 2).reshape(CODEBOOKS, rows)
    slots = jnp.arange(table.shape[1], dtype=jnp.int32)
    cot_rows = cot.reshape(-1, width)
    cot_in, codes_oth = core_swap(cot_rows), core_swap(codes_own)

    looked_up, pull_own, pull_oth = prepare_call(at, codes_own, cot_rows, down_own, down_oth, table)
    (pull_own, codes_oth, cot_in), = fence((pull_own, codes_oth, cot_in))
    (
        l_resid, l_act, l_rise, l_pack, l_act_oth, l_send, l_grad, l_frame, l_gains,
    ) = local_call(
        at, arrived, looked_up, cot, pull_own, pull_oth, gains_here, proj_own, proj_oth, out_own, out_oth, up_own, up_oth
    )
    global_moved = planes_out(global_low.reshape(batches, half, width), first)
    global_sent = to_local(global_moved)
    (l_frame, l_grad, l_act_oth, global_moved, global_sent), (l_send,) = fence(
        (l_frame, l_grad, l_act_oth, global_moved, global_sent), (l_send,)
    )
    grad_low = to_global(l_frame.astype(bf))

    flat = lambda a: a.reshape(-1, a.shape[-1])
    hidden = up_own.shape[1]

    def swap(a, bit, sections=everywhere):
        return linked(a, 1 << bit, 0, sections)

    def meet(mine, got):
        return (mine.astype(f32) + got.astype(f32)).astype(bf)

    def cols_of(a, which):
        return lax.dynamic_slice_in_dim(a, which * (width // 2), width // 2, 2)

    l_grad_in, l_act_in = core_swap(cols_of(l_grad, 1 - core)), core_swap(flat(l_act_oth), second)
    table_low, table_high = table_call(at, codes_own, codes_oth, cols_of(l_grad, core), l_grad_in, table.shape[1])
    l_down_mine, l_down_theirs = weight_call(
        at, 1, (cot_rows, cot_in, flat(l_act), l_act_in), (0, 0, 0, 0), True, "local_down_gradient", 4, width, hidden
    )
    (table_low, table_high, grad_low, l_down_theirs), (l_send,) = fence(
        (table_low, table_high, grad_low, l_down_theirs), (l_send,)
    )
    l_got = core_swap(flat(l_send), second)

    grad_in_low = core_swap(grad_low)
    rise_own, rise_oth, grad_resid, low_own, gain_mid = back_call(
        at, grad_low, resid, gains_here, slope_own, slope_oth, up_own, up_oth, down_own, down_oth
    )
    rise_in = core_swap(rise_oth)
    local_low = fall_call(at, flat(l_resid), flat(l_act), flat(l_act_oth), down_own, down_oth, batches, CODEBOOKS)
    (low_own, grad_in_low, local_low), (l_got,) = fence((low_own, grad_in_low, local_low), (l_got,))
    local_moved = planes_out(local_low, second)
    low_side = side_swap(low_own, first)
    down_mine, down_theirs = weight_call(
        at, 0, (grad_low, grad_in_low, act_own, act_in), (0, 0, 0, 0), True, "down_gradient", 8, width, hidden, l_down_theirs
    )
    l_up_mine, l_up_theirs = weight_call(
        at, 1, (flat(l_send), l_got, flat(l_rise), l_got),
        (hidden // width, hidden // width, 0, 0), False, "local_up_gradient", 4, width, hidden,
    )
    (down_theirs, l_up_theirs, local_moved), (rise_in, table_low) = fence(
        (down_theirs, l_up_theirs, local_moved), (rise_in, table_low)
    )
    table_moved = to_global(table_low)
    down_got = swap(down_theirs, 1)
    up_mine, up_theirs = weight_call(
        at, 0, (mid, mid_in, rise_own, rise_in), (0, 0, 0, 0), False, "up_gradient", 8, width, hidden, l_up_theirs
    )
    (up_theirs, low_side), (l_pack, l_act) = fence((up_theirs, low_side), (l_pack, l_act))
    up_got = swap(up_theirs, 0)
    low_at = hidden // width + 1
    l_rest_mine, l_rest_theirs = rest_call(
        at, 1, ((flat(l_send), low_at), (l_got, low_at)), ((flat(l_send), low_at + 1), (l_got, low_at + 1)),
        ((l_pack.reshape(4, CODEBOOKS * rows, -1), 0), (l_got, (hidden + 3 * width) // l_pack.shape[-1])),
        "local_rest_gradient", 0.01, width,
    )
    (l_rest_theirs, low_side), = fence((l_rest_theirs, low_side))
    low_all = jnp.concatenate([low_own, low_side, core_swap(low_own), core_swap(low_side)], 0)
    grad_att = against_rows(low_all, quarter(out_own, 0)).astype(bf)
    grad_packs = attend_back_call(at, q, k, v, grad_att, qid, kid, rows)
    rest_mine, rest_theirs = rest_call(
        at, 0, ((low_all, 0),), ((normed_all, 0),), ((jnp.stack([attended, *grad_packs]), 0),), "rest_gradient", 0.01, width
    )
    flip = side == 0
    empty = jnp.zeros_like(rest_mine)

    def spread_out(a):
        return jnp.concatenate([jnp.where(flip, a, empty), jnp.where(flip, empty, a)], 2)

    rest_theirs = jnp.where(on_first, spread_out(rest_theirs), l_rest_theirs)
    (rest_theirs, down_got, up_got), (grad_packs, rest_mine, local_moved) = fence(
        (rest_theirs, down_got, up_got), (grad_packs, rest_mine, local_moved)
    )
    rest_got = swap(rest_theirs, 0)
    rest_mine = jnp.where(on_first, spread_out(rest_mine), l_rest_mine)
    up_now = meet(jnp.where(on_first, up_mine, l_up_mine), up_got)
    up_got = swap(up_now[2:], 1)
    down_now = meet(jnp.where(on_first, down_mine, l_down_mine), down_got)
    down_got = swap(down_now[1], 2)
    part_normed = sum(against_rows(g, proj_mine[j]) for j, g in enumerate(grad_packs))
    pair = part_normed[: 2 * rows] + core_swap(part_normed[2 * rows :].astype(bf)).astype(f32)
    pair_side = side_swap(pair[rows:].astype(bf), first)
    local_sent = to_global(local_moved)
    (rest_got, rest_mine, up_got, down_got, pair_side, table_moved), = fence(
        (rest_got, rest_mine, up_got, down_got, pair_side, table_moved)
    )
    rest_now = meet(rest_mine, rest_got)
    (rest_now,), (up_got, down_got, pair_side) = fence((rest_now,), (up_got, down_got, pair_side))
    rest_got = swap(rest_now[2:], 1)
    down_now = meet(down_now[0], down_got)
    down_got = swap(down_now[1], 0)
    up_now = meet(up_now[:2], up_got)
    up_got = swap(up_now[1], 2)
    grad_normed = pair[:rows] + pair_side.astype(f32)
    back_in, gain_in = rms_back(x32, gains_here[0], grad_normed)
    grad_frames = grad_resid + back_in
    gain_sum = jnp.where(on_first, jnp.concatenate([gain_in[None], gain_mid]), l_gains)
    gain_sum = (gain_sum + core_swap(gain_sum)).reshape(2, batches, 2, -1)
    piece = width // count
    gain_rows = jnp.concatenate(
        [
            lax.dynamic_slice(gain_sum, (0, plane ^ (2 * j + i), side ^ y, 0), (2, 1, 1, piece)).reshape(1, -1)
            for y in range(2)
            for i in range(2)
            for j in range(2)
        ]
    ).reshape(2, batches, 2 * piece)
    gain_rows = jnp.pad(gain_rows.astype(bf)[:, :, None, :], ((0, 0), (0, 0), (0, 15), (0, width // 2 - 2 * piece)))
    table_now = jnp.where(on_first, table_moved, table_high).reshape(2, batches, -1, width // 2)
    table_now = jnp.concatenate([table_now, gain_rows], 2)
    table_got = swap(table_now[1], 0)
    inner = jnp.where(on_first, grad_frames, l_frame).astype(bf).reshape(2, 2, half, width)
    inner_got = swap(inner[1], 2)
    (rest_got, up_got, down_got, table_got, local_sent, inner_got), = fence(
        (rest_got, up_got, down_got, table_got, local_sent, inner_got)
    )
    rest_now = meet(rest_now[:2], rest_got)
    table_now = meet(table_now[0], table_got)
    (table_now, rest_now), (inner_got, local_sent) = fence((table_now, rest_now), (inner_got, local_sent))
    table_got = swap(table_now[2:], 1)
    rest_got = swap(rest_now[1], 2)
    near_got = swap(jnp.stack([inner[0, 1], inner_got[1]]), 1)
    local_out = join_cores(jnp.where(on_first, local_sent, local_moved), 2).transpose(0, 2, 1, 3)
    (near_got, rest_got, table_got, local_out), = fence((near_got, rest_got, table_got, local_out))
    blocks = (inner[0, 0], near_got[0], inner_got[0], near_got[1])
    inner = jnp.zeros((batches, half, width), bf)
    for k, block in enumerate(blocks):
        inner = lax.dynamic_update_slice_in_dim(inner, block[None], plane ^ k, 0)
    global_out = join_cores(jnp.where(on_first, global_moved, global_sent), 1)
    down_share = down_now[0].astype(f32) + down_got.astype(f32)
    up_share = up_now[0].astype(f32) + up_got.astype(f32)
    table_now = meet(table_now[:2], table_got)
    table_got = swap(table_now[1], 2)
    input_grads = join_cores(inner, 1).astype(f32)[None]
    mix = out_own.shape[0]
    rest_share = rest_now[0].astype(f32) + rest_got.astype(f32)
    proj_share = rest_share[1:].transpose(2, 0, 1, 3).reshape(piece, 3, mix)
    out_share = rest_share[0].transpose(0, 2, 1).reshape(mix, piece)
    (local_out, global_out, up_share, down_share, input_grads, proj_share, out_share), (table_got,) = fence(
        (local_out, global_out, up_share, down_share.T, input_grads, proj_share, out_share), (table_got,)
    )
    table_now = table_now[0].astype(f32) + table_got.astype(f32)
    gain_share = table_now[-16, : 2 * piece].reshape(2, piece)
    grad_table = join_cores(table_now[:-16].reshape(CODEBOOKS, -1, width // 2).astype(bf), 2).astype(f32)

    return (
        global_out,
        local_out,
        input_grads,
        proj_share[None],
        out_share[None],
        up_share[None],
        down_share[None],
        gain_share[None],
        grad_table,
    )


def solution(mesh):
    in_specs = (
        P(None, "dp", None),
        P(None, "dp", None),
        P(),
        P("section", None, None),
        P("section", None, None, "tensor"),
        P("section", "tensor", None),
        P("section", None, "tensor"),
        P("section", "tensor", None),
        P(),
        P(None, "dp", None, None),
    )
    out_specs = (
        P(None, "dp", None),
        P(None, "dp", None, None),
        P("section", None, "dp", None),
        P("section", "dp", None, "tensor"),
        P("section", "tensor", "dp"),
        P("section", "dp", "tensor"),
        P("section", "tensor", "dp"),
        P("section", None, "dp"),
        P(None, ("section", "dp"), None),
    )
    return jax.shard_map(body, mesh=mesh, in_specs=in_specs, out_specs=out_specs, check_vma=False)
```
